128 devices in a mesh: row: 8 (over y_lo, z), col: 16 (over y_hi, x, core).
Axes of the slice: x: 4, y: 4 (y_hi: 2, y_lo: 2; y = y_hi * 2 + y_lo), z: 4, core: 2. Of those that a mesh axis runs over, the one named last changes fastest.
Arguments:
- ocean_state: float32 [1024, 24, 4096], P('row', None, 'col'), may hold values from -6 to 6
- saved_checksums: float32 [1024, 4, 24, 256], P(('row', 'col')), may hold values from -24 to 24
- checksum_weights: int32 [4, 16], replicated, may hold values from 1 to 3
- failed_devices: int32 [8, 2], replicated, may hold values from 0 to 15, as said below
- column_op: float32 [24, 24], replicated, may hold values from -1.25 to 1.25
- diffusivity: float32 [24], replicated, may hold values from 0.04 to 0.2
Outputs:
- stepped_state: float32 [1024, 24, 4096], P('row', None, 'col')
- fresh_parity: float32 [1024, 4, 24, 256], P(('row', 'col'))
The draws below stay inside these ranges and needn't reach their ends.
Inputs may be any that keep to these rules, and one draw needn't show every extreme that they name: `failed_devices`: the two entries of a row differ.
All inputs are finite; a program needn't handle non-finite values.
Results may differ from the reference program's by a relative error of at most 0.00022.
Values sent between devices are 32-bit elements; how exact they have to be, the bound alone decides.
No kernel may reach another device: no remote copies, remote signals or barrier semaphores. Data moves between devices by JAX's collectives and lax.ppermute only.
A program may use at most 64 MiB of HBM per device.

```python
import math
import jax
import jax.numpy as jnp
from jax import lax

LOCAL_ROWS = 128
LOCAL_COLUMNS = 256
COLUMN_FIELDS = 24
CHECKSUM_BLOCKS = 4
GROUP = 16
NX = 1024
NY = 4096
N_ROW = 8
N_COL = 16


def draw_failed_devices(key, part):
    key = jax.random.fold_in(key, 11)
    key_a, key_d, key_r = jax.random.split(key, 3)
    first_lost = jax.random.randint(key_a, (N_ROW,), 0, N_COL)
    offset = jax.random.randint(key_d, (N_ROW,), 1, N_COL)
    chosen_row = jax.random.randint(key_r, (), 0, N_ROW)
    row_ids = jnp.arange(N_ROW)
    first_lost = jnp.where(row_ids == chosen_row, N_COL - 1, first_lost)
    first_lost = jnp.where(row_ids == (chosen_row + 1) % N_ROW, 0, first_lost)
    second_lost = (first_lost + offset) % N_COL
    return jnp.stack((first_lost, second_lost), axis=1).astype(jnp.int32)


def touch_ends(result, key, low, top_value):
    longest = result.shape.index(max(result.shape))
    spots = []
    for shift in (0, 1):
        where = [jax.random.randint(jax.random.fold_in(key, axis), (), 0, length) for axis, length in enumerate(result.shape)]
        where[longest] = (where[longest] + shift) % result.shape[longest]
        spots.append(tuple(where))
    return result.at[spots[0]].set(low).at[spots[1]].set(top_value)


def shard_levels(rng, shape, shards, low, high):
    level = 1.0
    for dim, parts in shards:
        draws = jax.random.uniform(jax.random.fold_in(jax.random.fold_in(rng, 6), dim), (parts,), jnp.float32, low / len(shards), high / len(shards))
        level = level * jnp.repeat(jnp.exp(draws), shape[dim] // parts).reshape((-1,) + (1,) * (len(shape) - 1 - dim))
    return level


def scatter_about(own_key, shape, width, limit, shards=(), kind=jnp.bfloat16):
    array = jax.random.normal(own_key, shape, jnp.float32) * width
    if len(shards) > 0:
        array = shard_levels(own_key, shape, shards, -0.22, 0.18) * array
    return jnp.clip(array, min=-limit, max=limit).astype(kind)


def setup_inputs(seed: int = 0) -> dict:
    keys = jax.random.split(jax.random.key(seed), 7)
    return {
        "ocean_state": scatter_about(keys[0], (NX, COLUMN_FIELDS, NY), 1.0, 6.0, ((0, 8), (2, 16)), jnp.float32),
        "saved_checksums": scatter_about(keys[1], (NX, CHECKSUM_BLOCKS, COLUMN_FIELDS, LOCAL_COLUMNS), 4.0, 24.0, ((0, 128),), jnp.float32),
        "checksum_weights": touch_ends(jax.random.randint(keys[2], (CHECKSUM_BLOCKS, GROUP), 1, 4), jax.random.fold_in(keys[2], 1), 1, 3).astype(jnp.int32),
        "failed_devices": draw_failed_devices(jax.random.fold_in(keys[6], 71), 0),
        "column_op": scatter_about(keys[4], (COLUMN_FIELDS, COLUMN_FIELDS), COLUMN_FIELDS ** -0.5, 1.25, (), jnp.float32),
        "diffusivity": jnp.clip(jnp.exp(jax.random.uniform(keys[5], (COLUMN_FIELDS,), jnp.float32, math.log(0.04), math.log(0.2))), 0.04, 0.2),
    }


def coefficients(float_weights, failed_devices):
    weight_a = jnp.take(float_weights, failed_devices[:, 0], axis=1).T
    weight_b = jnp.take(float_weights, failed_devices[:, 1], axis=1).T
    gram_aa = jnp.sum(weight_a * weight_a, axis=1, keepdims=True) + 1.0
    gram_bb = jnp.sum(weight_b * weight_b, axis=1, keepdims=True) + 1.0
    gram_ab = jnp.sum(weight_a * weight_b, axis=1, keepdims=True)
    determinant = gram_aa * gram_bb - gram_ab * gram_ab
    coeff_a = (gram_bb * weight_a - gram_ab * weight_b) / determinant
    coeff_b = (gram_aa * weight_b - gram_ab * weight_a) / determinant
    return coeff_a, coeff_b


def reference(ocean_state, saved_checksums, checksum_weights, failed_devices, column_op, diffusivity):
    highest_precision = lax.Precision.HIGHEST
    device_blocks = ocean_state.reshape(N_ROW, LOCAL_ROWS, COLUMN_FIELDS, N_COL, LOCAL_COLUMNS)
    float_weights = checksum_weights.astype(jnp.float32)
    col_ids = jnp.arange(N_COL, dtype=jnp.int32)
    is_a = col_ids[None, :] == failed_devices[:, 0:1]
    is_b = col_ids[None, :] == failed_devices[:, 1:2]
    survive = jnp.where(is_a | is_b, 0.0, 1.0).astype(jnp.float32)
    retained_weights = float_weights[None, :, :] * survive[:, None, :]
    living_devices = jnp.einsum("pqiun,psu->pqsin", device_blocks, retained_weights, precision=highest_precision)
    remaining_sum = saved_checksums.reshape(N_ROW, LOCAL_ROWS, CHECKSUM_BLOCKS, COLUMN_FIELDS, LOCAL_COLUMNS) - living_devices
    coeff_a, coeff_b = coefficients(float_weights, failed_devices)
    rebuilt_a = jnp.sum(remaining_sum * coeff_a[:, None, :, None, None], axis=2)
    rebuilt_b = jnp.sum(remaining_sum * coeff_b[:, None, :, None, None], axis=2)
    recovered = jnp.where(is_a[:, None, None, :, None], rebuilt_a[:, :, :, None, :],
                          jnp.where(is_b[:, None, None, :, None], rebuilt_b[:, :, :, None, :], device_blocks))
    fresh_parity = jnp.einsum("rxfcy,kc->rxkfy", recovered, float_weights, precision=highest_precision)
    fresh_parity = fresh_parity.reshape(NX, CHECKSUM_BLOCKS, COLUMN_FIELDS, LOCAL_COLUMNS)
    whole = recovered.reshape(NX, COLUMN_FIELDS, NY)
    mixed_state = whole + jnp.tanh(jnp.einsum("gf,xfy->xgy", column_op, whole, precision=highest_precision))
    padded = jnp.pad(mixed_state, ((1, 1), (0, 0), (1, 1)))
    laplace_term = padded[2:, :, 1:-1] + padded[:-2, :, 1:-1] + padded[1:-1, :, 2:] + padded[1:-1, :, :-2] - 4.0 * mixed_state
    stepped_state = mixed_state + diffusivity[None, :, None] * laplace_term
    return stepped_state, fresh_parity
```

```python
import jax
import jax.numpy as jnp
from jax import lax
from jax.sharding import PartitionSpec as P


def with_halo(cells, sides, width):
    for axis, dim in sides:
        count = lax.axis_size(axis)
        ends = count - 1
        head = lax.slice_in_dim(cells, 0, width, axis=dim)
        tail = lax.slice_in_dim(cells, cells.shape[dim] - width, cells.shape[dim], axis=dim)
        cells = jnp.concatenate(
            [
                lax.ppermute(tail, axis, [(i, (i + 1) % count) for i in range(ends)]),
                cells,
                lax.ppermute(head, axis, [((i + 1) % count, i) for i in range(ends)]),
            ],
            axis=dim,
        )
    return cells


def coefficients(float_weights, lost_a, lost_b):
    weight_a = jnp.take(float_weights, lost_a, axis=1)
    weight_b = jnp.take(float_weights, lost_b, axis=1)
    gram_aa = jnp.sum(weight_a * weight_a) + 1.0
    gram_bb = jnp.sum(weight_b * weight_b) + 1.0
    gram_ab = jnp.sum(weight_a * weight_b)
    determinant = gram_aa * gram_bb - gram_ab * gram_ab
    coeff_a = (gram_bb * weight_a - gram_ab * weight_b) / determinant
    coeff_b = (gram_aa * weight_b - gram_ab * weight_a) / determinant
    return weight_a, weight_b, coeff_a, coeff_b


def per_device(
    ocean_state, saved_checksums, checksum_weights, failed_devices, column_op, diffusivity
):
    count = lax.axis_size("col")
    my_col = lax.axis_index("col")
    my_row = lax.axis_index("row")
    lost_pair = lax.dynamic_index_in_dim(failed_devices, my_row, 0, keepdims=False)
    lost_a = lost_pair[0]
    lost_b = lost_pair[1]
    float_weights = checksum_weights.astype(jnp.float32)
    weight_a, weight_b, coeff_a, coeff_b = coefficients(float_weights, lost_a, lost_b)
    members = jnp.arange(count)
    member_a = members == lost_a
    member_b = members == lost_b
    survive_weights = jnp.where(member_a | member_b, 0.0, float_weights)

    rows, fields, columns = ocean_state.shape
    strip = rows // count
    strips = lax.all_to_all(ocean_state, "col", 0, 0, tiled=True)
    strips = strips.reshape(count, strip, fields, columns)
    living = [
        sum(survive_weights[k, c] * strips[c] for c in range(count))
        for k in range(float_weights.shape[0])
    ]
    residue = [saved_checksums[:, k] - living[k] for k in range(len(living))]
    rebuilt_a = sum(coeff_a[k] * residue[k] for k in range(len(living)))
    rebuilt_b = sum(coeff_b[k] * residue[k] for k in range(len(living)))
    fresh_parity = jnp.stack(
        [
            living[k] + weight_a[k] * rebuilt_a + weight_b[k] * rebuilt_b
            for k in range(len(living))
        ],
        axis=1,
    )
    back = jnp.where(member_a[:, None, None, None], rebuilt_a[None], rebuilt_b[None])
    chosen = lax.all_to_all(
        back.reshape(rows, fields, columns), "col", 0, 0, tiled=True
    )
    is_lost = (my_col == lost_a) | (my_col == lost_b)
    recovered = jnp.where(is_lost, chosen, ocean_state)
    mixed_state = recovered + jnp.tanh(
        jnp.einsum("gf,xfy->xgy", column_op, recovered, precision=lax.Precision.HIGHEST)
    )
    padded = with_halo(mixed_state, (("row", 0), ("col", 2)), 1)
    laplace_term = (
        padded[2:, :, 1:-1]
        + padded[:-2, :, 1:-1]
        + padded[1:-1, :, 2:]
        + padded[1:-1, :, :-2]
        - 4.0 * mixed_state
    )
    stepped_state = mixed_state + diffusivity[None, :, None] * laplace_term
    return (stepped_state, fresh_parity)


def solution(mesh):
    return jax.shard_map(
        per_device,
        mesh=mesh,
        in_specs=(P("row", None, "col"), P(("row", "col"), None, None, None), P(), P(), P(), P()),
        out_specs=(P("row", None, "col"), P(("row", "col"), None, None, None)),
        check_vma=False,
    )
```

```python
import jax
import jax.numpy as jnp
from jax import lax
from jax.experimental import pallas as pl
from jax.experimental.pallas import tpu as pltpu
from jax.sharding import PartitionSpec as P

CHUNK_STRIPS = 4
VMEM_BYTES = 40 * 1024 * 1024
SMEM = pl.BlockSpec(memory_space=pltpu.SMEM)
VMEM = pl.BlockSpec(memory_space=pltpu.VMEM)


def coefficients(float_weights, lost_a, lost_b):
    weight_a = jnp.take(float_weights, lost_a, axis=1)
    weight_b = jnp.take(float_weights, lost_b, axis=1)
    gram_aa = jnp.sum(weight_a * weight_a) + 1.0
    gram_bb = jnp.sum(weight_b * weight_b) + 1.0
    gram_ab = jnp.sum(weight_a * weight_b)
    determinant = gram_aa * gram_bb - gram_ab * gram_ab
    coeff_a = (gram_bb * weight_a - gram_ab * weight_b) / determinant
    coeff_b = (gram_aa * weight_b - gram_ab * weight_a) / determinant
    return weight_a, weight_b, coeff_a, coeff_b


def sums_kernel(lost, weights, pair, strips, saved, parity, rebuilt, back, edges):
    count, rows, fields, columns = strips.shape
    checks = saved.shape[1]
    half = columns // 2
    some = rows // 2
    wide = 2 * fields
    part = pl.program_id(0)
    lane = lax.broadcasted_iota(jnp.int32, (fields, half), 1)

    @pl.when(part == 0)
    def _():
        edges[...] = jnp.zeros_like(edges)

    @pl.loop(0, some)
    def _(p):
        i = part * some + p
        at = pl.multiple_of(i * wide, 8)
        to = pl.multiple_of(fields + p * wide, 8)
        living = [None] * checks
        for c in range(count):
            block = strips[c, i]
            for k in range(checks):
                term = weights[k, c] * block
                living[k] = term if c == 0 else living[k] + term
        whole = [jnp.zeros_like(living[0]), jnp.zeros_like(living[0])]
        for k in range(checks):
            residue = saved[p, k] - living[k]
            for b in range(2):
                whole[b] = whole[b] + pair[2 + b, k] * residue
        for k in range(checks):
            parity[p, k] = living[k] + pair[0, k] * whole[0] + pair[1, k] * whole[1]
        lines = []
        for b in range(2):
            lines.append(jnp.concatenate([whole[b][:, :half], whole[b][:, half:]], axis=0))
            rebuilt[b, pl.ds(at, wide), :] = lines[b]
            final = jnp.broadcast_to(whole[b][:, columns - 1 :], (fields, half))
            first = jnp.broadcast_to(whole[b][:, :1], (fields, half))
            kept = jnp.where(lane == i, final, edges[b])
            edges[b] = jnp.where(lane == i + rows, first, kept)
        for c in range(count // 2):
            back[2 * c + part, pl.ds(to, wide), :] = jnp.where(lost[0] // 2 == c, lines[0], lines[1])

    @pl.when(part == 1)
    def _():
        for c in range(count):
            west = jnp.where(lost[0] == c - 1, edges[0], edges[1])
            east = jnp.where(lost[0] == c + 1, edges[0], edges[1])
            back[c, 0:fields, :] = jnp.where(lane < rows, west, east)


def sums(lost, weights, pair, strips, saved):
    count, rows, fields, columns = strips.shape
    checks = saved.shape[1]
    half = columns // 2
    rows_of = pl.BlockSpec((rows // 2, checks, fields, columns), lambda g: (g, 0, 0, 0))
    return pl.pallas_call(
        sums_kernel,
        grid=(2,),
        out_shape=(
            jax.ShapeDtypeStruct(saved.shape, jnp.float32),
            jax.ShapeDtypeStruct((2, 2 * rows * fields, half), jnp.float32),
            jax.ShapeDtypeStruct((count, (rows + 1) * fields, half), jnp.float32),
        ),
        in_specs=[SMEM, SMEM, SMEM, VMEM, rows_of],
        out_specs=(rows_of, VMEM, VMEM),
        scratch_shapes=[pltpu.VMEM((2, fields, half), jnp.float32)],
        compiler_params=pltpu.CompilerParams(
            vmem_limit_bytes=VMEM_BYTES, dimension_semantics=("arbitrary",)
        ),
        cost_estimate=pl.CostEstimate(
            flops=8 * strips.size, bytes_accessed=8 * strips.size, transcendentals=0
        ),
    )(lost, weights, pair, strips, saved)


def spread_kernel(lost, rebuilt, short, back):
    count = short.shape[0]
    fields = back.shape[1] - rebuilt.shape[1]
    for c in range(count):
        back[c, 0:fields, :] = short[c, 0:fields, :]
        back[c, fields:, :] = jnp.where(lost[0] == c, rebuilt[0], rebuilt[1])


def spread_whole(lost, rebuilt, short):
    count, lines, half = short.shape
    whole = rebuilt.shape[1]
    fields = lines - whole // 2
    return pl.pallas_call(
        spread_kernel,
        out_shape=jax.ShapeDtypeStruct((count, fields + whole, half), jnp.float32),
        in_specs=[SMEM, VMEM, VMEM],
        out_specs=VMEM,
        compiler_params=pltpu.CompilerParams(vmem_limit_bytes=VMEM_BYTES),
    )(lost, rebuilt, short)


def step_kernel(
    flags, ocean, mine, other, op, number_of, west_raw, east_raw, out, mixed, sides, operator
):
    rows, fields, columns = ocean.shape
    half = columns // 2
    wide = 2 * fields
    count = mine.shape[0]
    strip = rows // count
    step = pl.program_id(0)
    lost = flags[0] != 0
    mine_first = flags[1] == 0
    lane = lax.broadcasted_iota(jnp.int32, (fields, half), 1)
    number = number_of[...]

    def mix_pair(flat):
        high = flat.astype(jnp.bfloat16)
        low = (flat - high.astype(jnp.float32)).astype(jnp.bfloat16)
        terms = jnp.concatenate([high, low, high], axis=0)
        return flat + jnp.tanh(
            jnp.dot(operator[...], terms, preferred_element_type=jnp.float32)
        )

    def mix(s):
        base = pl.multiple_of(s * strip, strip)
        head = None
        for t in range(0, strip, 2):
            units = []
            for q in (t, t + 1):
                p = fields + (q % (strip // 2)) * wide
                use_mine = mine_first if q < strip // 2 else jnp.logical_not(mine_first)
                sent = jnp.where(use_mine, mine[s, p : p + wide, :], other[s, p : p + wide, :])
                sent = jnp.concatenate([sent[:fields], sent[fields:]], axis=1)
                units.append(jnp.where(lost, sent, ocean[base + q]))
            done = mix_pair(jnp.concatenate(units, axis=0)).reshape(2, fields, columns)
            mixed[pl.ds(base + t + 1, 2)] = done
            if t == 0:
                head = done[0]
        return head

    @pl.when(step == 0)
    def _():
        both = op[...]
        high = both.astype(jnp.bfloat16)
        low = (both - high.astype(jnp.float32)).astype(jnp.bfloat16)
        operator[...] = jnp.concatenate([high, high, low], axis=1)
        mixed[0] = jnp.zeros((fields, columns), jnp.float32)
        mixed[rows + 1] = jnp.zeros((fields, columns), jnp.float32)
        west = jnp.zeros((fields, half), jnp.float32)
        east = jnp.zeros((fields, half), jnp.float32)
        for s in range(count):
            sent = mine[s, 0:fields, :]
            here = (lane >= s * strip) & (lane < (s + 1) * strip)
            west = jnp.where(here, pltpu.roll(sent, s * strip, 1) if s else sent, west)
            east = jnp.where(here, pltpu.roll(sent, (s * strip - strip) % half, 1) if s != 1 else sent, east)
        west = jnp.where(flags[2] != 0, west, west_raw[...])
        east = jnp.where(flags[3] != 0, east, east_raw[...])
        both_sides = jnp.concatenate([west, east], axis=1)
        both_sides = mix_pair(jnp.concatenate([both_sides, both_sides], axis=0))
        sides[0] = both_sides[:fields, :half]
        sides[1] = pltpu.roll(both_sides[:fields, half:], half - 1, 1)
        mix(0)

    def diffuse(s, t, below, west_side, east_side):
        i = s * strip + t + 1
        for part in range(2):
            own = slice(part * half, (part + 1) * half)
            here = mixed[i, :, own]
            across = mixed[i, :, (1 - part) * half : (2 - part) * half]
            if part == 0:
                side = pltpu.roll(west_side, half - t, 1) if t else west_side
                west = jnp.where(lane == 0, side, pltpu.roll(here, 1, 1))
                east = pltpu.roll(jnp.where(lane == 0, across, here), half - 1, 1)
            else:
                side = pltpu.roll(east_side, half - t, 1) if t else east_side
                west = pltpu.roll(jnp.where(lane == half - 1, across, here), 1, 1)
                east = jnp.where(lane == half - 1, side, pltpu.roll(here, half - 1, 1))
            under = mixed[i + 1, :, own] if below is None else below[:, own]
            around = under + mixed[i - 1, :, own] + east + west
            out[(s - step * CHUNK_STRIPS) * strip + t, :, own] = here + number * (
                around - 4.0 * here
            )

    def body(j, carry):
        s = step * CHUNK_STRIPS + j
        for t in range(strip - 1):
            diffuse(s, t, None, *carry)
        head = mix(jnp.minimum(s + 1, count - 1))
        head = jnp.where(s == count - 1, mixed[rows + 1], head)
        diffuse(s, strip - 1, head, *carry)
        return pltpu.roll(carry[0], half - strip, 1), pltpu.roll(carry[1], half - strip, 1)

    west_side, east_side = lax.fori_loop(0, CHUNK_STRIPS, body, (sides[0], sides[1]))
    sides[0] = west_side
    sides[1] = east_side


def step(flags, ocean, mine, other, op, number_of, west_raw, east_raw):
    rows, fields, columns = ocean.shape
    chunk = CHUNK_STRIPS * rows // mine.shape[0]
    return pl.pallas_call(
        step_kernel,
        grid=(rows // chunk,),
        out_shape=jax.ShapeDtypeStruct(ocean.shape, jnp.float32),
        in_specs=[SMEM] + [VMEM] * 7,
        out_specs=pl.BlockSpec((chunk, fields, columns), lambda g: (g, 0, 0)),
        scratch_shapes=[
            pltpu.VMEM((rows + 2, fields, columns), jnp.float32),
            pltpu.VMEM((2, fields, columns // 2), jnp.float32),
            pltpu.VMEM((2 * fields, 6 * fields), jnp.bfloat16),
        ],
        compiler_params=pltpu.CompilerParams(
            vmem_limit_bytes=VMEM_BYTES, dimension_semantics=("arbitrary",)
        ),
        cost_estimate=pl.CostEstimate(
            flops=150 * ocean.size, bytes_accessed=12 * ocean.size, transcendentals=ocean.size
        ),
    )(flags, ocean, mine, other, op, number_of, west_raw, east_raw)


def ends_kernel(stepped, above, below, op, number_of, out, row, sem):
    rows, fields, columns = stepped.shape
    outer = ((0, above), (rows - 1, below))
    reads = [
        pltpu.make_async_copy(out.at[at], row.at[n], sem.at[n]) for n, (at, _) in enumerate(outer)
    ]
    for copy in reads:
        copy.start()
    both = jnp.concatenate([above[...], below[...]], axis=0)
    coupled = jnp.dot(
        op[...], both, preferred_element_type=jnp.float32, precision=lax.Precision.HIGHEST
    )
    both = both + jnp.tanh(coupled)
    number = jnp.concatenate([number_of[...], number_of[...]], axis=1)
    writes = []
    for n, (at, _) in enumerate(outer):
        reads[n].wait()
        row[n] = row[n] + number * both[n * fields : (n + 1) * fields]
        writes.append(pltpu.make_async_copy(row.at[n], out.at[at], sem.at[n]))
        writes[n].start()
    for copy in writes:
        copy.wait()


def add_ends(stepped, above, below, op, number_of):
    fields, columns = above.shape
    anywhere = pl.BlockSpec(memory_space=pl.ANY)
    return pl.pallas_call(
        ends_kernel,
        out_shape=jax.ShapeDtypeStruct(stepped.shape, jnp.float32),
        in_specs=[anywhere] + [VMEM] * 4,
        out_specs=anywhere,
        input_output_aliases={0: 0},
        scratch_shapes=[
            pltpu.VMEM((2, fields, columns), jnp.float32),
            pltpu.SemaphoreType.DMA((2,)),
        ],
        compiler_params=pltpu.CompilerParams(vmem_limit_bytes=VMEM_BYTES),
    )(stepped, above, below, op, number_of)


def per_device(
    ocean_state, saved_checksums, checksum_weights, failed_devices, column_op, diffusivity
):
    count = lax.axis_size("col")
    lines = lax.axis_size("row")
    my_col = lax.axis_index("col")
    my_row = lax.axis_index("row")
    rows, fields, columns = ocean_state.shape
    half = columns // 2
    strip = rows // count
    east_pairs = [(i, i + 1) for i in range(count - 1)]
    west_pairs = [(i + 1, i) for i in range(count - 1)]
    down_pairs = [(i, i + 1) for i in range(lines - 1)]
    up_pairs = [(i + 1, i) for i in range(lines - 1)]
    twin_pairs = [(i, i ^ 1) for i in range(count)]

    strips = lax.all_to_all(ocean_state, "col", 0, 0, tiled=True)
    strips = strips.reshape(count, strip, fields, columns)

    west_raw = lax.ppermute(ocean_state[:, :, columns - 1].T, "col", east_pairs)
    east_raw = lax.ppermute(ocean_state[:, :, 0].T, "col", west_pairs)

    lost_pair = lax.dynamic_index_in_dim(failed_devices, my_row, 0, keepdims=False)
    lost_a = lost_pair[0]
    lost_b = lost_pair[1]
    same_chip = jnp.any(failed_devices[:, 0] // 2 == failed_devices[:, 1] // 2)
    float_weights = checksum_weights.astype(jnp.float32)
    pair = jnp.stack(coefficients(float_weights, lost_a, lost_b))
    members = jnp.arange(count)
    survive_weights = jnp.where((members == lost_a) | (members == lost_b), 0.0, float_weights)

    def is_lost(member):
        return (member == lost_a) | (member == lost_b)

    flags = jnp.stack(
        [
            is_lost(my_col),
            (my_col % 2 == 1) & ~same_chip,
            is_lost(my_col - 1),
            is_lost(my_col + 1),
        ]
    ).astype(jnp.int32)
    op = jnp.kron(jnp.eye(2, dtype=jnp.float32), column_op)
    number_of = jnp.broadcast_to(diffusivity[:, None], (fields, half))

    fresh_parity, rebuilt, back = sums(
        lost_pair, survive_weights, pair, strips, saved_checksums
    )

    def exchange_halves(rebuilt, back):
        mine = lax.all_to_all(back, "col", 0, 0, tiled=True)
        return mine, lax.ppermute(mine, "col", twin_pairs)

    def exchange_whole(rebuilt, back):
        got = lax.all_to_all(spread_whole(lost_pair, rebuilt, back), "col", 0, 0, tiled=True)
        length = back.shape[1]
        return got[:, :length], got[:, length - fields :]

    mine, other = lax.cond(same_chip, exchange_whole, exchange_halves, rebuilt, back)

    mine_first = flags[1] == 0
    lost = flags[0] != 0

    def sent_row(first, at):
        sent = jnp.where(first, mine[at], other[at])
        return sent

    top = jnp.where(mine_first, mine[0, fields : 3 * fields], other[0, fields : 3 * fields])
    bottom = jnp.where(mine_first, other[count - 1, -2 * fields :], mine[count - 1, -2 * fields :])
    top = jnp.concatenate([top[:fields], top[fields:]], axis=1)
    bottom = jnp.concatenate([bottom[:fields], bottom[fields:]], axis=1)
    top = jnp.where(lost, top, ocean_state[0])
    bottom = jnp.where(lost, bottom, ocean_state[rows - 1])
    above = lax.ppermute(bottom, "row", down_pairs)
    below = lax.ppermute(top, "row", up_pairs)
    stepped_state = step(
        flags, ocean_state, mine, other, op, number_of, west_raw, east_raw
    )
    stepped_state = add_ends(stepped_state, above, below, op, number_of)
    return (stepped_state, fresh_parity)


def solution(mesh):
    return jax.shard_map(
        per_device,
        mesh=mesh,
        in_specs=(P("row", None, "col"), P(("row", "col"), None, None, None), P(), P(), P(), P()),
        out_specs=(P("row", None, "col"), P(("row", "col"), None, None, None)),
        check_vma=False,
    )
```

```python
import functools

import jax
import jax.numpy as jnp
from jax import lax
from jax.experimental import pallas as pl
from jax.experimental.pallas import tpu as pltpu
from jax.sharding import PartitionSpec as P

CHUNK_STRIPS = 4
VMEM_BYTES = 20 * 1024 * 1024
SMEM = pl.BlockSpec(memory_space=pltpu.SMEM)
VMEM = pl.BlockSpec(memory_space=pltpu.VMEM)

GROUP = 8
MEMBERS = ("y_hi", "x", "core")


def column(weights, member):
    return [weights[k, member] for k in range(weights.shape[0])]


def dot(left, right):
    return sum(x * y for x, y in zip(left, right))


def rebuild_kernel(
    failed, weights, strips, saved, parity, rebuilt, back, shared, edges, factors, stored, sem
):
    count, rows, fields, columns = strips.shape
    checks = saved.shape[1]
    half = columns // 2
    wide = 2 * fields
    fetch = pltpu.make_async_copy(saved, stored, sem)
    fetch.start()
    lane = lax.broadcasted_iota(jnp.int32, (fields, half), 1)
    edges[...] = jnp.zeros_like(edges)
    line = lax.axis_index("row")
    lost = (failed[0, line], failed[1, line])

    any_shared = jnp.int32(0)
    for r in range(failed.shape[1]):
        any_shared |= (failed[0, r] // 2 == failed[1, r] // 2).astype(jnp.int32)
    shared[0] = any_shared

    u, v = column(weights, lost[0]), column(weights, lost[1])
    gram_aa, gram_bb, gram_ab = dot(u, u) + 1, dot(v, v) + 1, dot(u, v)
    determinant = (gram_aa * gram_bb - gram_ab * gram_ab).astype(jnp.float32)
    scale = 1.0 / jnp.full((fields, columns), determinant, jnp.float32)
    for c in range(count):
        kept = ((lost[0] != c) & (lost[1] != c)).astype(jnp.int32)
        for k in range(checks):
            factors[k, c] = (kept * weights[k, c]).astype(jnp.float32)
    for k in range(checks):
        factors[k, count] = u[k].astype(jnp.float32)
        factors[k, count + 1] = v[k].astype(jnp.float32)
        factors[k, count + 2] = (gram_bb * u[k] - gram_ab * v[k]).astype(jnp.float32)
        factors[k, count + 3] = (gram_aa * v[k] - gram_ab * u[k]).astype(jnp.float32)
    fetch.wait()

    def keep_edges(n, i, first, final):
        ends = pltpu.roll(jnp.where(lane == 0, first, final), 2 * i + 1, 1)
        edges[n] = jnp.where((lane == 2 * i) | (lane == 2 * i + 1), ends, edges[n])

    @pl.loop(0, rows)
    def _(i):
        at = pl.multiple_of(i * wide, 8)
        living = [None] * checks
        for c in range(count):
            block = strips[c, i]
            keep_edges(c, i, block[:, :half], block[:, half:])
            for k in range(checks):
                term = factors[k, c] * block
                living[k] = term if c == 0 else living[k] + term
        whole = [None, None]
        for k in range(checks):
            residue = stored[i, k] - living[k]
            for b in range(2):
                term = factors[k, count + 2 + b] * residue
                whole[b] = term if k == 0 else whole[b] + term
        whole = [x * scale for x in whole]
        for k in range(checks):
            parity[i, k] = (
                living[k] + factors[k, count] * whole[0] + factors[k, count + 1] * whole[1]
            )
        for b in range(2):
            first, final = whole[b][:, :half], whole[b][:, half:]
            keep_edges(count + b, i, first, final)
            whole[b] = jnp.concatenate([first, final], axis=0)
            rebuilt[b, pl.ds(at, wide), :] = whole[b]
        for c in range(count // 2):
            chosen = jnp.where(lost[0] // 2 == c, whole[0], whole[1])
            back[c, pl.ds(at + GROUP, wide), :] = chosen

    def recovered_edges(c):
        if c < 0 or c >= count:
            return jnp.zeros((fields, half), jnp.float32)
        raw = jnp.where(lost[1] == c, edges[count + 1], edges[c])
        return jnp.where(lost[0] == c, edges[count], raw)

    for c in range(0, count, 2):
        near = [recovered_edges(c + d) for d in (-1, 0, 1, 2)]
        both = jnp.where(lane % 2 == 0, near[0], near[2])
        both = both + pltpu.roll(jnp.where(lane % 2 == 0, near[1], near[3]), 2 * rows, 1)
        packed = both[:GROUP]
        for g in range(1, fields // GROUP):
            packed = packed + pltpu.roll(both[g * GROUP : (g + 1) * GROUP], 4 * rows * g, 1)
        back[c // 2, 0:GROUP, :] = packed


def rebuild(failed, weights, strips, saved):
    count, rows, fields, columns = strips.shape
    half = columns // 2
    whole = 2 * rows * fields
    checks = weights.shape[0]
    return pl.pallas_call(
        rebuild_kernel,
        out_shape=(
            jax.ShapeDtypeStruct(saved.shape, jnp.float32),
            jax.ShapeDtypeStruct((2, whole, half), jnp.float32),
            jax.ShapeDtypeStruct((count // 2, GROUP + whole, half), jnp.float32),
            jax.ShapeDtypeStruct((1,), jnp.int32),
        ),
        in_specs=[SMEM, SMEM, VMEM, pl.BlockSpec(memory_space=pl.ANY)],
        out_specs=(VMEM, VMEM, VMEM, SMEM),
        scratch_shapes=[
            pltpu.VMEM((count + 2, fields, half), jnp.float32),
            pltpu.SMEM((checks, count + 4), jnp.float32),
            pltpu.VMEM(saved.shape, jnp.float32),
            pltpu.SemaphoreType.DMA,
        ],
        compiler_params=pltpu.CompilerParams(vmem_limit_bytes=VMEM_BYTES),
        cost_estimate=pl.CostEstimate(
            flops=8 * strips.size, bytes_accessed=6 * strips.size, transcendentals=0
        ),
    )(failed, weights, strips, saved)


def spread_kernel(failed, rebuilt, short, back):
    lost_a = failed[0, lax.axis_index("row")]
    for c in range(back.shape[0]):
        back[c, 0:GROUP, :] = short[c // 2, 0:GROUP, :]
        back[c, GROUP:, :] = jnp.where(lost_a == c, rebuilt[0], rebuilt[1])


def spread_whole(failed, rebuilt, short):
    chips, lines, half = short.shape
    return pl.pallas_call(
        spread_kernel,
        out_shape=jax.ShapeDtypeStruct((2 * chips, lines, half), jnp.float32),
        in_specs=[SMEM, VMEM, VMEM],
        out_specs=VMEM,
        compiler_params=pltpu.CompilerParams(vmem_limit_bytes=VMEM_BYTES),
    )(failed, rebuilt, short)


def step_kernel(whole, *refs):
    if whole:
        failed, ocean, sent, row_above, row_below, op, diffusivity, *refs = refs
    else:
        failed, ocean, mine, other, row_straight, row_crossed, row_raw, op, diffusivity, *refs = refs
    out, mixed, sides, operator, number_of = refs
    rows, fields, columns = ocean.shape
    half = columns // 2
    wide = 2 * fields
    count = sent.shape[0] if whole else 2 * mine.shape[0]
    strip = rows // count
    step = pl.program_id(0)
    line = lax.axis_index("row")
    member = lax.axis_index(MEMBERS)
    core = member % 2
    lost = (failed[0, line] == member) | (failed[1, line] == member)
    lane = lax.broadcasted_iota(jnp.int32, (fields, half), 1)

    def received(s, own):
        if whole:
            return sent[s, own, :]
        use_mine = s % 2 == core
        return jnp.where(use_mine, mine[s // 2, own, :], other[s // 2, own, :])

    def lanes_beside(cells):
        return jnp.concatenate([cells[:fields], cells[fields:]], axis=1)

    def mix_pair(flat):
        high = flat.astype(jnp.bfloat16)
        low = (flat - high.astype(jnp.float32)).astype(jnp.bfloat16)
        terms = jnp.concatenate([high, low, high], axis=0)
        return flat + jnp.tanh(
            jnp.dot(operator[...], terms, preferred_element_type=jnp.float32)
        )

    def mix(s):
        base = pl.multiple_of(s * strip, strip)
        head = None
        for t in range(0, strip, 2):
            units = []
            for q in (t, t + 1):
                own = slice(GROUP + q * wide, GROUP + (q + 1) * wide)
                units.append(jnp.where(lost, lanes_beside(received(s, own)), ocean[base + q]))
            done = mix_pair(jnp.concatenate(units, axis=0)).reshape(2, fields, columns)
            mixed[pl.ds(base + t + 1, 2)] = done
            if t == 0:
                head = done[0]
        return head

    def double_operator():
        tall = lax.broadcasted_iota(jnp.int32, (wide, fields), 0) % fields
        tall = (tall == lax.broadcasted_iota(jnp.int32, (wide, fields), 1)).astype(jnp.float32)
        flat = lax.broadcasted_iota(jnp.int32, (fields, wide), 1) % fields
        flat = (flat == lax.broadcasted_iota(jnp.int32, (fields, wide), 0)).astype(jnp.float32)
        exact = dict(preferred_element_type=jnp.float32, precision=lax.Precision.HIGHEST)
        tiled = jnp.dot(jnp.dot(tall, op[...], **exact), flat, **exact)
        down = lax.broadcasted_iota(jnp.int32, (wide, wide), 0) // fields
        across = lax.broadcasted_iota(jnp.int32, (wide, wide), 1) // fields
        return jnp.where(down == across, tiled, 0.0)

    def outer_rows():
        before, after = jnp.maximum(line - 1, 0), jnp.minimum(line + 1, failed.shape[1] - 1)
        lost_above = (failed[0, before] == member) | (failed[1, before] == member)
        lost_below = (failed[0, after] == member) | (failed[1, after] == member)

        def chosen(is_lost, pair):
            return jnp.where(is_lost, pair[wide:, :], pair[:wide, :])

        if whole:
            return chosen(lost_above, row_above), chosen(lost_below, row_below)
        crossed, raw = row_crossed[...], row_raw[...]
        above = jnp.where(
            core == 0, jnp.where(lost_above, crossed, raw), chosen(lost_above, row_straight)
        )
        below = jnp.where(
            core == 0, chosen(lost_below, row_straight), jnp.where(lost_below, crossed, raw)
        )
        return above, below

    @pl.when(step == 0)
    def _():
        both = double_operator()
        high = both.astype(jnp.bfloat16)
        low = (both - high.astype(jnp.float32)).astype(jnp.bfloat16)
        operator[...] = jnp.concatenate([high, high, low], axis=1)
        field = lax.broadcasted_iota(jnp.int32, (fields, half), 0)
        number = jnp.zeros((fields, half), jnp.float32)
        for f in range(fields):
            number = jnp.where(field == f, diffusivity[f], number)
        number_of[...] = number
        above, below = outer_rows()
        outer = mix_pair(jnp.concatenate([lanes_beside(above), lanes_beside(below)], axis=0))
        mixed[0] = outer[:fields]
        mixed[rows + 1] = outer[fields:]
        narrow = lane[:GROUP]
        ends = []
        for g in range(fields // GROUP):
            parts = []
            for h in range(2):
                part = jnp.zeros((GROUP, half), jnp.float32)
                for n in range(count // 2):
                    tile = received(h * count // 2 + n, slice(0, GROUP))
                    shift = (2 * strip * (n - 2 * g)) % half
                    near = pltpu.roll(tile, shift, 1) if shift else tile
                    shift = (2 * strip * (n - 2 * g - 1)) % half
                    far = pltpu.roll(tile, shift, 1) if shift else tile
                    part = jnp.where(
                        narrow // (2 * strip) == n, jnp.where(core == 0, near, far), part
                    )
                parts.append(part)
            ends.append(jnp.concatenate(parts, axis=1))
        ends = jnp.concatenate(ends, axis=0)
        ends = mix_pair(jnp.concatenate([ends, ends], axis=0))[:fields]
        for h in range(2):
            part = ends[:, h * half : (h + 1) * half]
            part = jnp.where(lane % 2 == 0, pltpu.roll(part, half - 1, 1), pltpu.roll(part, 1, 1))
            for n in range(count // 2):
                sides[h * count // 2 + n] = pltpu.roll(part, half - 2 * strip * n, 1) if n else part
        mix(0)

    number = number_of[...]

    def diffuse(s, t, below):
        i = s * strip + t + 1
        side = pltpu.roll(sides[s], half - 2 * t - 1, 1)
        for part in range(2):
            own = slice(part * half, (part + 1) * half)
            here = mixed[i, :, own]
            across = mixed[i, :, (1 - part) * half : (2 - part) * half]
            if part == 0:
                west = jnp.where(lane == 0, side, pltpu.roll(here, 1, 1))
                east = pltpu.roll(jnp.where(lane == 0, across, here), half - 1, 1)
            else:
                west = pltpu.roll(jnp.where(lane == half - 1, across, here), 1, 1)
                east = jnp.where(lane == half - 1, side, pltpu.roll(here, half - 1, 1))
            under = mixed[i + 1, :, own] if below is None else below[:, own]
            around = under + mixed[i - 1, :, own] + east + west
            out[(s - step * CHUNK_STRIPS) * strip + t, :, own] = here + number * (
                around - 4.0 * here
            )

    @pl.loop(0, CHUNK_STRIPS)
    def _(j):
        s = step * CHUNK_STRIPS + j
        for t in range(strip - 1):
            diffuse(s, t, None)
        head = mix(jnp.minimum(s + 1, count - 1))
        head = jnp.where(s == count - 1, mixed[rows + 1], head)
        diffuse(s, strip - 1, head)


def step(failed, ocean, sent, outer, op, diffusivity):
    rows, fields, columns = ocean.shape
    whole = len(sent) == 1
    count = sent[0].shape[0] * len(sent)
    chunk = CHUNK_STRIPS * rows // count
    return pl.pallas_call(
        functools.partial(step_kernel, whole),
        grid=(rows // chunk,),
        out_shape=jax.ShapeDtypeStruct(ocean.shape, jnp.float32),
        in_specs=[SMEM] + [VMEM] * (2 + len(sent) + len(outer)) + [SMEM],
        out_specs=pl.BlockSpec((chunk, fields, columns), lambda g: (g, 0, 0)),
        scratch_shapes=[
            pltpu.VMEM((rows + 2, fields, columns), jnp.float32),
            pltpu.VMEM((count, fields, columns // 2), jnp.float32),
            pltpu.VMEM((2 * fields, 6 * fields), jnp.bfloat16),
            pltpu.VMEM((fields, columns // 2), jnp.float32),
        ],
        compiler_params=pltpu.CompilerParams(
            vmem_limit_bytes=VMEM_BYTES, dimension_semantics=("arbitrary",)
        ),
        cost_estimate=pl.CostEstimate(
            flops=150 * ocean.size, bytes_accessed=12 * ocean.size, transcendentals=ocean.size
        ),
    )(failed, ocean, *sent, *outer, op, diffusivity)


def per_device(
    ocean_state, saved_checksums, checksum_weights, failed_devices, column_op, diffusivity
):
    lines = lax.axis_size("row")
    rows, fields, columns = ocean_state.shape
    count = checksum_weights.shape[1]
    half = columns // 2
    strip = rows // count

    strips = lax.all_to_all(ocean_state, MEMBERS, 0, 0, tiled=True)
    strips, ocean, saved, weights, failed, op, number = lax.optimization_barrier(
        (
            strips,
            ocean_state,
            saved_checksums,
            checksum_weights,
            failed_devices.T,
            column_op,
            diffusivity,
        )
    )
    strips = strips.reshape(count, strip, fields, columns)
    fresh_parity, rebuilt, back, shared = rebuild(failed, weights, strips, saved)

    def row_pairs(up_core, down_core, swap):
        pairs = []
        for r in range(lines):
            for c in range(count):
                to = c ^ 1 if swap else c
                if c % 2 == up_core and r > 0:
                    pairs.append((r * count + c, (r - 1) * count + to))
                if c % 2 == down_core and r < lines - 1:
                    pairs.append((r * count + c, (r + 1) * count + to))
        return pairs

    def shift_rows(cells, pairs):
        return lax.ppermute(cells, ("row",) + MEMBERS, pairs)

    def own_row(ocean, at):
        return jnp.concatenate([ocean[at, :, :half], ocean[at, :, half:]], axis=0)

    def exchange_chips(rebuilt, back, ocean):
        mine = lax.all_to_all(back, ("y_hi", "x"), 0, 0, tiled=True)
        mine, ocean = lax.optimization_barrier((mine, ocean))
        other = lax.ppermute(mine, "core", [(0, 1), (1, 0)])
        top, bottom = own_row(ocean, 0), own_row(ocean, rows - 1)
        even = lax.axis_index("core") == 0
        sent = jnp.where(even, mine[0, GROUP : GROUP + 2 * fields], mine[-1, -2 * fields :])
        straight = jnp.concatenate([jnp.where(even, top, bottom), sent], axis=0)
        raw = jnp.where(even, bottom, top)
        outer = (
            shift_rows(straight, row_pairs(0, 1, False)),
            shift_rows(sent, row_pairs(0, 1, True)),
            shift_rows(raw, row_pairs(1, 0, False)),
        )
        return step(failed, ocean, (mine, other), outer, op, number)

    def exchange_whole(rebuilt, back, ocean):
        back = spread_whole(failed, rebuilt, back)
        sent = lax.all_to_all(back, MEMBERS, 0, 0, tiled=True)
        sent, ocean = lax.optimization_barrier((sent, ocean))
        top = [own_row(ocean, 0), sent[0, GROUP : GROUP + 2 * fields]]
        bottom = [own_row(ocean, rows - 1), sent[-1, -2 * fields :]]
        outer = (
            lax.ppermute(jnp.concatenate(bottom), "row", [(r, r + 1) for r in range(lines - 1)]),
            lax.ppermute(jnp.concatenate(top), "row", [(r + 1, r) for r in range(lines - 1)]),
        )
        return step(failed, ocean, (sent,), outer, op, number)

    stepped_state = lax.cond(
        shared[0] != 0, exchange_whole, exchange_chips, rebuilt, back, ocean
    )
    return stepped_state, fresh_parity


def solution(mesh):
    row, col = mesh.axis_names
    shape = (mesh.shape[row], 2, 4, 2)
    chips = jax.sharding.Mesh(mesh.devices.reshape(shape), ("row", "y_hi", "x", "core"))
    col = MEMBERS
    return jax.shard_map(
        per_device,
        mesh=chips,
        in_specs=(P("row", None, col), P(("row", *col), None, None, None), P(), P(), P(), P()),
        out_specs=(P("row", None, col), P(("row", *col), None, None, None)),
        check_vma=False,
    )
```

```python
import functools

import jax
import jax.numpy as jnp
from jax import lax
from jax.experimental import pallas as pl
from jax.experimental.pallas import tpu as pltpu
from jax.sharding import PartitionSpec as P

CHUNK_PAIRS = 2
VMEM_BYTES = 20 * 1024 * 1024
SMEM = pl.BlockSpec(memory_space=pltpu.SMEM)
VMEM = pl.BlockSpec(memory_space=pltpu.VMEM)

GROUP = 8
MEMBERS = ("y_hi", "x", "core")


def column(weights, member):
    return [weights[k, member] for k in range(weights.shape[0])]


def dot(left, right):
    return sum(x * y for x, y in zip(left, right))


def rebuild_kernel(
    failed, weights, strips, saved, parity, rebuilt, back, shared, edges, factors, fresh, sem
):
    count, rows, fields, columns = strips.shape
    checks = saved.shape[1]
    half = columns // 2
    wide = 2 * fields
    lane = lax.broadcasted_iota(jnp.int32, (fields, half), 1)
    edges[...] = jnp.zeros_like(edges)
    line = lax.axis_index("row")
    lost = (failed[0, line], failed[1, line])

    any_shared = jnp.int32(0)
    for r in range(failed.shape[1]):
        any_shared |= (failed[0, r] // 2 == failed[1, r] // 2).astype(jnp.int32)
    shared[0] = any_shared

    u, v = column(weights, lost[0]), column(weights, lost[1])
    gram_aa, gram_bb, gram_ab = dot(u, u) + 1, dot(v, v) + 1, dot(u, v)
    determinant = (gram_aa * gram_bb - gram_ab * gram_ab).astype(jnp.float32)
    scale = 1.0 / jnp.full((fields, columns), determinant, jnp.float32)
    for c in range(count):
        kept = ((lost[0] != c) & (lost[1] != c)).astype(jnp.int32)
        for k in range(checks):
            factors[k, c] = (kept * weights[k, c]).astype(jnp.float32)
    for k in range(checks):
        factors[k, count] = u[k].astype(jnp.float32)
        factors[k, count + 1] = v[k].astype(jnp.float32)
        factors[k, count + 2] = (gram_bb * u[k] - gram_ab * v[k]).astype(jnp.float32)
        factors[k, count + 3] = (gram_aa * v[k] - gram_ab * u[k]).astype(jnp.float32)

    def keep_edges(n, i, first, final):
        ends = pltpu.roll(jnp.where(lane == 0, first, final), 2 * i + 1, 1)
        edges[n] = jnp.where((lane == 2 * i) | (lane == 2 * i + 1), ends, edges[n])

    @pl.loop(0, rows)
    def _(i):
        at = pl.multiple_of(i * wide, 8)
        living = [None] * checks
        for c in range(count):
            block = strips[c, i]
            keep_edges(c, i, block[:, :half], block[:, half:])
            for k in range(checks):
                term = factors[k, c] * block
                living[k] = term if c == 0 else living[k] + term
        whole = [None, None]
        for k in range(checks):
            residue = saved[i, k] - living[k]
            for b in range(2):
                term = factors[k, count + 2 + b] * residue
                whole[b] = term if k == 0 else whole[b] + term
        whole = [x * scale for x in whole]
        for k in range(checks):
            fresh[i, k] = (
                living[k] + factors[k, count] * whole[0] + factors[k, count + 1] * whole[1]
            )
        pltpu.make_async_copy(fresh.at[i], parity.at[i], sem.at[i]).start()
        for b in range(2):
            first, final = whole[b][:, :half], whole[b][:, half:]
            keep_edges(count + b, i, first, final)
            whole[b] = jnp.concatenate([first, final], axis=0)
            rebuilt[b, pl.ds(at, wide), :] = whole[b]
        for c in range(count // 2):
            chosen = jnp.where(lost[0] // 2 == c, whole[0], whole[1])
            back[c, pl.ds(at + GROUP, wide), :] = chosen

    def recovered_edges(c):
        if c < 0 or c >= count:
            return jnp.zeros((fields, half), jnp.float32)
        raw = jnp.where(lost[1] == c, edges[count + 1], edges[c])
        return jnp.where(lost[0] == c, edges[count], raw)

    for c in range(0, count, 2):
        near = [recovered_edges(c + d) for d in (-1, 0, 1, 2)]
        both = jnp.where(lane % 2 == 0, near[0], near[2])
        both = both + pltpu.roll(jnp.where(lane % 2 == 0, near[1], near[3]), 2 * rows, 1)
        packed = both[:GROUP]
        for g in range(1, fields // GROUP):
            packed = packed + pltpu.roll(both[g * GROUP : (g + 1) * GROUP], 4 * rows * g, 1)
        back[c // 2, 0:GROUP, :] = packed
    for i in range(rows):
        pltpu.make_async_copy(fresh.at[i], parity.at[i], sem.at[i]).wait()


def rebuild(failed, weights, strips, saved):
    count, rows, fields, columns = strips.shape
    half = columns // 2
    whole = 2 * rows * fields
    checks = weights.shape[0]
    return pl.pallas_call(
        rebuild_kernel,
        out_shape=(
            jax.ShapeDtypeStruct(saved.shape, jnp.float32),
            jax.ShapeDtypeStruct((2, whole, half), jnp.float32),
            jax.ShapeDtypeStruct((count // 2, GROUP + whole, half), jnp.float32),
            jax.ShapeDtypeStruct((1,), jnp.int32),
        ),
        in_specs=[SMEM, SMEM, VMEM, VMEM],
        out_specs=(pl.BlockSpec(memory_space=pl.ANY), VMEM, VMEM, SMEM),
        scratch_shapes=[
            pltpu.VMEM((count + 2, fields, half), jnp.float32),
            pltpu.SMEM((checks, count + 4), jnp.float32),
            pltpu.VMEM(saved.shape, jnp.float32),
            pltpu.SemaphoreType.DMA((rows,)),
        ],
        compiler_params=pltpu.CompilerParams(vmem_limit_bytes=VMEM_BYTES),
        cost_estimate=pl.CostEstimate(
            flops=8 * strips.size, bytes_accessed=6 * strips.size, transcendentals=0
        ),
    )(failed, weights, strips, saved)


def spread_kernel(failed, rebuilt, short, back):
    lost_a = failed[0, lax.axis_index("row")]
    for c in range(back.shape[0]):
        back[c, 0:GROUP, :] = short[c // 2, 0:GROUP, :]
        back[c, GROUP:, :] = jnp.where(lost_a == c, rebuilt[0], rebuilt[1])


def spread_whole(failed, rebuilt, short):
    chips, lines, half = short.shape
    return pl.pallas_call(
        spread_kernel,
        out_shape=jax.ShapeDtypeStruct((2 * chips, lines, half), jnp.float32),
        in_specs=[SMEM, VMEM, VMEM],
        out_specs=VMEM,
        compiler_params=pltpu.CompilerParams(vmem_limit_bytes=VMEM_BYTES),
    )(failed, rebuilt, short)


def beside(cells):
    half = cells.shape[0] // 2
    return jnp.concatenate([cells[:half], cells[half:]], axis=1)


def below(cells):
    half = cells.shape[1] // 2
    return jnp.concatenate([cells[:, :half], cells[:, half:]], axis=0)


def mix_pair(operator, flat):
    high = flat.astype(jnp.bfloat16)
    low = (flat - high.astype(jnp.float32)).astype(jnp.bfloat16)
    terms = jnp.concatenate([high, low, high], axis=0)
    return flat + jnp.tanh(jnp.dot(operator[...], terms, preferred_element_type=jnp.float32))


def mix_strip(operator, lost, sent, base, ocean, strip, store):
    fields, columns = ocean.shape[1:]
    wide = 2 * fields
    head = None
    for t in range(0, strip, 2):
        units = []
        for q in (t, t + 1):
            own = slice(GROUP + q * wide, GROUP + (q + 1) * wide)
            units.append(jnp.where(lost, beside(sent(own)), ocean[base + q]))
        done = mix_pair(operator, jnp.concatenate(units, axis=0)).reshape(2, fields, columns)
        store(t, done)
        if t == 0:
            head = done[0]
    return head


def my_place(failed):
    line = lax.axis_index("row")
    member = lax.axis_index(MEMBERS)
    lost = (failed[0, line] == member) | (failed[1, line] == member)
    return line, member, member % 2, lost


def double_operator(op):
    fields = op.shape[0]
    wide = 2 * fields
    tall = lax.broadcasted_iota(jnp.int32, (wide, fields), 0) % fields
    tall = (tall == lax.broadcasted_iota(jnp.int32, (wide, fields), 1)).astype(jnp.float32)
    flat = lax.broadcasted_iota(jnp.int32, (fields, wide), 1) % fields
    flat = (flat == lax.broadcasted_iota(jnp.int32, (fields, wide), 0)).astype(jnp.float32)
    exact = dict(preferred_element_type=jnp.float32, precision=lax.Precision.HIGHEST)
    tiled = jnp.dot(jnp.dot(tall, op[...], **exact), flat, **exact)
    down = lax.broadcasted_iota(jnp.int32, (wide, wide), 0) // fields
    across = lax.broadcasted_iota(jnp.int32, (wide, wide), 1) // fields
    both = jnp.where(down == across, tiled, 0.0)
    high = both.astype(jnp.bfloat16)
    low = (both - high.astype(jnp.float32)).astype(jnp.bfloat16)
    return jnp.concatenate([high, high, low], axis=1)


def rows_kernel(whole, failed, ocean, *refs):
    *sent, row_top, row_bottom = refs
    rows, fields, columns = ocean.shape
    wide = 2 * fields
    last = sent[0].shape[0] - 1
    first = slice(GROUP, GROUP + wide)
    final = slice(sent[0].shape[1] - wide, sent[0].shape[1])
    _, _, core, lost = my_place(failed)
    if whole:
        top, bottom = sent[0][0, first, :], sent[0][last, final, :]
    else:
        mine, other = sent
        top = jnp.where(core == 0, mine[0, first, :], other[0, first, :])
        bottom = jnp.where(core == 0, other[last, final, :], mine[last, final, :])
    row_top[...] = jnp.where(lost, top, below(ocean[0]))
    row_bottom[...] = jnp.where(lost, bottom, below(ocean[rows - 1]))


def outer_lines(failed, ocean, sent):
    rows, fields, columns = ocean.shape
    line = jax.ShapeDtypeStruct((2 * fields, columns // 2), jnp.float32)
    return pl.pallas_call(
        functools.partial(rows_kernel, len(sent) == 1),
        out_shape=(line, line),
        in_specs=[SMEM] + [VMEM] * (1 + len(sent)),
        out_specs=(VMEM, VMEM),
        compiler_params=pltpu.CompilerParams(vmem_limit_bytes=VMEM_BYTES),
    )(failed, ocean, *sent)


def first_kernel(whole, failed, ocean, sent, op, diffusivity, strips, operator, number_of):
    rows, fields, columns = ocean.shape
    half = columns // 2
    count = 2 * strips.shape[0]
    strip = rows // count
    _, _, core, lost = my_place(failed)
    operator[...] = double_operator(op)
    field = lax.broadcasted_iota(jnp.int32, (fields, half), 0)
    number = jnp.zeros((fields, half), jnp.float32)
    for f in range(fields):
        number = jnp.where(field == f, diffusivity[f], number)
    number_of[...] = number

    @pl.loop(0, count // 2)
    def _(p):
        s = 2 * p + core
        at = s if whole else p

        def store(t, done):
            strips[p, pl.ds(t, 2)] = done

        base = pl.multiple_of(s * strip, strip)
        mix_strip(operator, lost, lambda own: sent[at, own, :], base, ocean, strip, store)


def first_half(failed, ocean, sent, op, diffusivity, whole, count):
    rows, fields, columns = ocean.shape
    half = columns // 2
    wide = 2 * fields
    shapes = [jax.ShapeDtypeStruct((count // 2, rows // count, fields, columns), jnp.float32)]
    shapes.append(jax.ShapeDtypeStruct((wide, 3 * wide), jnp.bfloat16))
    shapes.append(jax.ShapeDtypeStruct((fields, half), jnp.float32))
    return pl.pallas_call(
        functools.partial(first_kernel, whole),
        out_shape=tuple(shapes),
        in_specs=[SMEM, VMEM, VMEM, VMEM, SMEM],
        out_specs=(VMEM,) * len(shapes),
        compiler_params=pltpu.CompilerParams(vmem_limit_bytes=VMEM_BYTES),
        cost_estimate=pl.CostEstimate(
            flops=75 * ocean.size, bytes_accessed=4 * ocean.size, transcendentals=ocean.size // 2
        ),
    )(failed, ocean, sent, op, diffusivity)


def step_kernel(whole, failed, ocean, *refs):
    if whole:
        sent, strips, operator, number_of, *refs = refs
    else:
        mine, other, strips, operator, number_of, *refs = refs
    out, mixed, sides = refs
    rows, fields, columns = ocean.shape
    half = columns // 2
    wide = 2 * fields
    pairs = strips.shape[0]
    count = 2 * pairs
    strip = rows // count
    step = pl.program_id(0)
    _, _, core, lost = my_place(failed)
    lane = lax.broadcasted_iota(jnp.int32, (fields, half), 1)
    number = number_of[...]

    def prepare(p):
        kept = pl.multiple_of((2 * p + core) * strip, strip)
        base = pl.multiple_of((2 * p + 1 - core) * strip, strip)
        at = 2 * p + 1 - core if whole else p
        source = sent if whole else other
        for t in range(0, strip, 2):
            mixed[pl.ds(kept + t + 1, 2)] = strips[p, pl.ds(t, 2)]

        def store(t, done):
            mixed[pl.ds(base + t + 1, 2)] = done

        head = mix_strip(operator, lost, lambda own: source[at, own, :], base, ocean, strip, store)
        return jnp.where(core == 0, strips[p, 0], head)

    def tile_of(s):
        if whole:
            return sent[s, 0:GROUP, :]
        return jnp.where(core == s % 2, mine[s // 2, 0:GROUP, :], other[s // 2, 0:GROUP, :])

    @pl.when(step == 0)
    def _():
        mixed[0] = jnp.zeros((fields, columns), jnp.float32)
        mixed[rows + 1] = jnp.zeros((fields, columns), jnp.float32)
        narrow = lane[:GROUP]
        ends = []
        for g in range(fields // GROUP):
            parts = []
            for h in range(2):
                part = jnp.zeros((GROUP, half), jnp.float32)
                for n in range(count // 2):
                    tile = tile_of(h * count // 2 + n)
                    shift = (2 * strip * (n - 2 * g)) % half
                    near = pltpu.roll(tile, shift, 1) if shift else tile
                    shift = (2 * strip * (n - 2 * g - 1)) % half
                    far = pltpu.roll(tile, shift, 1) if shift else tile
                    part = jnp.where(
                        narrow // (2 * strip) == n, jnp.where(core == 0, near, far), part
                    )
                parts.append(part)
            ends.append(jnp.concatenate(parts, axis=1))
        ends = jnp.concatenate(ends, axis=0)
        ends = mix_pair(operator, jnp.concatenate([ends, ends], axis=0))[:fields]
        for h in range(2):
            part = ends[:, h * half : (h + 1) * half]
            part = jnp.where(lane % 2 == 0, pltpu.roll(part, half - 1, 1), pltpu.roll(part, 1, 1))
            for n in range(count // 2):
                sides[h * count // 2 + n] = pltpu.roll(part, half - 2 * strip * n, 1) if n else part
        prepare(0)

    def diffuse(s, t, at, under_row):
        i = s * strip + t + 1
        side = pltpu.roll(sides[s], half - 2 * t - 1, 1)
        for part in range(2):
            own = slice(part * half, (part + 1) * half)
            here = mixed[i, :, own]
            across = mixed[i, :, (1 - part) * half : (2 - part) * half]
            if part == 0:
                west = jnp.where(lane == 0, side, pltpu.roll(here, 1, 1))
                east = pltpu.roll(jnp.where(lane == 0, across, here), half - 1, 1)
            else:
                west = pltpu.roll(jnp.where(lane == half - 1, across, here), 1, 1)
                east = jnp.where(lane == half - 1, side, pltpu.roll(here, half - 1, 1))
            under = mixed[i + 1, :, own] if under_row is None else under_row[:, own]
            around = under + mixed[i - 1, :, own] + east + west
            out[at, :, own] = here + number * (around - 4.0 * here)

    @pl.loop(0, CHUNK_PAIRS)
    def _(j):
        p = step * CHUNK_PAIRS + j
        for t in range(2 * strip - 1):
            diffuse(2 * p + t // strip, t % strip, 2 * strip * j + t, None)
        head = prepare(jnp.minimum(p + 1, pairs - 1))
        head = jnp.where(p == pairs - 1, mixed[rows + 1], head)
        diffuse(2 * p + 1, strip - 1, 2 * strip * (j + 1) - 1, head)


def step(failed, ocean, sent, strips, operator, number_of):
    rows, fields, columns = ocean.shape
    whole = len(sent) == 1
    pairs = strips.shape[0]
    chunk = CHUNK_PAIRS * rows // pairs
    return pl.pallas_call(
        functools.partial(step_kernel, whole),
        grid=(rows // chunk,),
        out_shape=jax.ShapeDtypeStruct(ocean.shape, jnp.float32),
        in_specs=[SMEM] + [VMEM] * (4 + len(sent)),
        out_specs=pl.BlockSpec((chunk, fields, columns), lambda g: (g, 0, 0)),
        scratch_shapes=[
            pltpu.VMEM((rows + 2, fields, columns), jnp.float32),
            pltpu.VMEM((2 * pairs, fields, columns // 2), jnp.float32),
        ],
        compiler_params=pltpu.CompilerParams(
            vmem_limit_bytes=VMEM_BYTES, dimension_semantics=("arbitrary",)
        ),
        cost_estimate=pl.CostEstimate(
            flops=100 * ocean.size, bytes_accessed=12 * ocean.size, transcendentals=ocean.size // 2
        ),
    )(failed, ocean, *sent, strips, operator, number_of)


def ends_kernel(stepped, above, under, operator, number_of, out, row, sem):
    rows, fields, columns = stepped.shape
    places = (0, rows - 1)
    reads = [
        pltpu.make_async_copy(out.at[at], row.at[n], sem.at[n]) for n, at in enumerate(places)
    ]
    for copy in reads:
        copy.start()
    both = jnp.concatenate([beside(above[...]), beside(under[...])], axis=0)
    both = mix_pair(operator, both)
    number = jnp.concatenate([number_of[...], number_of[...]], axis=1)
    writes = []
    for n, at in enumerate(places):
        reads[n].wait()
        row[n] = row[n] + number * both[n * fields : (n + 1) * fields]
        writes.append(pltpu.make_async_copy(row.at[n], out.at[at], sem.at[n]))
        writes[n].start()
    for copy in writes:
        copy.wait()


def add_ends(stepped, above, under, operator, number_of):
    rows, fields, columns = stepped.shape
    anywhere = pl.BlockSpec(memory_space=pl.ANY)
    return pl.pallas_call(
        ends_kernel,
        out_shape=jax.ShapeDtypeStruct(stepped.shape, jnp.float32),
        in_specs=[anywhere] + [VMEM] * 4,
        out_specs=anywhere,
        input_output_aliases={0: 0},
        scratch_shapes=[
            pltpu.VMEM((2, fields, columns), jnp.float32),
            pltpu.SemaphoreType.DMA((2,)),
        ],
        compiler_params=pltpu.CompilerParams(vmem_limit_bytes=VMEM_BYTES),
    )(stepped, above, under, operator, number_of)


def per_device(
    ocean_state, saved_checksums, checksum_weights, failed_devices, column_op, diffusivity
):
    lines = lax.axis_size("row")
    rows, fields, columns = ocean_state.shape
    count = checksum_weights.shape[1]
    half = columns // 2
    strip = rows // count

    strips = lax.all_to_all(ocean_state, MEMBERS, 0, 0, tiled=True)
    strips, ocean, saved, weights, failed, op, number = lax.optimization_barrier(
        (
            strips,
            ocean_state,
            saved_checksums,
            checksum_weights,
            failed_devices.T,
            column_op,
            diffusivity,
        )
    )
    strips = strips.reshape(count, strip, fields, columns)
    fresh_parity, rebuilt, back, shared = rebuild(failed, weights, strips, saved)

    def finish(ocean, sent, kept):
        top, bottom = outer_lines(failed, ocean, sent)
        above = lax.ppermute(bottom, "row", [(r, r + 1) for r in range(lines - 1)])
        under = lax.ppermute(top, "row", [(r + 1, r) for r in range(lines - 1)])
        stepped = step(failed, ocean, sent, *kept)
        return add_ends(stepped, above, under, *kept[1:])

    def exchange_chips(rebuilt, back, ocean):
        mine = lax.all_to_all(back, ("y_hi", "x"), 0, 0, tiled=True)
        mine, ocean = lax.optimization_barrier((mine, ocean))
        other = lax.ppermute(mine, "core", [(0, 1), (1, 0)])
        kept = first_half(failed, ocean, mine, op, number, False, count)
        other, kept = lax.optimization_barrier((other, kept))
        return finish(ocean, (mine, other), kept)

    def exchange_whole(rebuilt, back, ocean):
        back = spread_whole(failed, rebuilt, back)
        sent = lax.all_to_all(back, MEMBERS, 0, 0, tiled=True)
        sent, ocean = lax.optimization_barrier((sent, ocean))
        kept = first_half(failed, ocean, sent, op, number, True, count)
        return finish(ocean, (sent,), kept)

    stepped_state = lax.cond(
        shared[0] != 0, exchange_whole, exchange_chips, rebuilt, back, ocean
    )
    return stepped_state, fresh_parity


def solution(mesh):
    row, col = mesh.axis_names
    shape = (mesh.shape[row], 2, 4, 2)
    chips = jax.sharding.Mesh(mesh.devices.reshape(shape), ("row", "y_hi", "x", "core"))
    col = MEMBERS
    return jax.shard_map(
        per_device,
        mesh=chips,
        in_specs=(P("row", None, col), P(("row", *col), None, None, None), P(), P(), P(), P()),
        out_specs=(P("row", None, col), P(("row", *col), None, None, None)),
        check_vma=False,
    )
```

```python
import functools

import jax
import jax.numpy as jnp
from jax import lax
from jax.experimental import pallas as pl
from jax.experimental.pallas import tpu as pltpu
from jax.sharding import PartitionSpec as P

VMEM_BYTES = 20 * 1024 * 1024
SMEM = pl.BlockSpec(memory_space=pltpu.SMEM)
VMEM = pl.BlockSpec(memory_space=pltpu.VMEM)

GROUP = 8
MEMBERS = ("y_hi", "x", "core")


def column(weights, member):
    return [weights[k, member] for k in range(weights.shape[0])]


def dot(left, right):
    return sum(x * y for x, y in zip(left, right))


def rebuild_kernel(
    failed, weights, strips, saved, fresh, rebuilt, back, shared, edges, factors
):
    count, rows, fields, columns = strips.shape
    checks = saved.shape[1]
    half = columns // 2
    wide = 2 * fields
    lane = lax.broadcasted_iota(jnp.int32, (fields, half), 1)
    edges[...] = jnp.zeros_like(edges)
    line = lax.axis_index("row")
    lost = (failed[0, line], failed[1, line])

    any_shared = jnp.int32(0)
    for r in range(failed.shape[1]):
        any_shared |= (failed[0, r] // 2 == failed[1, r] // 2).astype(jnp.int32)
    shared[0] = any_shared

    u, v = column(weights, lost[0]), column(weights, lost[1])
    gram_aa, gram_bb, gram_ab = dot(u, u) + 1, dot(v, v) + 1, dot(u, v)
    determinant = (gram_aa * gram_bb - gram_ab * gram_ab).astype(jnp.float32)
    scale = 1.0 / jnp.full((fields, columns), determinant, jnp.float32)
    for c in range(count):
        kept = ((lost[0] != c) & (lost[1] != c)).astype(jnp.int32)
        for k in range(checks):
            factors[k, c] = (kept * weights[k, c]).astype(jnp.float32)
    for k in range(checks):
        factors[k, count] = u[k].astype(jnp.float32)
        factors[k, count + 1] = v[k].astype(jnp.float32)
        factors[k, count + 2] = (gram_bb * u[k] - gram_ab * v[k]).astype(jnp.float32)
        factors[k, count + 3] = (gram_aa * v[k] - gram_ab * u[k]).astype(jnp.float32)

    def keep_edges(n, i, first, final):
        ends = pltpu.roll(jnp.where(lane == 0, first, final), 2 * i + 1, 1)
        edges[n] = jnp.where((lane == 2 * i) | (lane == 2 * i + 1), ends, edges[n])

    @pl.loop(0, rows)
    def _(i):
        at = pl.multiple_of(i * wide, 8)
        living = [None] * checks
        for c in range(count):
            block = strips[c, i]
            keep_edges(c, i, block[:, :half], block[:, half:])
            for k in range(checks):
                term = factors[k, c] * block
                living[k] = term if c == 0 else living[k] + term
        whole = [None, None]
        for k in range(checks):
            residue = saved[i, k] - living[k]
            for b in range(2):
                term = factors[k, count + 2 + b] * residue
                whole[b] = term if k == 0 else whole[b] + term
        whole = [x * scale for x in whole]
        for k in range(checks):
            fresh[i, k] = (
                living[k] + factors[k, count] * whole[0] + factors[k, count + 1] * whole[1]
            )
        for b in range(2):
            first, final = whole[b][:, :half], whole[b][:, half:]
            keep_edges(count + b, i, first, final)
            whole[b] = jnp.concatenate([first, final], axis=0)
            rebuilt[b, pl.ds(at, wide), :] = whole[b]
        for c in range(count // 2):
            chosen = jnp.where(lost[0] // 2 == c, whole[0], whole[1])
            back[c, pl.ds(at + GROUP, wide), :] = chosen

    def recovered_edges(c):
        if c < 0 or c >= count:
            return jnp.zeros((fields, half), jnp.float32)
        raw = jnp.where(lost[1] == c, edges[count + 1], edges[c])
        return jnp.where(lost[0] == c, edges[count], raw)

    for c in range(0, count, 2):
        near = [recovered_edges(c + d) for d in (-1, 0, 1, 2)]
        both = jnp.where(lane % 2 == 0, near[0], near[2])
        both = both + pltpu.roll(jnp.where(lane % 2 == 0, near[1], near[3]), 2 * rows, 1)
        packed = both[:GROUP]
        for g in range(1, fields // GROUP):
            packed = packed + pltpu.roll(both[g * GROUP : (g + 1) * GROUP], 4 * rows * g, 1)
        back[c // 2, 0:GROUP, :] = packed


def rebuild(failed, weights, strips, saved):
    count, rows, fields, columns = strips.shape
    half = columns // 2
    whole = 2 * rows * fields
    checks = weights.shape[0]
    return pl.pallas_call(
        rebuild_kernel,
        out_shape=(
            jax.ShapeDtypeStruct(saved.shape, jnp.float32),
            jax.ShapeDtypeStruct((2, whole, half), jnp.float32),
            jax.ShapeDtypeStruct((count // 2, GROUP + whole, half), jnp.float32),
            jax.ShapeDtypeStruct((1,), jnp.int32),
        ),
        in_specs=[SMEM, SMEM, VMEM, VMEM],
        out_specs=(VMEM, VMEM, VMEM, SMEM),
        scratch_shapes=[
            pltpu.VMEM((count + 2, fields, half), jnp.float32),
            pltpu.SMEM((checks, count + 4), jnp.float32),
        ],
        compiler_params=pltpu.CompilerParams(vmem_limit_bytes=VMEM_BYTES),
        cost_estimate=pl.CostEstimate(
            flops=8 * strips.size, bytes_accessed=6 * strips.size, transcendentals=0
        ),
    )(failed, weights, strips, saved)


def spread_kernel(failed, rebuilt, short, back):
    lost_a = failed[0, lax.axis_index("row")]
    for c in range(back.shape[0]):
        back[c, 0:GROUP, :] = short[c // 2, 0:GROUP, :]
        back[c, GROUP:, :] = jnp.where(lost_a == c, rebuilt[0], rebuilt[1])


def spread_whole(failed, rebuilt, short):
    chips, lines, half = short.shape
    return pl.pallas_call(
        spread_kernel,
        out_shape=jax.ShapeDtypeStruct((2 * chips, lines, half), jnp.float32),
        in_specs=[SMEM, VMEM, VMEM],
        out_specs=VMEM,
        compiler_params=pltpu.CompilerParams(vmem_limit_bytes=VMEM_BYTES),
    )(failed, rebuilt, short)


def beside(cells):
    half = cells.shape[0] // 2
    return jnp.concatenate([cells[:half], cells[half:]], axis=1)


def below(cells):
    half = cells.shape[1] // 2
    return jnp.concatenate([cells[:, :half], cells[:, half:]], axis=0)


def mix_pair(operator, flat):
    high = flat.astype(jnp.bfloat16)
    low = (flat - high.astype(jnp.float32)).astype(jnp.bfloat16)
    terms = jnp.concatenate([high, low, high], axis=0)
    return flat + jnp.tanh(jnp.dot(operator[...], terms, preferred_element_type=jnp.float32))


def mix_strip(operator, lost, sent, base, ocean, strip, store):
    fields, columns = ocean.shape[1:]
    wide = 2 * fields
    head = None
    for t in range(0, strip, 2):
        units = []
        for q in (t, t + 1):
            own = slice(GROUP + q * wide, GROUP + (q + 1) * wide)
            units.append(jnp.where(lost, beside(sent(own)), ocean[base + q]))
        done = mix_pair(operator, jnp.concatenate(units, axis=0)).reshape(2, fields, columns)
        store(t, done)
        if t == 0:
            head = done[0]
    return head


def my_place(failed):
    line = lax.axis_index("row")
    member = lax.axis_index(MEMBERS)
    lost = (failed[0, line] == member) | (failed[1, line] == member)
    return line, member, member % 2, lost


def double_operator(op):
    fields = op.shape[0]
    wide = 2 * fields
    tall = lax.broadcasted_iota(jnp.int32, (wide, fields), 0) % fields
    tall = (tall == lax.broadcasted_iota(jnp.int32, (wide, fields), 1)).astype(jnp.float32)
    flat = lax.broadcasted_iota(jnp.int32, (fields, wide), 1) % fields
    flat = (flat == lax.broadcasted_iota(jnp.int32, (fields, wide), 0)).astype(jnp.float32)
    exact = dict(preferred_element_type=jnp.float32, precision=lax.Precision.HIGHEST)
    tiled = jnp.dot(jnp.dot(tall, op[...], **exact), flat, **exact)
    down = lax.broadcasted_iota(jnp.int32, (wide, wide), 0) // fields
    across = lax.broadcasted_iota(jnp.int32, (wide, wide), 1) // fields
    both = jnp.where(down == across, tiled, 0.0)
    high = both.astype(jnp.bfloat16)
    low = (both - high.astype(jnp.float32)).astype(jnp.bfloat16)
    return jnp.concatenate([high, high, low], axis=1)


def rows_kernel(whole, failed, ocean, *refs):
    *sent, row_top, row_bottom = refs
    rows, fields, columns = ocean.shape
    wide = 2 * fields
    last = sent[0].shape[0] - 1
    first = slice(GROUP, GROUP + wide)
    final = slice(sent[0].shape[1] - wide, sent[0].shape[1])
    _, _, core, lost = my_place(failed)
    if whole:
        top, bottom = sent[0][0, first, :], sent[0][last, final, :]
    else:
        mine, other = sent
        top = jnp.where(core == 0, mine[0, first, :], other[0, first, :])
        bottom = jnp.where(core == 0, other[last, final, :], mine[last, final, :])
    row_top[...] = jnp.where(lost, top, below(ocean[0]))
    row_bottom[...] = jnp.where(lost, bottom, below(ocean[rows - 1]))


def outer_lines(failed, ocean, sent):
    rows, fields, columns = ocean.shape
    line = jax.ShapeDtypeStruct((2 * fields, columns // 2), jnp.float32)
    return pl.pallas_call(
        functools.partial(rows_kernel, len(sent) == 1),
        out_shape=(line, line),
        in_specs=[SMEM] + [VMEM] * (1 + len(sent)),
        out_specs=(VMEM, VMEM),
        compiler_params=pltpu.CompilerParams(vmem_limit_bytes=VMEM_BYTES),
    )(failed, ocean, *sent)


def first_kernel(
    whole, failed, ocean, sent, op, diffusivity, fresh, strips, operator, number_of, parity, sem
):
    leave = pltpu.make_async_copy(fresh, parity, sem)
    leave.start()
    rows, fields, columns = ocean.shape
    half = columns // 2
    count = 2 * strips.shape[0]
    strip = rows // count
    _, _, core, lost = my_place(failed)
    operator[...] = double_operator(op)
    field = lax.broadcasted_iota(jnp.int32, (fields, half), 0)
    number = jnp.zeros((fields, half), jnp.float32)
    for f in range(fields):
        number = jnp.where(field == f, diffusivity[f], number)
    number_of[...] = number

    @pl.loop(0, count // 2)
    def _(p):
        s = 2 * p + core
        at = s if whole else p

        def store(t, done):
            strips[p, pl.ds(t, 2)] = done

        base = pl.multiple_of(s * strip, strip)
        mix_strip(operator, lost, lambda own: sent[at, own, :], base, ocean, strip, store)

    leave.wait()


def first_half(failed, ocean, sent, op, diffusivity, fresh, whole, count):
    rows, fields, columns = ocean.shape
    half = columns // 2
    wide = 2 * fields
    shapes = [jax.ShapeDtypeStruct((count // 2, rows // count, fields, columns), jnp.float32)]
    shapes.append(jax.ShapeDtypeStruct((wide, 3 * wide), jnp.bfloat16))
    shapes.append(jax.ShapeDtypeStruct((fields, half), jnp.float32))
    shapes.append(jax.ShapeDtypeStruct(fresh.shape, jnp.float32))
    return pl.pallas_call(
        functools.partial(first_kernel, whole),
        out_shape=tuple(shapes),
        in_specs=[SMEM, VMEM, VMEM, VMEM, SMEM, VMEM],
        out_specs=(VMEM, VMEM, VMEM, pl.BlockSpec(memory_space=pl.ANY)),
        scratch_shapes=[pltpu.SemaphoreType.DMA],
        compiler_params=pltpu.CompilerParams(vmem_limit_bytes=VMEM_BYTES),
        cost_estimate=pl.CostEstimate(
            flops=75 * ocean.size, bytes_accessed=4 * ocean.size, transcendentals=ocean.size // 2
        ),
    )(failed, ocean, sent, op, diffusivity, fresh)


def step_kernel(whole, failed, ocean, *refs):
    if whole:
        sent, strips, operator, number_of, above, under, *refs = refs
    else:
        mine, other, strips, operator, number_of, *refs = refs
    out, mixed, sides = refs
    rows, fields, columns = ocean.shape
    half = columns // 2
    wide = 2 * fields
    pairs = strips.shape[0]
    count = 2 * pairs
    strip = rows // count
    _, _, core, lost = my_place(failed)
    lane = lax.broadcasted_iota(jnp.int32, (fields, half), 1)
    number = number_of[...]

    def prepare(p):
        kept = pl.multiple_of((2 * p + core) * strip, strip)
        base = pl.multiple_of((2 * p + 1 - core) * strip, strip)
        at = 2 * p + 1 - core if whole else p
        source = sent if whole else other
        for t in range(0, strip, 2):
            mixed[pl.ds(kept + t + 1, 2)] = strips[p, pl.ds(t, 2)]

        def store(t, done):
            mixed[pl.ds(base + t + 1, 2)] = done

        head = mix_strip(operator, lost, lambda own: source[at, own, :], base, ocean, strip, store)
        return jnp.where(core == 0, strips[p, 0], head)

    def tile_of(s):
        if whole:
            return sent[s, 0:GROUP, :]
        return jnp.where(core == s % 2, mine[s // 2, 0:GROUP, :], other[s // 2, 0:GROUP, :])

    if whole:
        outer = jnp.concatenate([beside(above[...]), beside(under[...])], axis=0)
        outer = mix_pair(operator, outer)
        mixed[0] = outer[:fields]
        mixed[rows + 1] = outer[fields:]
    else:
        mixed[0] = jnp.zeros((fields, columns), jnp.float32)
        mixed[rows + 1] = jnp.zeros((fields, columns), jnp.float32)
    narrow = lane[:GROUP]
    ends = []
    for g in range(fields // GROUP):
        parts = []
        for h in range(2):
            part = jnp.zeros((GROUP, half), jnp.float32)
            for n in range(count // 2):
                tile = tile_of(h * count // 2 + n)
                shift = (2 * strip * (n - 2 * g)) % half
                near = pltpu.roll(tile, shift, 1) if shift else tile
                shift = (2 * strip * (n - 2 * g - 1)) % half
                far = pltpu.roll(tile, shift, 1) if shift else tile
                part = jnp.where(
                    narrow // (2 * strip) == n, jnp.where(core == 0, near, far), part
                )
            parts.append(part)
        ends.append(jnp.concatenate(parts, axis=1))
    ends = jnp.concatenate(ends, axis=0)
    ends = mix_pair(operator, jnp.concatenate([ends, ends], axis=0))[:fields]
    for h in range(2):
        part = ends[:, h * half : (h + 1) * half]
        part = jnp.where(lane % 2 == 0, pltpu.roll(part, half - 1, 1), pltpu.roll(part, 1, 1))
        for n in range(count // 2):
            sides[h * count // 2 + n] = pltpu.roll(part, half - 2 * strip * n, 1) if n else part
    prepare(0)

    def diffuse(s, t, under_row):
        i = s * strip + t + 1
        side = pltpu.roll(sides[s], half - 2 * t - 1, 1)
        for part in range(2):
            own = slice(part * half, (part + 1) * half)
            here = mixed[i, :, own]
            across = mixed[i, :, (1 - part) * half : (2 - part) * half]
            if part == 0:
                west = jnp.where(lane == 0, side, pltpu.roll(here, 1, 1))
                east = pltpu.roll(jnp.where(lane == 0, across, here), half - 1, 1)
            else:
                west = pltpu.roll(jnp.where(lane == half - 1, across, here), 1, 1)
                east = jnp.where(lane == half - 1, side, pltpu.roll(here, half - 1, 1))
            under = mixed[i + 1, :, own] if under_row is None else under_row[:, own]
            around = under + mixed[i - 1, :, own] + east + west
            out[i - 1, :, own] = here + number * (around - 4.0 * here)

    @pl.loop(0, pairs)
    def _(p):
        for t in range(2 * strip - 1):
            diffuse(2 * p + t // strip, t % strip, None)
        head = prepare(jnp.minimum(p + 1, pairs - 1))
        head = jnp.where(p == pairs - 1, mixed[rows + 1], head)
        diffuse(2 * p + 1, strip - 1, head)


def step(failed, ocean, sent, strips, operator, number_of, *outer):
    rows, fields, columns = ocean.shape
    whole = len(sent) == 1
    pairs = strips.shape[0]
    return pl.pallas_call(
        functools.partial(step_kernel, whole),
        out_shape=jax.ShapeDtypeStruct(ocean.shape, jnp.float32),
        in_specs=[SMEM] + [VMEM] * (4 + len(sent) + len(outer)),
        out_specs=VMEM,
        scratch_shapes=[
            pltpu.VMEM((rows + 2, fields, columns), jnp.float32),
            pltpu.VMEM((2 * pairs, fields, columns // 2), jnp.float32),
        ],
        compiler_params=pltpu.CompilerParams(vmem_limit_bytes=VMEM_BYTES),
        cost_estimate=pl.CostEstimate(
            flops=100 * ocean.size, bytes_accessed=12 * ocean.size, transcendentals=ocean.size // 2
        ),
    )(failed, ocean, *sent, strips, operator, number_of, *outer)


def ends_kernel(stepped, above, under, operator, number_of, out, row, sem):
    rows, fields, columns = stepped.shape
    places = (0, rows - 1)
    reads = [
        pltpu.make_async_copy(out.at[at], row.at[n], sem.at[n]) for n, at in enumerate(places)
    ]
    for copy in reads:
        copy.start()
    both = jnp.concatenate([beside(above[...]), beside(under[...])], axis=0)
    both = mix_pair(operator, both)
    number = jnp.concatenate([number_of[...], number_of[...]], axis=1)
    writes = []
    for n, at in enumerate(places):
        reads[n].wait()
        row[n] = row[n] + number * both[n * fields : (n + 1) * fields]
        writes.append(pltpu.make_async_copy(row.at[n], out.at[at], sem.at[n]))
        writes[n].start()
    for copy in writes:
        copy.wait()


def add_ends(stepped, above, under, operator, number_of):
    rows, fields, columns = stepped.shape
    anywhere = pl.BlockSpec(memory_space=pl.ANY)
    return pl.pallas_call(
        ends_kernel,
        out_shape=jax.ShapeDtypeStruct(stepped.shape, jnp.float32),
        in_specs=[anywhere] + [VMEM] * 4,
        out_specs=anywhere,
        input_output_aliases={0: 0},
        scratch_shapes=[
            pltpu.VMEM((2, fields, columns), jnp.float32),
            pltpu.SemaphoreType.DMA((2,)),
        ],
        compiler_params=pltpu.CompilerParams(vmem_limit_bytes=VMEM_BYTES),
    )(stepped, above, under, operator, number_of)


def per_device(
    ocean_state, saved_checksums, checksum_weights, failed_devices, column_op, diffusivity
):
    lines = lax.axis_size("row")
    rows, fields, columns = ocean_state.shape
    count = checksum_weights.shape[1]
    half = columns // 2
    strip = rows // count

    strips = lax.all_to_all(ocean_state, MEMBERS, 0, 0, tiled=True)
    strips, ocean, saved, weights, failed, op, number = lax.optimization_barrier(
        (
            strips,
            ocean_state,
            saved_checksums,
            checksum_weights,
            failed_devices.T,
            column_op,
            diffusivity,
        )
    )
    strips = strips.reshape(count, strip, fields, columns)
    fresh, rebuilt, back, shared = rebuild(failed, weights, strips, saved)

    def exchange_rows(ocean, sent):
        top, bottom = outer_lines(failed, ocean, sent)
        above = lax.ppermute(bottom, "row", [(r, r + 1) for r in range(lines - 1)])
        under = lax.ppermute(top, "row", [(r + 1, r) for r in range(lines - 1)])
        return above, under

    def exchange_chips(rebuilt, back, ocean, fresh):
        mine = lax.all_to_all(back, ("y_hi", "x"), 0, 0, tiled=True)
        mine, ocean = lax.optimization_barrier((mine, ocean))
        other = lax.ppermute(mine, "core", [(0, 1), (1, 0)])
        *kept, parity = first_half(failed, ocean, mine, op, number, fresh, False, count)
        other, kept = lax.optimization_barrier((other, kept))
        above, under = exchange_rows(ocean, (mine, other))
        stepped = step(failed, ocean, (mine, other), *kept)
        return add_ends(stepped, above, under, *kept[1:]), parity

    def exchange_whole(rebuilt, back, ocean, fresh):
        back = spread_whole(failed, rebuilt, back)
        sent = lax.all_to_all(back, MEMBERS, 0, 0, tiled=True)
        sent, ocean = lax.optimization_barrier((sent, ocean))
        above, under = exchange_rows(ocean, (sent,))
        *kept, parity = first_half(failed, ocean, sent, op, number, fresh, True, count)
        return step(failed, ocean, (sent,), *kept, above, under), parity

    return lax.cond(
        shared[0] != 0, exchange_whole, exchange_chips, rebuilt, back, ocean, fresh
    )


def solution(mesh):
    row, col = mesh.axis_names
    shape = (mesh.shape[row], 2, 4, 2)
    chips = jax.sharding.Mesh(mesh.devices.reshape(shape), ("row", "y_hi", "x", "core"))
    col = MEMBERS
    return jax.shard_map(
        per_device,
        mesh=chips,
        in_specs=(P("row", None, col), P(("row", *col), None, None, None), P(), P(), P(), P()),
        out_specs=(P("row", None, col), P(("row", *col), None, None, None)),
        check_vma=False,
    )
```

```python
import functools

import jax
import jax.numpy as jnp
from jax import lax
from jax.experimental import pallas as pl
from jax.experimental.pallas import tpu as pltpu
from jax.sharding import PartitionSpec as P

VMEM_BYTES = 20 * 1024 * 1024
SMEM = pl.BlockSpec(memory_space=pltpu.SMEM)
VMEM = pl.BlockSpec(memory_space=pltpu.VMEM)

GROUP = 8
MEMBERS = ("y_hi", "x", "core")


def column(weights, member):
    return [weights[k, member] for k in range(weights.shape[0])]


def dot(left, right):
    return sum(x * y for x, y in zip(left, right))


def rebuild_kernel(
    failed, weights, strips, saved, fresh, rebuilt, back, shared, edges, factors
):
    count, rows, fields, columns = strips.shape
    checks = saved.shape[1]
    half = columns // 2
    wide = 2 * fields
    lane = lax.broadcasted_iota(jnp.int32, (fields, half), 1)
    edges[...] = jnp.zeros_like(edges)
    line = lax.axis_index("row")
    lost = (failed[0, line], failed[1, line])

    any_shared = jnp.int32(0)
    for r in range(failed.shape[1]):
        any_shared |= (failed[0, r] // 2 == failed[1, r] // 2).astype(jnp.int32)
    shared[0] = any_shared

    u, v = column(weights, lost[0]), column(weights, lost[1])
    gram_aa, gram_bb, gram_ab = dot(u, u) + 1, dot(v, v) + 1, dot(u, v)
    determinant = (gram_aa * gram_bb - gram_ab * gram_ab).astype(jnp.float32)
    scale = 1.0 / jnp.full((fields, columns), determinant, jnp.float32)
    for c in range(count):
        kept = ((lost[0] != c) & (lost[1] != c)).astype(jnp.int32)
        for k in range(checks):
            factors[k, c] = (kept * weights[k, c]).astype(jnp.float32)
    for k in range(checks):
        factors[k, count] = u[k].astype(jnp.float32)
        factors[k, count + 1] = v[k].astype(jnp.float32)
        factors[k, count + 2] = (gram_bb * u[k] - gram_ab * v[k]).astype(jnp.float32)
        factors[k, count + 3] = (gram_aa * v[k] - gram_ab * u[k]).astype(jnp.float32)

    def keep_edges(n, i, first, final):
        ends = pltpu.roll(jnp.where(lane == 0, first, final), 2 * i + 1, 1)
        edges[n] = jnp.where((lane == 2 * i) | (lane == 2 * i + 1), ends, edges[n])

    for i in range(rows):
        at = i * wide
        living = [None] * checks
        for c in range(count):
            block = strips[c, i]
            keep_edges(c, i, block[:, :half], block[:, half:])
            for k in range(checks):
                term = factors[k, c] * block
                living[k] = term if c == 0 else living[k] + term
        whole = [None, None]
        for k in range(checks):
            residue = saved[i, k] - living[k]
            for b in range(2):
                term = factors[k, count + 2 + b] * residue
                whole[b] = term if k == 0 else whole[b] + term
        whole = [x * scale for x in whole]
        for k in range(checks):
            fresh[i, k] = (
                living[k] + factors[k, count] * whole[0] + factors[k, count + 1] * whole[1]
            )
        for b in range(2):
            first, final = whole[b][:, :half], whole[b][:, half:]
            keep_edges(count + b, i, first, final)
            whole[b] = jnp.concatenate([first, final], axis=0)
            rebuilt[b, pl.ds(at, wide), :] = whole[b]
        for c in range(count // 2):
            chosen = jnp.where(lost[0] // 2 == c, whole[0], whole[1])
            back[c, pl.ds(at + GROUP, wide), :] = chosen

    def recovered_edges(c):
        if c < 0 or c >= count:
            return jnp.zeros((fields, half), jnp.float32)
        raw = jnp.where(lost[1] == c, edges[count + 1], edges[c])
        return jnp.where(lost[0] == c, edges[count], raw)

    for c in range(0, count, 2):
        near = [recovered_edges(c + d) for d in (-1, 0, 1, 2)]
        both = jnp.where(lane % 2 == 0, near[0], near[2])
        both = both + pltpu.roll(jnp.where(lane % 2 == 0, near[1], near[3]), 2 * rows, 1)
        packed = both[:GROUP]
        for g in range(1, fields // GROUP):
            packed = packed + pltpu.roll(both[g * GROUP : (g + 1) * GROUP], 4 * rows * g, 1)
        back[c // 2, 0:GROUP, :] = packed


def rebuild(failed, weights, strips, saved):
    count, rows, fields, columns = strips.shape
    half = columns // 2
    whole = 2 * rows * fields
    checks = weights.shape[0]
    return pl.pallas_call(
        rebuild_kernel,
        out_shape=(
            jax.ShapeDtypeStruct(saved.shape, jnp.float32),
            jax.ShapeDtypeStruct((2, whole, half), jnp.float32),
            jax.ShapeDtypeStruct((count // 2, GROUP + whole, half), jnp.float32),
            jax.ShapeDtypeStruct((1,), jnp.int32),
        ),
        in_specs=[SMEM, SMEM, VMEM, VMEM],
        out_specs=(VMEM, VMEM, VMEM, SMEM),
        scratch_shapes=[
            pltpu.VMEM((count + 2, fields, half), jnp.float32),
            pltpu.SMEM((checks, count + 4), jnp.float32),
        ],
        compiler_params=pltpu.CompilerParams(vmem_limit_bytes=VMEM_BYTES),
        cost_estimate=pl.CostEstimate(
            flops=8 * strips.size, bytes_accessed=6 * strips.size, transcendentals=0
        ),
    )(failed, weights, strips, saved)


def spread_kernel(failed, rebuilt, short, back):
    lost_a = failed[0, lax.axis_index("row")]
    for c in range(back.shape[0]):
        back[c, 0:GROUP, :] = short[c // 2, 0:GROUP, :]
        back[c, GROUP:, :] = jnp.where(lost_a == c, rebuilt[0], rebuilt[1])


def spread_whole(failed, rebuilt, short):
    chips, lines, half = short.shape
    return pl.pallas_call(
        spread_kernel,
        out_shape=jax.ShapeDtypeStruct((2 * chips, lines, half), jnp.float32),
        in_specs=[SMEM, VMEM, VMEM],
        out_specs=VMEM,
        compiler_params=pltpu.CompilerParams(vmem_limit_bytes=VMEM_BYTES),
    )(failed, rebuilt, short)


def beside(cells):
    half = cells.shape[0] // 2
    return jnp.concatenate([cells[:half], cells[half:]], axis=1)


def below(cells):
    half = cells.shape[1] // 2
    return jnp.concatenate([cells[:, :half], cells[:, half:]], axis=0)


def mix_pair(operator, flat):
    high = flat.astype(jnp.bfloat16)
    low = (flat - high.astype(jnp.float32)).astype(jnp.bfloat16)
    terms = jnp.concatenate([high, low, high], axis=0)
    return flat + jnp.tanh(jnp.dot(operator[...], terms, preferred_element_type=jnp.float32))


def mix_strip(operator, lost, sent, base, ocean, strip, store):
    fields, columns = ocean.shape[1:]
    wide = 2 * fields
    head = None
    for t in range(0, strip, 2):
        units = []
        for q in (t, t + 1):
            own = slice(GROUP + q * wide, GROUP + (q + 1) * wide)
            units.append(jnp.where(lost, beside(sent(own)), ocean[base + q]))
        done = mix_pair(operator, jnp.concatenate(units, axis=0)).reshape(2, fields, columns)
        store(t, done)
        if t == 0:
            head = done[0]
    return head


def my_place(failed):
    line = lax.axis_index("row")
    member = lax.axis_index(MEMBERS)
    lost = (failed[0, line] == member) | (failed[1, line] == member)
    return line, member, member % 2, lost


def double_operator(op):
    fields = op.shape[0]
    wide = 2 * fields
    tall = lax.broadcasted_iota(jnp.int32, (wide, fields), 0) % fields
    tall = (tall == lax.broadcasted_iota(jnp.int32, (wide, fields), 1)).astype(jnp.float32)
    flat = lax.broadcasted_iota(jnp.int32, (fields, wide), 1) % fields
    flat = (flat == lax.broadcasted_iota(jnp.int32, (fields, wide), 0)).astype(jnp.float32)
    exact = dict(preferred_element_type=jnp.float32, precision=lax.Precision.HIGHEST)
    tiled = jnp.dot(jnp.dot(tall, op[...], **exact), flat, **exact)
    down = lax.broadcasted_iota(jnp.int32, (wide, wide), 0) // fields
    across = lax.broadcasted_iota(jnp.int32, (wide, wide), 1) // fields
    both = jnp.where(down == across, tiled, 0.0)
    high = both.astype(jnp.bfloat16)
    low = (both - high.astype(jnp.float32)).astype(jnp.bfloat16)
    return jnp.concatenate([high, high, low], axis=1)


def rows_kernel(whole, failed, ocean, *refs):
    *sent, row_top, row_bottom = refs
    rows, fields, columns = ocean.shape
    wide = 2 * fields
    last = sent[0].shape[0] - 1
    first = slice(GROUP, GROUP + wide)
    final = slice(sent[0].shape[1] - wide, sent[0].shape[1])
    _, _, core, lost = my_place(failed)
    if whole:
        top, bottom = sent[0][0, first, :], sent[0][last, final, :]
    else:
        mine, other = sent
        top = jnp.where(core == 0, mine[0, first, :], other[0, first, :])
        bottom = jnp.where(core == 0, other[last, final, :], mine[last, final, :])
    row_top[...] = jnp.where(lost, top, below(ocean[0]))
    row_bottom[...] = jnp.where(lost, bottom, below(ocean[rows - 1]))


def outer_lines(failed, ocean, sent):
    rows, fields, columns = ocean.shape
    line = jax.ShapeDtypeStruct((2 * fields, columns // 2), jnp.float32)
    return pl.pallas_call(
        functools.partial(rows_kernel, len(sent) == 1),
        out_shape=(line, line),
        in_specs=[SMEM] + [VMEM] * (1 + len(sent)),
        out_specs=(VMEM, VMEM),
        compiler_params=pltpu.CompilerParams(vmem_limit_bytes=VMEM_BYTES),
    )(failed, ocean, *sent)


def first_kernel(
    whole, failed, ocean, sent, op, diffusivity, fresh, strips, operator, number_of, parity, sem
):
    leave = pltpu.make_async_copy(fresh, parity, sem)
    leave.start()
    rows, fields, columns = ocean.shape
    half = columns // 2
    count = 2 * strips.shape[0]
    strip = rows // count
    _, _, core, lost = my_place(failed)
    operator[...] = double_operator(op)
    field = lax.broadcasted_iota(jnp.int32, (fields, half), 0)
    number = jnp.zeros((fields, half), jnp.float32)
    for f in range(fields):
        number = jnp.where(field == f, diffusivity[f], number)
    number_of[...] = number

    @pl.loop(0, count // 2, unroll=4)
    def _(p):
        s = 2 * p + core
        at = s if whole else p

        def store(t, done):
            strips[p, pl.ds(t, 2)] = done

        base = pl.multiple_of(s * strip, strip)
        mix_strip(operator, lost, lambda own: sent[at, own, :], base, ocean, strip, store)

    leave.wait()


def first_half(failed, ocean, sent, op, diffusivity, fresh, whole, count):
    rows, fields, columns = ocean.shape
    half = columns // 2
    wide = 2 * fields
    shapes = [jax.ShapeDtypeStruct((count // 2, rows // count, fields, columns), jnp.float32)]
    shapes.append(jax.ShapeDtypeStruct((wide, 3 * wide), jnp.bfloat16))
    shapes.append(jax.ShapeDtypeStruct((fields, half), jnp.float32))
    shapes.append(jax.ShapeDtypeStruct(fresh.shape, jnp.float32))
    return pl.pallas_call(
        functools.partial(first_kernel, whole),
        out_shape=tuple(shapes),
        in_specs=[SMEM, VMEM, VMEM, VMEM, SMEM, VMEM],
        out_specs=(VMEM, VMEM, VMEM, pl.BlockSpec(memory_space=pl.ANY)),
        scratch_shapes=[pltpu.SemaphoreType.DMA],
        compiler_params=pltpu.CompilerParams(vmem_limit_bytes=VMEM_BYTES),
        cost_estimate=pl.CostEstimate(
            flops=75 * ocean.size, bytes_accessed=4 * ocean.size, transcendentals=ocean.size // 2
        ),
    )(failed, ocean, sent, op, diffusivity, fresh)


def step_kernel(whole, failed, ocean, *refs):
    if whole:
        sent, strips, operator, number_of, above, under, *refs = refs
    else:
        mine, other, strips, operator, number_of, *refs = refs
    out, mixed, sides = refs
    rows, fields, columns = ocean.shape
    half = columns // 2
    wide = 2 * fields
    pairs = strips.shape[0]
    count = 2 * pairs
    strip = rows // count
    _, _, core, lost = my_place(failed)
    lane = lax.broadcasted_iota(jnp.int32, (fields, half), 1)
    number = number_of[...]

    def prepare(p):
        kept = pl.multiple_of((2 * p + core) * strip, strip)
        base = pl.multiple_of((2 * p + 1 - core) * strip, strip)
        at = 2 * p + 1 - core if whole else p
        source = sent if whole else other
        for t in range(0, strip, 2):
            mixed[pl.ds(kept + t + 1, 2)] = strips[p, pl.ds(t, 2)]

        def store(t, done):
            mixed[pl.ds(base + t + 1, 2)] = done

        head = mix_strip(operator, lost, lambda own: source[at, own, :], base, ocean, strip, store)
        return jnp.where(core == 0, strips[p, 0], head)

    def tile_of(s):
        if whole:
            return sent[s, 0:GROUP, :]
        return jnp.where(core == s % 2, mine[s // 2, 0:GROUP, :], other[s // 2, 0:GROUP, :])

    if whole:
        outer = jnp.concatenate([beside(above[...]), beside(under[...])], axis=0)
        outer = mix_pair(operator, outer)
        mixed[0] = outer[:fields]
        mixed[rows + 1] = outer[fields:]
    else:
        mixed[0] = jnp.zeros((fields, columns), jnp.float32)
        mixed[rows + 1] = jnp.zeros((fields, columns), jnp.float32)
    narrow = lane[:GROUP]
    ends = []
    for g in range(fields // GROUP):
        parts = []
        for h in range(2):
            part = jnp.zeros((GROUP, half), jnp.float32)
            for n in range(count // 2):
                tile = tile_of(h * count // 2 + n)
                shift = (2 * strip * (n - 2 * g)) % half
                near = pltpu.roll(tile, shift, 1) if shift else tile
                shift = (2 * strip * (n - 2 * g - 1)) % half
                far = pltpu.roll(tile, shift, 1) if shift else tile
                part = jnp.where(
                    narrow // (2 * strip) == n, jnp.where(core == 0, near, far), part
                )
            parts.append(part)
        ends.append(jnp.concatenate(parts, axis=1))
    ends = jnp.concatenate(ends, axis=0)
    ends = mix_pair(operator, jnp.concatenate([ends, ends], axis=0))[:fields]
    for h in range(2):
        part = ends[:, h * half : (h + 1) * half]
        part = jnp.where(lane % 2 == 0, pltpu.roll(part, half - 1, 1), pltpu.roll(part, 1, 1))
        for n in range(count // 2):
            sides[h * count // 2 + n] = pltpu.roll(part, half - 2 * strip * n, 1) if n else part
    prepare(0)

    def diffuse(s, t, under_row):
        i = s * strip + t + 1
        side = pltpu.roll(sides[s], half - 2 * t - 1, 1)
        for part in range(2):
            own = slice(part * half, (part + 1) * half)
            here = mixed[i, :, own]
            across = mixed[i, :, (1 - part) * half : (2 - part) * half]
            if part == 0:
                west = jnp.where(lane == 0, side, pltpu.roll(here, 1, 1))
                east = pltpu.roll(jnp.where(lane == 0, across, here), half - 1, 1)
            else:
                west = pltpu.roll(jnp.where(lane == half - 1, across, here), 1, 1)
                east = jnp.where(lane == half - 1, side, pltpu.roll(here, half - 1, 1))
            under = mixed[i + 1, :, own] if under_row is None else under_row[:, own]
            around = under + mixed[i - 1, :, own] + east + west
            out[i - 1, :, own] = here + number * (around - 4.0 * here)

    @pl.loop(0, pairs)
    def _(p):
        for t in range(2 * strip - 1):
            diffuse(2 * p + t // strip, t % strip, None)
        head = prepare(jnp.minimum(p + 1, pairs - 1))
        head = jnp.where(p == pairs - 1, mixed[rows + 1], head)
        diffuse(2 * p + 1, strip - 1, head)


def step(failed, ocean, sent, strips, operator, number_of, *outer):
    rows, fields, columns = ocean.shape
    whole = len(sent) == 1
    pairs = strips.shape[0]
    return pl.pallas_call(
        functools.partial(step_kernel, whole),
        out_shape=jax.ShapeDtypeStruct(ocean.shape, jnp.float32),
        in_specs=[SMEM] + [VMEM] * (4 + len(sent) + len(outer)),
        out_specs=VMEM,
        scratch_shapes=[
            pltpu.VMEM((rows + 2, fields, columns), jnp.float32),
            pltpu.VMEM((2 * pairs, fields, columns // 2), jnp.float32),
        ],
        compiler_params=pltpu.CompilerParams(vmem_limit_bytes=VMEM_BYTES),
        cost_estimate=pl.CostEstimate(
            flops=100 * ocean.size, bytes_accessed=12 * ocean.size, transcendentals=ocean.size // 2
        ),
    )(failed, ocean, *sent, strips, operator, number_of, *outer)


def ends_kernel(stepped, above, under, operator, number_of, out, row, sem):
    rows, fields, columns = stepped.shape
    places = (0, rows - 1)
    reads = [
        pltpu.make_async_copy(out.at[at], row.at[n], sem.at[n]) for n, at in enumerate(places)
    ]
    for copy in reads:
        copy.start()
    both = jnp.concatenate([beside(above[...]), beside(under[...])], axis=0)
    both = mix_pair(operator, both)
    number = jnp.concatenate([number_of[...], number_of[...]], axis=1)
    writes = []
    for n, at in enumerate(places):
        reads[n].wait()
        row[n] = row[n] + number * both[n * fields : (n + 1) * fields]
        writes.append(pltpu.make_async_copy(row.at[n], out.at[at], sem.at[n]))
        writes[n].start()
    for copy in writes:
        copy.wait()


def add_ends(stepped, above, under, operator, number_of):
    rows, fields, columns = stepped.shape
    anywhere = pl.BlockSpec(memory_space=pl.ANY)
    return pl.pallas_call(
        ends_kernel,
        out_shape=jax.ShapeDtypeStruct(stepped.shape, jnp.float32),
        in_specs=[anywhere] + [VMEM] * 4,
        out_specs=anywhere,
        input_output_aliases={0: 0},
        scratch_shapes=[
            pltpu.VMEM((2, fields, columns), jnp.float32),
            pltpu.SemaphoreType.DMA((2,)),
        ],
        compiler_params=pltpu.CompilerParams(vmem_limit_bytes=VMEM_BYTES),
    )(stepped, above, under, operator, number_of)


def per_device(
    ocean_state, saved_checksums, checksum_weights, failed_devices, column_op, diffusivity
):
    lines = lax.axis_size("row")
    rows, fields, columns = ocean_state.shape
    count = checksum_weights.shape[1]
    half = columns // 2
    strip = rows // count

    strips = lax.all_to_all(ocean_state, MEMBERS, 0, 0, tiled=True)
    strips, ocean, saved, weights, failed, op, number = lax.optimization_barrier(
        (
            strips,
            ocean_state,
            saved_checksums,
            checksum_weights,
            failed_devices.T,
            column_op,
            diffusivity,
        )
    )
    strips = strips.reshape(count, strip, fields, columns)
    fresh, rebuilt, back, shared = rebuild(failed, weights, strips, saved)

    def exchange_rows(ocean, sent):
        top, bottom = outer_lines(failed, ocean, sent)
        above = lax.ppermute(bottom, "row", [(r, r + 1) for r in range(lines - 1)])
        under = lax.ppermute(top, "row", [(r + 1, r) for r in range(lines - 1)])
        return above, under

    def exchange_chips(rebuilt, back, ocean, fresh):
        mine = lax.all_to_all(back, ("y_hi", "x"), 0, 0, tiled=True)
        mine, ocean = lax.optimization_barrier((mine, ocean))
        other = lax.ppermute(mine, "core", [(0, 1), (1, 0)])
        *kept, parity = first_half(failed, ocean, mine, op, number, fresh, False, count)
        other, kept = lax.optimization_barrier((other, kept))
        above, under = exchange_rows(ocean, (mine, other))
        stepped = step(failed, ocean, (mine, other), *kept)
        return add_ends(stepped, above, under, *kept[1:]), parity

    def exchange_whole(rebuilt, back, ocean, fresh):
        back = spread_whole(failed, rebuilt, back)
        sent = lax.all_to_all(back, MEMBERS, 0, 0, tiled=True)
        sent, ocean = lax.optimization_barrier((sent, ocean))
        above, under = exchange_rows(ocean, (sent,))
        *kept, parity = first_half(failed, ocean, sent, op, number, fresh, True, count)
        return step(failed, ocean, (sent,), *kept, above, under), parity

    return lax.cond(
        shared[0] != 0, exchange_whole, exchange_chips, rebuilt, back, ocean, fresh
    )


def solution(mesh):
    row, col = mesh.axis_names
    shape = (mesh.shape[row], 2, 4, 2)
    chips = jax.sharding.Mesh(mesh.devices.reshape(shape), ("row", "y_hi", "x", "core"))
    col = MEMBERS
    return jax.shard_map(
        per_device,
        mesh=chips,
        in_specs=(P("row", None, col), P(("row", *col), None, None, None), P(), P(), P(), P()),
        out_specs=(P("row", None, col), P(("row", *col), None, None, None)),
        check_vma=False,
    )
```

```python
import functools

import jax
import jax.numpy as jnp
from jax import lax
from jax.experimental import pallas as pl
from jax.experimental.pallas import tpu as pltpu
from jax.sharding import PartitionSpec as P

VMEM_BYTES = 20 * 1024 * 1024
SMEM = pl.BlockSpec(memory_space=pltpu.SMEM)
VMEM = pl.BlockSpec(memory_space=pltpu.VMEM)

GROUP = 8
MEMBERS = ("y_hi", "x", "core")


def column(weights, member):
    return [weights[k, member] for k in range(weights.shape[0])]


def dot(left, right):
    return sum(x * y for x, y in zip(left, right))


def rebuild_kernel(
    failed, weights, strips, saved, fresh, rebuilt, back, shared, edges, factors
):
    count, rows, fields, columns = strips.shape
    checks = saved.shape[1]
    half = columns // 2
    wide = 2 * fields
    lane = lax.broadcasted_iota(jnp.int32, (fields, half), 1)
    edges[...] = jnp.zeros_like(edges)
    line = lax.axis_index("row")
    lost = (failed[0, line], failed[1, line])

    any_shared = jnp.int32(0)
    for r in range(failed.shape[1]):
        any_shared |= (failed[0, r] // 2 == failed[1, r] // 2).astype(jnp.int32)
    shared[0] = any_shared

    u, v = column(weights, lost[0]), column(weights, lost[1])
    gram_aa, gram_bb, gram_ab = dot(u, u) + 1, dot(v, v) + 1, dot(u, v)
    determinant = (gram_aa * gram_bb - gram_ab * gram_ab).astype(jnp.float32)
    scale = 1.0 / jnp.full((fields, columns), determinant, jnp.float32)
    for c in range(count):
        kept = ((lost[0] != c) & (lost[1] != c)).astype(jnp.int32)
        for k in range(checks):
            factors[k, c] = (kept * weights[k, c]).astype(jnp.float32)
    for k in range(checks):
        factors[k, count] = u[k].astype(jnp.float32)
        factors[k, count + 1] = v[k].astype(jnp.float32)
        factors[k, count + 2] = (gram_bb * u[k] - gram_ab * v[k]).astype(jnp.float32)
        factors[k, count + 3] = (gram_aa * v[k] - gram_ab * u[k]).astype(jnp.float32)

    def keep_edges(n, i, first, final):
        ends = pltpu.roll(jnp.where(lane == 0, first, final), 2 * i + 1, 1)
        edges[n] = jnp.where((lane == 2 * i) | (lane == 2 * i + 1), ends, edges[n])

    for i in range(rows):
        at = i * wide
        living = [None] * checks
        for c in range(count):
            block = strips[c, i]
            keep_edges(c, i, block[:, :half], block[:, half:])
            for k in range(checks):
                term = factors[k, c] * block
                living[k] = term if c == 0 else living[k] + term
        whole = [None, None]
        for k in range(checks):
            residue = saved[i, k] - living[k]
            for b in range(2):
                term = factors[k, count + 2 + b] * residue
                whole[b] = term if k == 0 else whole[b] + term
        whole = [x * scale for x in whole]
        for k in range(checks):
            fresh[i, k] = (
                living[k] + factors[k, count] * whole[0] + factors[k, count + 1] * whole[1]
            )
        for b in range(2):
            first, final = whole[b][:, :half], whole[b][:, half:]
            keep_edges(count + b, i, first, final)
            whole[b] = jnp.concatenate([first, final], axis=0)
            rebuilt[b, pl.ds(at, wide), :] = whole[b]
        for c in range(count // 2):
            chosen = jnp.where(lost[0] // 2 == c, whole[0], whole[1])
            back[c, pl.ds(at + GROUP, wide), :] = chosen

    def recovered_edges(c):
        if c < 0 or c >= count:
            return jnp.zeros((fields, half), jnp.float32)
        raw = jnp.where(lost[1] == c, edges[count + 1], edges[c])
        return jnp.where(lost[0] == c, edges[count], raw)

    for c in range(0, count, 2):
        near = [recovered_edges(c + d) for d in (-1, 0, 1, 2)]
        both = jnp.where(lane % 2 == 0, near[0], near[2])
        both = both + pltpu.roll(jnp.where(lane % 2 == 0, near[1], near[3]), 2 * rows, 1)
        packed = both[:GROUP]
        for g in range(1, fields // GROUP):
            packed = packed + pltpu.roll(both[g * GROUP : (g + 1) * GROUP], 4 * rows * g, 1)
        back[c // 2, 0:GROUP, :] = packed


def rebuild(failed, weights, strips, saved):
    count, rows, fields, columns = strips.shape
    half = columns // 2
    whole = 2 * rows * fields
    checks = weights.shape[0]
    return pl.pallas_call(
        rebuild_kernel,
        out_shape=(
            jax.ShapeDtypeStruct(saved.shape, jnp.float32),
            jax.ShapeDtypeStruct((2, whole, half), jnp.float32),
            jax.ShapeDtypeStruct((count // 2, GROUP + whole, half), jnp.float32),
            jax.ShapeDtypeStruct((1,), jnp.int32),
        ),
        in_specs=[SMEM, SMEM, VMEM, VMEM],
        out_specs=(VMEM, VMEM, VMEM, SMEM),
        scratch_shapes=[
            pltpu.VMEM((count + 2, fields, half), jnp.float32),
            pltpu.SMEM((checks, count + 4), jnp.float32),
        ],
        compiler_params=pltpu.CompilerParams(vmem_limit_bytes=VMEM_BYTES),
        cost_estimate=pl.CostEstimate(
            flops=8 * strips.size, bytes_accessed=6 * strips.size, transcendentals=0
        ),
    )(failed, weights, strips, saved)


def spread_kernel(failed, rebuilt, short, back):
    lost_a = failed[0, lax.axis_index("row")]
    for c in range(back.shape[0]):
        back[c, 0:GROUP, :] = short[c // 2, 0:GROUP, :]
        back[c, GROUP:, :] = jnp.where(lost_a == c, rebuilt[0], rebuilt[1])


def spread_whole(failed, rebuilt, short):
    chips, lines, half = short.shape
    return pl.pallas_call(
        spread_kernel,
        out_shape=jax.ShapeDtypeStruct((2 * chips, lines, half), jnp.float32),
        in_specs=[SMEM, VMEM, VMEM],
        out_specs=VMEM,
        compiler_params=pltpu.CompilerParams(vmem_limit_bytes=VMEM_BYTES),
    )(failed, rebuilt, short)


def beside(cells):
    half = cells.shape[0] // 2
    return jnp.concatenate([cells[:half], cells[half:]], axis=1)


def below(cells):
    half = cells.shape[1] // 2
    return jnp.concatenate([cells[:, :half], cells[:, half:]], axis=0)


def mix_pair(operator, flat):
    high = flat.astype(jnp.bfloat16)
    low = (flat - high.astype(jnp.float32)).astype(jnp.bfloat16)
    terms = jnp.concatenate([high, low, high], axis=0)
    return flat + jnp.tanh(jnp.dot(operator[...], terms, preferred_element_type=jnp.float32))


def mix_strip(operator, lost, sent, base, ocean, strip, store):
    fields, columns = ocean.shape[1:]
    wide = 2 * fields
    head = None
    for t in range(0, strip, 2):
        units = []
        for q in (t, t + 1):
            own = slice(GROUP + q * wide, GROUP + (q + 1) * wide)
            units.append(jnp.where(lost, beside(sent(own)), ocean[base + q]))
        done = mix_pair(operator, jnp.concatenate(units, axis=0)).reshape(2, fields, columns)
        store(t, done)
        if t == 0:
            head = done[0]
    return head


def my_place(failed):
    line = lax.axis_index("row")
    member = lax.axis_index(MEMBERS)
    lost = (failed[0, line] == member) | (failed[1, line] == member)
    return line, member, member % 2, lost


def double_operator(op):
    fields = op.shape[0]
    wide = 2 * fields
    tall = lax.broadcasted_iota(jnp.int32, (wide, fields), 0) % fields
    tall = (tall == lax.broadcasted_iota(jnp.int32, (wide, fields), 1)).astype(jnp.float32)
    flat = lax.broadcasted_iota(jnp.int32, (fields, wide), 1) % fields
    flat = (flat == lax.broadcasted_iota(jnp.int32, (fields, wide), 0)).astype(jnp.float32)
    exact = dict(preferred_element_type=jnp.float32, precision=lax.Precision.HIGHEST)
    tiled = jnp.dot(jnp.dot(tall, op[...], **exact), flat, **exact)
    down = lax.broadcasted_iota(jnp.int32, (wide, wide), 0) // fields
    across = lax.broadcasted_iota(jnp.int32, (wide, wide), 1) // fields
    both = jnp.where(down == across, tiled, 0.0)
    high = both.astype(jnp.bfloat16)
    low = (both - high.astype(jnp.float32)).astype(jnp.bfloat16)
    return jnp.concatenate([high, high, low], axis=1)


def strip_sides(operator, tiles, core, shape, strip):
    fields, half = shape
    lane = lax.broadcasted_iota(jnp.int32, shape, 1)
    narrow = lane[:GROUP]
    ends = []
    for g in range(fields // GROUP):
        part = jnp.zeros((GROUP, half), jnp.float32)
        for n, tile in enumerate(tiles):
            shift = (2 * strip * (n - 2 * g)) % half
            near = pltpu.roll(tile, shift, 1) if shift else tile
            shift = (2 * strip * (n - 2 * g - 1)) % half
            far = pltpu.roll(tile, shift, 1) if shift else tile
            part = jnp.where(narrow // (2 * strip) == n, jnp.where(core == 0, near, far), part)
        ends.append(part)
    ends = jnp.concatenate(ends, axis=0)
    ends = jnp.concatenate([ends, ends], axis=1)
    ends = mix_pair(operator, jnp.concatenate([ends, ends], axis=0))[:fields, :half]
    ends = jnp.where(lane % 2 == 0, pltpu.roll(ends, half - 1, 1), pltpu.roll(ends, 1, 1))
    return [pltpu.roll(ends, half - 2 * strip * n, 1) if n else ends for n in range(len(tiles))]


def diffuse_row(read, store, side, t, number):
    fields, half = number.shape
    lane = lax.broadcasted_iota(jnp.int32, (fields, half), 1)
    side = pltpu.roll(side, half - 2 * t - 1, 1)
    for part in range(2):
        own = slice(part * half, (part + 1) * half)
        here = read(0, own)
        across = read(0, slice((1 - part) * half, (2 - part) * half))
        if part == 0:
            west = jnp.where(lane == 0, side, pltpu.roll(here, 1, 1))
            east = pltpu.roll(jnp.where(lane == 0, across, here), half - 1, 1)
        else:
            west = pltpu.roll(jnp.where(lane == half - 1, across, here), 1, 1)
            east = jnp.where(lane == half - 1, side, pltpu.roll(here, half - 1, 1))
        around = read(1, own) + read(-1, own) + east + west
        store(own, here + number * (around - 4.0 * here))


def rows_kernel(whole, failed, ocean, *refs):
    *sent, row_top, row_bottom = refs
    rows, fields, columns = ocean.shape
    wide = 2 * fields
    last = sent[0].shape[0] - 1
    first = slice(GROUP, GROUP + wide)
    final = slice(sent[0].shape[1] - wide, sent[0].shape[1])
    _, _, core, lost = my_place(failed)
    if whole:
        top, bottom = sent[0][0, first, :], sent[0][last, final, :]
    else:
        mine, other = sent
        top = jnp.where(core == 0, mine[0, first, :], other[0, first, :])
        bottom = jnp.where(core == 0, other[last, final, :], mine[last, final, :])
    row_top[...] = jnp.where(lost, top, below(ocean[0]))
    row_bottom[...] = jnp.where(lost, bottom, below(ocean[rows - 1]))


def outer_lines(failed, ocean, sent):
    rows, fields, columns = ocean.shape
    line = jax.ShapeDtypeStruct((2 * fields, columns // 2), jnp.float32)
    return pl.pallas_call(
        functools.partial(rows_kernel, len(sent) == 1),
        out_shape=(line, line),
        in_specs=[SMEM] + [VMEM] * (1 + len(sent)),
        out_specs=(VMEM, VMEM),
        compiler_params=pltpu.CompilerParams(vmem_limit_bytes=VMEM_BYTES),
    )(failed, ocean, *sent)


def first_kernel(
    whole,
    failed,
    ocean,
    sent,
    op,
    diffusivity,
    fresh,
    strips,
    operator,
    number_of,
    inner,
    sides,
    parity,
    sem,
):
    leave = pltpu.make_async_copy(fresh, parity, sem)
    leave.start()
    rows, fields, columns = ocean.shape
    half = columns // 2
    count = 2 * strips.shape[0]
    strip = rows // count
    _, _, core, lost = my_place(failed)
    operator[...] = double_operator(op)
    field = lax.broadcasted_iota(jnp.int32, (fields, half), 0)
    number = jnp.zeros((fields, half), jnp.float32)
    for f in range(fields):
        number = jnp.where(field == f, diffusivity[f], number)
    number_of[...] = number

    def source(p):
        return 2 * p + core if whole else p

    tiles = [sent[source(p), 0:GROUP, :] for p in range(count // 2)]
    for p, side in enumerate(strip_sides(operator, tiles, core, (fields, half), strip)):
        sides[p] = side

    def mix(p):
        def store(t, done):
            strips[p, pl.ds(t, 2)] = done

        base = pl.multiple_of((2 * p + core) * strip, strip)
        at = source(p)
        mix_strip(operator, lost, lambda own: sent[at, own, :], base, ocean, strip, store)

    mix(0)

    @pl.loop(0, count // 2, unroll=4)
    def _(p):
        for t in range(1, strip - 1):

            def store(own, cells):
                inner[p, t - 1, :, own] = cells

            diffuse_row(lambda d, own: strips[p, t + d, :, own], store, sides[p], t, number)
        mix(jnp.minimum(p + 1, count // 2 - 1))

    leave.wait()


def first_half(failed, ocean, sent, op, diffusivity, fresh, whole, count):
    rows, fields, columns = ocean.shape
    half = columns // 2
    wide = 2 * fields
    shapes = [jax.ShapeDtypeStruct((count // 2, rows // count, fields, columns), jnp.float32)]
    shapes.append(jax.ShapeDtypeStruct((wide, 3 * wide), jnp.bfloat16))
    shapes.append(jax.ShapeDtypeStruct((fields, half), jnp.float32))
    inner = (count // 2, rows // count - 2, fields, columns)
    shapes.append(jax.ShapeDtypeStruct(inner, jnp.float32))
    shapes.append(jax.ShapeDtypeStruct((count // 2, fields, half), jnp.float32))
    shapes.append(jax.ShapeDtypeStruct(fresh.shape, jnp.float32))
    return pl.pallas_call(
        functools.partial(first_kernel, whole),
        out_shape=tuple(shapes),
        in_specs=[SMEM, VMEM, VMEM, VMEM, SMEM, VMEM],
        out_specs=(VMEM,) * 5 + (pl.BlockSpec(memory_space=pl.ANY),),
        scratch_shapes=[pltpu.SemaphoreType.DMA],
        compiler_params=pltpu.CompilerParams(vmem_limit_bytes=VMEM_BYTES),
        cost_estimate=pl.CostEstimate(
            flops=75 * ocean.size, bytes_accessed=4 * ocean.size, transcendentals=ocean.size // 2
        ),
    )(failed, ocean, sent, op, diffusivity, fresh)


def step_kernel(whole, failed, ocean, *refs):
    if whole:
        sent, strips, operator, number_of, inner, near, above, under, *refs = refs
    else:
        mine, other, strips, operator, number_of, inner, near, *refs = refs
    out, mixed, sides = refs
    rows, fields, columns = ocean.shape
    half = columns // 2
    wide = 2 * fields
    pairs = strips.shape[0]
    count = 2 * pairs
    strip = rows // count
    _, _, core, lost = my_place(failed)
    number = number_of[...]

    def prepare(p):
        kept = pl.multiple_of((2 * p + core) * strip, strip)
        base = pl.multiple_of((2 * p + 1 - core) * strip, strip)
        at = 2 * p + 1 - core if whole else p
        source = sent if whole else other
        for t in range(0, strip, 2):
            mixed[pl.ds(kept + t + 1, 2)] = strips[p, pl.ds(t, 2)]

        def store(t, done):
            mixed[pl.ds(base + t + 1, 2)] = done

        head = mix_strip(operator, lost, lambda own: source[at, own, :], base, ocean, strip, store)
        return jnp.where(core == 0, strips[p, 0], head)

    if whole:
        outer = jnp.concatenate([beside(above[...]), beside(under[...])], axis=0)
        outer = mix_pair(operator, outer)
        mixed[0] = outer[:fields]
        mixed[rows + 1] = outer[fields:]
    else:
        mixed[0] = jnp.zeros((fields, columns), jnp.float32)
        mixed[rows + 1] = jnp.zeros((fields, columns), jnp.float32)
    tiles = []
    for p in range(pairs):
        tiles.append(sent[2 * p + 1 - core, 0:GROUP, :] if whole else other[p, 0:GROUP, :])
    for p, side in enumerate(strip_sides(operator, tiles, core, (fields, half), strip)):
        sides[2 * p + 1 - core] = side
        sides[2 * p + core] = near[p]
    prepare(0)

    def diffuse(s, t, under_row=None):
        i = s * strip + t + 1

        def read(d, own):
            if d == 1 and under_row is not None:
                return under_row[:, own]
            return mixed[i + d, :, own]

        def store(own, cells):
            out[i - 1, :, own] = cells

        diffuse_row(read, store, sides[s], t, number)

    @pl.loop(0, pairs, unroll=2)
    def _(p):
        out[pl.ds((2 * p + core) * strip + 1, strip - 2)] = inner[p]
        diffuse(2 * p, 0)
        for t in range(1, strip - 1):
            diffuse(2 * p + 1 - core, t)
        diffuse(2 * p, strip - 1)
        diffuse(2 * p + 1, 0)
        head = prepare(jnp.minimum(p + 1, pairs - 1))
        head = jnp.where(p == pairs - 1, mixed[rows + 1], head)
        diffuse(2 * p + 1, strip - 1, head)


def step(failed, ocean, sent, strips, operator, number_of, inner, near, *outer):
    rows, fields, columns = ocean.shape
    whole = len(sent) == 1
    pairs = strips.shape[0]
    return pl.pallas_call(
        functools.partial(step_kernel, whole),
        out_shape=jax.ShapeDtypeStruct(ocean.shape, jnp.float32),
        in_specs=[SMEM] + [VMEM] * (6 + len(sent) + len(outer)),
        out_specs=VMEM,
        scratch_shapes=[
            pltpu.VMEM((rows + 2, fields, columns), jnp.float32),
            pltpu.VMEM((2 * pairs, fields, columns // 2), jnp.float32),
        ],
        compiler_params=pltpu.CompilerParams(vmem_limit_bytes=VMEM_BYTES),
        cost_estimate=pl.CostEstimate(
            flops=100 * ocean.size, bytes_accessed=12 * ocean.size, transcendentals=ocean.size // 2
        ),
    )(failed, ocean, *sent, strips, operator, number_of, inner, near, *outer)


def ends_kernel(stepped, above, under, operator, number_of, out, row, sem):
    rows, fields, columns = stepped.shape
    places = (0, rows - 1)
    reads = [
        pltpu.make_async_copy(out.at[at], row.at[n], sem.at[n]) for n, at in enumerate(places)
    ]
    for copy in reads:
        copy.start()
    both = jnp.concatenate([beside(above[...]), beside(under[...])], axis=0)
    both = mix_pair(operator, both)
    number = jnp.concatenate([number_of[...], number_of[...]], axis=1)
    writes = []
    for n, at in enumerate(places):
        reads[n].wait()
        row[n] = row[n] + number * both[n * fields : (n + 1) * fields]
        writes.append(pltpu.make_async_copy(row.at[n], out.at[at], sem.at[n]))
        writes[n].start()
    for copy in writes:
        copy.wait()


def add_ends(stepped, above, under, operator, number_of):
    rows, fields, columns = stepped.shape
    anywhere = pl.BlockSpec(memory_space=pl.ANY)
    return pl.pallas_call(
        ends_kernel,
        out_shape=jax.ShapeDtypeStruct(stepped.shape, jnp.float32),
        in_specs=[anywhere] + [VMEM] * 4,
        out_specs=anywhere,
        input_output_aliases={0: 0},
        scratch_shapes=[
            pltpu.VMEM((2, fields, columns), jnp.float32),
            pltpu.SemaphoreType.DMA((2,)),
        ],
        compiler_params=pltpu.CompilerParams(vmem_limit_bytes=VMEM_BYTES),
    )(stepped, above, under, operator, number_of)


def per_device(
    ocean_state, saved_checksums, checksum_weights, failed_devices, column_op, diffusivity
):
    lines = lax.axis_size("row")
    rows, fields, columns = ocean_state.shape
    count = checksum_weights.shape[1]
    half = columns // 2
    strip = rows // count

    strips = lax.all_to_all(ocean_state, MEMBERS, 0, 0, tiled=True)
    strips, ocean, saved, weights, failed, op, number = lax.optimization_barrier(
        (
            strips,
            ocean_state,
            saved_checksums,
            checksum_weights,
            failed_devices.T,
            column_op,
            diffusivity,
        )
    )
    strips = strips.reshape(count, strip, fields, columns)
    fresh, rebuilt, back, shared = rebuild(failed, weights, strips, saved)

    def exchange_rows(ocean, sent):
        top, bottom = outer_lines(failed, ocean, sent)
        above = lax.ppermute(bottom, "row", [(r, r + 1) for r in range(lines - 1)])
        under = lax.ppermute(top, "row", [(r + 1, r) for r in range(lines - 1)])
        return above, under

    def exchange_chips(rebuilt, back, ocean, fresh):
        mine = lax.all_to_all(back, ("y_hi", "x"), 0, 0, tiled=True)
        mine, ocean = lax.optimization_barrier((mine, ocean))
        other = lax.ppermute(mine, "core", [(0, 1), (1, 0)])
        *kept, parity = first_half(failed, ocean, mine, op, number, fresh, False, count)
        other, kept = lax.optimization_barrier((other, kept))
        above, under = exchange_rows(ocean, (mine, other))
        stepped = step(failed, ocean, (mine, other), *kept)
        return add_ends(stepped, above, under, *kept[1:3]), parity

    def exchange_whole(rebuilt, back, ocean, fresh):
        back = spread_whole(failed, rebuilt, back)
        sent = lax.all_to_all(back, MEMBERS, 0, 0, tiled=True)
        sent, ocean = lax.optimization_barrier((sent, ocean))
        above, under = exchange_rows(ocean, (sent,))
        *kept, parity = first_half(failed, ocean, sent, op, number, fresh, True, count)
        return step(failed, ocean, (sent,), *kept, above, under), parity

    return lax.cond(
        shared[0] != 0, exchange_whole, exchange_chips, rebuilt, back, ocean, fresh
    )


def solution(mesh):
    row, col = mesh.axis_names
    shape = (mesh.shape[row], 2, 4, 2)
    chips = jax.sharding.Mesh(mesh.devices.reshape(shape), ("row", "y_hi", "x", "core"))
    col = MEMBERS
    return jax.shard_map(
        per_device,
        mesh=chips,
        in_specs=(P("row", None, col), P(("row", *col), None, None, None), P(), P(), P(), P()),
        out_specs=(P("row", None, col), P(("row", *col), None, None, None)),
        check_vma=False,
    )
```

```python
import functools

import jax
import jax.numpy as jnp
from jax import lax
from jax.experimental import pallas as pl
from jax.experimental.pallas import tpu as pltpu
from jax.sharding import PartitionSpec as P

VMEM_BYTES = 20 * 1024 * 1024
SMEM = pl.BlockSpec(memory_space=pltpu.SMEM)
VMEM = pl.BlockSpec(memory_space=pltpu.VMEM)

GROUP = 8
MEMBERS = ("y_hi", "x", "core")
CHIPS = ("x", "y_hi")


def chip_slot(chip):
    return (chip & 3) * 2 + (chip >> 2)


def column(weights, member):
    return [weights[k, member] for k in range(weights.shape[0])]


def dot(left, right):
    return sum(x * y for x, y in zip(left, right))


def rebuild_kernel(
    failed, weights, strips, saved, fresh, rebuilt, back, shared, edges, factors
):
    count, rows, fields, columns = strips.shape
    checks = saved.shape[1]
    half = columns // 2
    wide = 2 * fields
    lane = lax.broadcasted_iota(jnp.int32, (fields, half), 1)
    edges[...] = jnp.zeros_like(edges)
    line = lax.axis_index("row")
    lost = (failed[0, line], failed[1, line])

    any_shared = jnp.int32(0)
    for r in range(failed.shape[1]):
        any_shared |= ((failed[0, r] >> 1) == (failed[1, r] >> 1)).astype(jnp.int32)
    shared[0] = any_shared

    u, v = column(weights, lost[0]), column(weights, lost[1])
    gram_aa, gram_bb, gram_ab = dot(u, u) + 1, dot(v, v) + 1, dot(u, v)
    determinant = (gram_aa * gram_bb - gram_ab * gram_ab).astype(jnp.float32)
    scale = 1.0 / jnp.full((fields, columns), determinant, jnp.float32)
    for c in range(count):
        kept = ((lost[0] != c) & (lost[1] != c)).astype(jnp.int32)
        for k in range(checks):
            factors[k, c] = (kept * weights[k, c]).astype(jnp.float32)
    for k in range(checks):
        factors[k, count] = u[k].astype(jnp.float32)
        factors[k, count + 1] = v[k].astype(jnp.float32)
        factors[k, count + 2] = (gram_bb * u[k] - gram_ab * v[k]).astype(jnp.float32)
        factors[k, count + 3] = (gram_aa * v[k] - gram_ab * u[k]).astype(jnp.float32)

    def keep_edges(n, i, first, final):
        ends = pltpu.roll(jnp.where(lane == 0, first, final), 2 * i + 1, 1)
        edges[n] = jnp.where((lane == 2 * i) | (lane == 2 * i + 1), ends, edges[n])

    for i in range(rows):
        at = i * wide
        living = [None] * checks
        for c in range(count):
            block = strips[c, i]
            keep_edges(c, i, block[:, :half], block[:, half:])
            for k in range(checks):
                term = factors[k, c] * block
                living[k] = term if c == 0 else living[k] + term
        whole = [None, None]
        for k in range(checks):
            residue = saved[i, k] - living[k]
            for b in range(2):
                term = factors[k, count + 2 + b] * residue
                whole[b] = term if k == 0 else whole[b] + term
        whole = [x * scale for x in whole]
        for k in range(checks):
            fresh[i, k] = (
                living[k] + factors[k, count] * whole[0] + factors[k, count + 1] * whole[1]
            )
        for b in range(2):
            first, final = whole[b][:, :half], whole[b][:, half:]
            keep_edges(count + b, i, first, final)
            whole[b] = jnp.concatenate([first, final], axis=0)
            rebuilt[b, pl.ds(at, wide), :] = whole[b]
        for c in range(count // 2):
            chosen = jnp.where((lost[0] >> 1) == c, whole[0], whole[1])
            back[chip_slot(c), pl.ds(at + GROUP, wide), :] = chosen

    def recovered_edges(c):
        if c < 0 or c >= count:
            return jnp.zeros((fields, half), jnp.float32)
        raw = jnp.where(lost[1] == c, edges[count + 1], edges[c])
        return jnp.where(lost[0] == c, edges[count], raw)

    for c in range(0, count, 2):
        near = [recovered_edges(c + d) for d in (-1, 0, 1, 2)]
        both = jnp.where(lane % 2 == 0, near[0], near[2])
        both = both + pltpu.roll(jnp.where(lane % 2 == 0, near[1], near[3]), 2 * rows, 1)
        packed = both[:GROUP]
        for g in range(1, fields // GROUP):
            packed = packed + pltpu.roll(both[g * GROUP : (g + 1) * GROUP], 4 * rows * g, 1)
        back[chip_slot(c // 2), 0:GROUP, :] = packed


def rebuild(failed, weights, strips, saved):
    count, rows, fields, columns = strips.shape
    half = columns // 2
    whole = 2 * rows * fields
    checks = weights.shape[0]
    return pl.pallas_call(
        rebuild_kernel,
        out_shape=(
            jax.ShapeDtypeStruct(saved.shape, jnp.float32),
            jax.ShapeDtypeStruct((2, whole, half), jnp.float32),
            jax.ShapeDtypeStruct((count // 2, GROUP + whole, half), jnp.float32),
            jax.ShapeDtypeStruct((1,), jnp.int32),
        ),
        in_specs=[SMEM, SMEM, VMEM, VMEM],
        out_specs=(VMEM, VMEM, VMEM, SMEM),
        scratch_shapes=[
            pltpu.VMEM((count + 2, fields, half), jnp.float32),
            pltpu.SMEM((checks, count + 4), jnp.float32),
        ],
        compiler_params=pltpu.CompilerParams(vmem_limit_bytes=VMEM_BYTES),
        cost_estimate=pl.CostEstimate(
            flops=8 * strips.size, bytes_accessed=6 * strips.size, transcendentals=0
        ),
    )(failed, weights, strips, saved)


def spread_kernel(failed, rebuilt, short, back):
    lost_a = failed[0, lax.axis_index("row")]
    for c in range(back.shape[0]):
        back[c, 0:GROUP, :] = short[chip_slot(c // 2), 0:GROUP, :]
        back[c, GROUP:, :] = jnp.where(lost_a == c, rebuilt[0], rebuilt[1])


def spread_whole(failed, rebuilt, short):
    chips, lines, half = short.shape
    return pl.pallas_call(
        spread_kernel,
        out_shape=jax.ShapeDtypeStruct((2 * chips, lines, half), jnp.float32),
        in_specs=[SMEM, VMEM, VMEM],
        out_specs=VMEM,
        compiler_params=pltpu.CompilerParams(vmem_limit_bytes=VMEM_BYTES),
    )(failed, rebuilt, short)


def beside(cells):
    half = cells.shape[0] // 2
    return jnp.concatenate([cells[:half], cells[half:]], axis=1)


def below(cells):
    half = cells.shape[1] // 2
    return jnp.concatenate([cells[:, :half], cells[:, half:]], axis=0)


def mix_pair(operator, flat):
    high = flat.astype(jnp.bfloat16)
    low = (flat - high.astype(jnp.float32)).astype(jnp.bfloat16)
    terms = jnp.concatenate([high, low, high], axis=0)
    return flat + jnp.tanh(jnp.dot(operator[...], terms, preferred_element_type=jnp.float32))


def mix_strip(operator, lost, sent, base, ocean, strip, store):
    fields, columns = ocean.shape[1:]
    wide = 2 * fields
    head = None
    for t in range(0, strip, 2):
        units = []
        for q in (t, t + 1):
            own = slice(GROUP + q * wide, GROUP + (q + 1) * wide)
            units.append(jnp.where(lost, beside(sent(own)), ocean[base + q]))
        done = mix_pair(operator, jnp.concatenate(units, axis=0)).reshape(2, fields, columns)
        store(t, done)
        if t == 0:
            head = done[0]
    return head


def my_place(failed):
    line = lax.axis_index("row")
    member = lax.axis_index(MEMBERS)
    lost = (failed[0, line] == member) | (failed[1, line] == member)
    return line, member, member % 2, lost


def double_operator(op):
    fields = op.shape[0]
    wide = 2 * fields
    tall = lax.broadcasted_iota(jnp.int32, (wide, fields), 0) % fields
    tall = (tall == lax.broadcasted_iota(jnp.int32, (wide, fields), 1)).astype(jnp.float32)
    flat = lax.broadcasted_iota(jnp.int32, (fields, wide), 1) % fields
    flat = (flat == lax.broadcasted_iota(jnp.int32, (fields, wide), 0)).astype(jnp.float32)
    exact = dict(preferred_element_type=jnp.float32, precision=lax.Precision.HIGHEST)
    tiled = jnp.dot(jnp.dot(tall, op[...], **exact), flat, **exact)
    down = lax.broadcasted_iota(jnp.int32, (wide, wide), 0) // fields
    across = lax.broadcasted_iota(jnp.int32, (wide, wide), 1) // fields
    both = jnp.where(down == across, tiled, 0.0)
    high = both.astype(jnp.bfloat16)
    low = (both - high.astype(jnp.float32)).astype(jnp.bfloat16)
    return jnp.concatenate([high, high, low], axis=1)


def strip_sides(operator, tiles, core, shape, strip):
    fields, half = shape
    lane = lax.broadcasted_iota(jnp.int32, shape, 1)
    narrow = lane[:GROUP]
    ends = []
    for g in range(fields // GROUP):
        part = jnp.zeros((GROUP, half), jnp.float32)
        for n, tile in enumerate(tiles):
            shift = (2 * strip * (n - 2 * g)) % half
            near = pltpu.roll(tile, shift, 1) if shift else tile
            shift = (2 * strip * (n - 2 * g - 1)) % half
            far = pltpu.roll(tile, shift, 1) if shift else tile
            part = jnp.where(narrow // (2 * strip) == n, jnp.where(core == 0, near, far), part)
        ends.append(part)
    ends = jnp.concatenate(ends, axis=0)
    ends = jnp.concatenate([ends, ends], axis=1)
    ends = mix_pair(operator, jnp.concatenate([ends, ends], axis=0))[:fields, :half]
    ends = jnp.where(lane % 2 == 0, pltpu.roll(ends, half - 1, 1), pltpu.roll(ends, 1, 1))
    return [pltpu.roll(ends, half - 2 * strip * n, 1) if n else ends for n in range(len(tiles))]


def diffuse_row(read, store, side, t, number):
    fields, half = number.shape
    lane = lax.broadcasted_iota(jnp.int32, (fields, half), 1)
    side = pltpu.roll(side, half - 2 * t - 1, 1)
    for part in range(2):
        own = slice(part * half, (part + 1) * half)
        here = read(0, own)
        across = read(0, slice((1 - part) * half, (2 - part) * half))
        if part == 0:
            west = jnp.where(lane == 0, side, pltpu.roll(here, 1, 1))
            east = pltpu.roll(jnp.where(lane == 0, across, here), half - 1, 1)
        else:
            west = pltpu.roll(jnp.where(lane == half - 1, across, here), 1, 1)
            east = jnp.where(lane == half - 1, side, pltpu.roll(here, half - 1, 1))
        around = read(1, own) + read(-1, own) + east + west
        store(own, here + number * (around - 4.0 * here))


def rows_kernel(whole, failed, ocean, *refs):
    *sent, row_top, row_bottom = refs
    rows, fields, columns = ocean.shape
    wide = 2 * fields
    last = sent[0].shape[0] - 1
    first = slice(GROUP, GROUP + wide)
    final = slice(sent[0].shape[1] - wide, sent[0].shape[1])
    _, _, core, lost = my_place(failed)
    if whole:
        top, bottom = sent[0][0, first, :], sent[0][last, final, :]
    else:
        mine, other = sent
        top = jnp.where(core == 0, mine[0, first, :], other[0, first, :])
        bottom = jnp.where(core == 0, other[last, final, :], mine[last, final, :])
    row_top[...] = jnp.where(lost, top, below(ocean[0]))
    row_bottom[...] = jnp.where(lost, bottom, below(ocean[rows - 1]))


def outer_lines(failed, ocean, sent):
    rows, fields, columns = ocean.shape
    line = jax.ShapeDtypeStruct((2 * fields, columns // 2), jnp.float32)
    return pl.pallas_call(
        functools.partial(rows_kernel, len(sent) == 1),
        out_shape=(line, line),
        in_specs=[SMEM] + [VMEM] * (1 + len(sent)),
        out_specs=(VMEM, VMEM),
        compiler_params=pltpu.CompilerParams(vmem_limit_bytes=VMEM_BYTES),
    )(failed, ocean, *sent)


def first_kernel(
    whole,
    failed,
    ocean,
    sent,
    op,
    diffusivity,
    fresh,
    strips,
    operator,
    number_of,
    inner,
    sides,
    parity,
    sem,
):
    leave = pltpu.make_async_copy(fresh, parity, sem)
    leave.start()
    rows, fields, columns = ocean.shape
    half = columns // 2
    count = 2 * strips.shape[0]
    strip = rows // count
    _, _, core, lost = my_place(failed)
    operator[...] = double_operator(op)
    field = lax.broadcasted_iota(jnp.int32, (fields, half), 0)
    number = jnp.zeros((fields, half), jnp.float32)
    for f in range(fields):
        number = jnp.where(field == f, diffusivity[f], number)
    number_of[...] = number

    def source(p):
        return 2 * p + core if whole else chip_slot(p)

    tiles = [sent[source(p), 0:GROUP, :] for p in range(count // 2)]
    for p, side in enumerate(strip_sides(operator, tiles, core, (fields, half), strip)):
        sides[p] = side

    def mix(p):
        def store(t, done):
            strips[p, pl.ds(t, 2)] = done

        base = pl.multiple_of((2 * p + core) * strip, strip)
        at = source(p)
        mix_strip(operator, lost, lambda own: sent[at, own, :], base, ocean, strip, store)

    mix(0)

    @pl.loop(0, count // 2, unroll=4)
    def _(p):
        for t in range(1, strip - 1):

            def store(own, cells):
                inner[p, t - 1, :, own] = cells

            diffuse_row(lambda d, own: strips[p, t + d, :, own], store, sides[p], t, number)
        mix(jnp.minimum(p + 1, count // 2 - 1))

    leave.wait()


def first_half(failed, ocean, sent, op, diffusivity, fresh, whole, count):
    rows, fields, columns = ocean.shape
    half = columns // 2
    wide = 2 * fields
    shapes = [jax.ShapeDtypeStruct((count // 2, rows // count, fields, columns), jnp.float32)]
    shapes.append(jax.ShapeDtypeStruct((wide, 3 * wide), jnp.bfloat16))
    shapes.append(jax.ShapeDtypeStruct((fields, half), jnp.float32))
    inner = (count // 2, rows // count - 2, fields, columns)
    shapes.append(jax.ShapeDtypeStruct(inner, jnp.float32))
    shapes.append(jax.ShapeDtypeStruct((count // 2, fields, half), jnp.float32))
    shapes.append(jax.ShapeDtypeStruct(fresh.shape, jnp.float32))
    return pl.pallas_call(
        functools.partial(first_kernel, whole),
        out_shape=tuple(shapes),
        in_specs=[SMEM, VMEM, VMEM, VMEM, SMEM, VMEM],
        out_specs=(VMEM,) * 5 + (pl.BlockSpec(memory_space=pl.ANY),),
        scratch_shapes=[pltpu.SemaphoreType.DMA],
        compiler_params=pltpu.CompilerParams(vmem_limit_bytes=VMEM_BYTES),
        cost_estimate=pl.CostEstimate(
            flops=75 * ocean.size, bytes_accessed=4 * ocean.size, transcendentals=ocean.size // 2
        ),
    )(failed, ocean, sent, op, diffusivity, fresh)


def step_kernel(whole, failed, ocean, *refs):
    if whole:
        sent, strips, operator, number_of, inner, near, above, under, *refs = refs
    else:
        mine, other, strips, operator, number_of, inner, near, *refs = refs
    out, mixed, sides = refs
    rows, fields, columns = ocean.shape
    half = columns // 2
    wide = 2 * fields
    pairs = strips.shape[0]
    count = 2 * pairs
    strip = rows // count
    _, _, core, lost = my_place(failed)
    number = number_of[...]

    def prepare(p):
        kept = pl.multiple_of((2 * p + core) * strip, strip)
        base = pl.multiple_of((2 * p + 1 - core) * strip, strip)
        at = 2 * p + 1 - core if whole else chip_slot(p)
        source = sent if whole else other
        for t in range(0, strip, 2):
            mixed[pl.ds(kept + t + 1, 2)] = strips[p, pl.ds(t, 2)]

        def store(t, done):
            mixed[pl.ds(base + t + 1, 2)] = done

        head = mix_strip(operator, lost, lambda own: source[at, own, :], base, ocean, strip, store)
        return jnp.where(core == 0, strips[p, 0], head)

    if whole:
        outer = jnp.concatenate([beside(above[...]), beside(under[...])], axis=0)
        outer = mix_pair(operator, outer)
        mixed[0] = outer[:fields]
        mixed[rows + 1] = outer[fields:]
    else:
        mixed[0] = jnp.zeros((fields, columns), jnp.float32)
        mixed[rows + 1] = jnp.zeros((fields, columns), jnp.float32)
    tiles = []
    for p in range(pairs):
        tiles.append(sent[2 * p + 1 - core, 0:GROUP, :] if whole else other[chip_slot(p), 0:GROUP, :])
    for p, side in enumerate(strip_sides(operator, tiles, core, (fields, half), strip)):
        sides[2 * p + 1 - core] = side
        sides[2 * p + core] = near[p]
    prepare(0)

    def diffuse(s, t, under_row=None):
        i = s * strip + t + 1

        def read(d, own):
            if d == 1 and under_row is not None:
                return under_row[:, own]
            return mixed[i + d, :, own]

        def store(own, cells):
            out[i - 1, :, own] = cells

        diffuse_row(read, store, sides[s], t, number)

    @pl.loop(0, pairs, unroll=2)
    def _(p):
        out[pl.ds((2 * p + core) * strip + 1, strip - 2)] = inner[p]
        diffuse(2 * p, 0)
        for t in range(1, strip - 1):
            diffuse(2 * p + 1 - core, t)
        diffuse(2 * p, strip - 1)
        diffuse(2 * p + 1, 0)
        head = prepare(jnp.minimum(p + 1, pairs - 1))
        head = jnp.where(p == pairs - 1, mixed[rows + 1], head)
        diffuse(2 * p + 1, strip - 1, head)


def step(failed, ocean, sent, strips, operator, number_of, inner, near, *outer):
    rows, fields, columns = ocean.shape
    whole = len(sent) == 1
    pairs = strips.shape[0]
    return pl.pallas_call(
        functools.partial(step_kernel, whole),
        out_shape=jax.ShapeDtypeStruct(ocean.shape, jnp.float32),
        in_specs=[SMEM] + [VMEM] * (6 + len(sent) + len(outer)),
        out_specs=VMEM,
        scratch_shapes=[
            pltpu.VMEM((rows + 2, fields, columns), jnp.float32),
            pltpu.VMEM((2 * pairs, fields, columns // 2), jnp.float32),
        ],
        compiler_params=pltpu.CompilerParams(vmem_limit_bytes=VMEM_BYTES),
        cost_estimate=pl.CostEstimate(
            flops=100 * ocean.size, bytes_accessed=12 * ocean.size, transcendentals=ocean.size // 2
        ),
    )(failed, ocean, *sent, strips, operator, number_of, inner, near, *outer)


def ends_kernel(stepped, above, under, operator, number_of, out, row, sem):
    rows, fields, columns = stepped.shape
    places = (0, rows - 1)
    reads = [
        pltpu.make_async_copy(out.at[at], row.at[n], sem.at[n]) for n, at in enumerate(places)
    ]
    for copy in reads:
        copy.start()
    both = jnp.concatenate([beside(above[...]), beside(under[...])], axis=0)
    both = mix_pair(operator, both)
    number = jnp.concatenate([number_of[...], number_of[...]], axis=1)
    writes = []
    for n, at in enumerate(places):
        reads[n].wait()
        row[n] = row[n] + number * both[n * fields : (n + 1) * fields]
        writes.append(pltpu.make_async_copy(row.at[n], out.at[at], sem.at[n]))
        writes[n].start()
    for copy in writes:
        copy.wait()


def add_ends(stepped, above, under, operator, number_of):
    rows, fields, columns = stepped.shape
    anywhere = pl.BlockSpec(memory_space=pl.ANY)
    return pl.pallas_call(
        ends_kernel,
        out_shape=jax.ShapeDtypeStruct(stepped.shape, jnp.float32),
        in_specs=[anywhere] + [VMEM] * 4,
        out_specs=anywhere,
        input_output_aliases={0: 0},
        scratch_shapes=[
            pltpu.VMEM((2, fields, columns), jnp.float32),
            pltpu.SemaphoreType.DMA((2,)),
        ],
        compiler_params=pltpu.CompilerParams(vmem_limit_bytes=VMEM_BYTES),
    )(stepped, above, under, operator, number_of)


def per_device(
    ocean_state, saved_checksums, checksum_weights, failed_devices, column_op, diffusivity
):
    lines = lax.axis_size("row")
    rows, fields, columns = ocean_state.shape
    count = checksum_weights.shape[1]
    half = columns // 2
    strip = rows // count

    strips = lax.all_to_all(ocean_state, MEMBERS, 0, 0, tiled=True)
    strips, ocean, saved, weights, failed, op, number = lax.optimization_barrier(
        (
            strips,
            ocean_state,
            saved_checksums,
            checksum_weights,
            failed_devices.T,
            column_op,
            diffusivity,
        )
    )
    strips = strips.reshape(count, strip, fields, columns)
    fresh, rebuilt, back, shared = rebuild(failed, weights, strips, saved)

    def exchange_rows(ocean, sent):
        top, bottom = outer_lines(failed, ocean, sent)
        above = lax.ppermute(bottom, "row", [(r, r + 1) for r in range(lines - 1)])
        under = lax.ppermute(top, "row", [(r + 1, r) for r in range(lines - 1)])
        return above, under

    def exchange_chips(rebuilt, back, ocean, fresh):
        mine = lax.all_to_all(back, CHIPS, 0, 0, tiled=True)
        mine, ocean = lax.optimization_barrier((mine, ocean))
        other = lax.ppermute(mine, "core", [(0, 1), (1, 0)])
        *kept, parity = first_half(failed, ocean, mine, op, number, fresh, False, count)
        other, kept = lax.optimization_barrier((other, kept))
        above, under = exchange_rows(ocean, (mine, other))
        stepped = step(failed, ocean, (mine, other), *kept)
        return add_ends(stepped, above, under, *kept[1:3]), parity

    def exchange_whole(rebuilt, back, ocean, fresh):
        back = spread_whole(failed, rebuilt, back)
        sent = lax.all_to_all(back, MEMBERS, 0, 0, tiled=True)
        sent, ocean = lax.optimization_barrier((sent, ocean))
        above, under = exchange_rows(ocean, (sent,))
        *kept, parity = first_half(failed, ocean, sent, op, number, fresh, True, count)
        return step(failed, ocean, (sent,), *kept, above, under), parity

    return lax.cond(
        shared[0] != 0, exchange_whole, exchange_chips, rebuilt, back, ocean, fresh
    )


def solution(mesh):
    row, col = mesh.axis_names
    shape = (mesh.shape[row], 2, 4, 2)
    chips = jax.sharding.Mesh(mesh.devices.reshape(shape), ("row", "y_hi", "x", "core"))
    col = MEMBERS
    return jax.shard_map(
        per_device,
        mesh=chips,
        in_specs=(P("row", None, col), P(("row", *col), None, None, None), P(), P(), P(), P()),
        out_specs=(P("row", None, col), P(("row", *col), None, None, None)),
        check_vma=False,
    )
```

```python
import functools

import jax
import jax.numpy as jnp
from jax import lax
from jax.experimental import pallas as pl
from jax.experimental.pallas import tpu as pltpu
from jax.sharding import PartitionSpec as P

VMEM_BYTES = 20 * 1024 * 1024
SMEM = pl.BlockSpec(memory_space=pltpu.SMEM)
VMEM = pl.BlockSpec(memory_space=pltpu.VMEM)

GROUP = 8
MEMBERS = ("y_hi", "x", "core")
CHIPS = ("x", "y_hi")


def chip_slot(chip):
    return (chip & 3) * 2 + (chip >> 2)


def column(weights, member):
    return [weights[k, member] for k in range(weights.shape[0])]


def dot(left, right):
    return sum(x * y for x, y in zip(left, right))


def rebuild_kernel(
    failed, weights, strips, saved, fresh, rebuilt, back, shared, edges, factors
):
    count, rows, fields, columns = strips.shape
    checks = saved.shape[1]
    half = columns // 2
    wide = 2 * fields
    lane = lax.broadcasted_iota(jnp.int32, (fields, half), 1)
    edges[...] = jnp.zeros_like(edges)
    line = lax.axis_index("row")
    lost = (failed[0, line], failed[1, line])

    any_shared = jnp.int32(0)
    for r in range(failed.shape[1]):
        any_shared |= ((failed[0, r] >> 1) == (failed[1, r] >> 1)).astype(jnp.int32)
    shared[0] = any_shared

    u, v = column(weights, lost[0]), column(weights, lost[1])
    gram_aa, gram_bb, gram_ab = dot(u, u) + 1, dot(v, v) + 1, dot(u, v)
    determinant = (gram_aa * gram_bb - gram_ab * gram_ab).astype(jnp.float32)
    scale = 1.0 / jnp.full((fields, columns), determinant, jnp.float32)
    for c in range(count):
        kept = ((lost[0] != c) & (lost[1] != c)).astype(jnp.int32)
        for k in range(checks):
            factors[k, c] = (kept * weights[k, c]).astype(jnp.float32)
    for k in range(checks):
        factors[k, count] = u[k].astype(jnp.float32)
        factors[k, count + 1] = v[k].astype(jnp.float32)
        factors[k, count + 2] = (gram_bb * u[k] - gram_ab * v[k]).astype(jnp.float32)
        factors[k, count + 3] = (gram_aa * v[k] - gram_ab * u[k]).astype(jnp.float32)

    def keep_edges(n, i, first, final):
        ends = pltpu.roll(jnp.where(lane == 0, first, final), 2 * i + 1, 1)
        edges[n] = jnp.where((lane == 2 * i) | (lane == 2 * i + 1), ends, edges[n])

    for i in range(rows):
        at = i * wide
        living = [None] * checks
        for c in range(count):
            block = strips[c, i]
            keep_edges(c, i, block[:, :half], block[:, half:])
            for k in range(checks):
                term = factors[k, c] * block
                living[k] = term if c == 0 else living[k] + term
        whole = [None, None]
        for k in range(checks):
            residue = saved[i, k] - living[k]
            for b in range(2):
                term = factors[k, count + 2 + b] * residue
                whole[b] = term if k == 0 else whole[b] + term
        whole = [x * scale for x in whole]
        for k in range(checks):
            fresh[i, k] = (
                living[k] + factors[k, count] * whole[0] + factors[k, count + 1] * whole[1]
            )
        for b in range(2):
            first, final = whole[b][:, :half], whole[b][:, half:]
            keep_edges(count + b, i, first, final)
            whole[b] = jnp.concatenate([first, final], axis=0)
            rebuilt[b, pl.ds(at, wide), :] = whole[b]
        for c in range(count // 2):
            chosen = jnp.where((lost[0] >> 1) == c, whole[0], whole[1])
            back[chip_slot(c), pl.ds(at + GROUP, wide), :] = chosen

    def recovered_edges(c):
        if c < 0 or c >= count:
            return jnp.zeros((fields, half), jnp.float32)
        raw = jnp.where(lost[1] == c, edges[count + 1], edges[c])
        return jnp.where(lost[0] == c, edges[count], raw)

    for c in range(0, count, 2):
        near = [recovered_edges(c + d) for d in (-1, 0, 1, 2)]
        both = jnp.where(lane % 2 == 0, near[0], near[2])
        both = both + pltpu.roll(jnp.where(lane % 2 == 0, near[1], near[3]), 2 * rows, 1)
        packed = both[:GROUP]
        for g in range(1, fields // GROUP):
            packed = packed + pltpu.roll(both[g * GROUP : (g + 1) * GROUP], 4 * rows * g, 1)
        back[chip_slot(c // 2), 0:GROUP, :] = packed


def rebuild(failed, weights, strips, saved):
    count, rows, fields, columns = strips.shape
    half = columns // 2
    whole = 2 * rows * fields
    checks = weights.shape[0]
    return pl.pallas_call(
        rebuild_kernel,
        out_shape=(
            jax.ShapeDtypeStruct(saved.shape, jnp.float32),
            jax.ShapeDtypeStruct((2, whole, half), jnp.float32),
            jax.ShapeDtypeStruct((count // 2, GROUP + whole, half), jnp.float32),
            jax.ShapeDtypeStruct((1,), jnp.int32),
        ),
        in_specs=[SMEM, SMEM, VMEM, VMEM],
        out_specs=(VMEM, VMEM, VMEM, SMEM),
        scratch_shapes=[
            pltpu.VMEM((count + 2, fields, half), jnp.float32),
            pltpu.SMEM((checks, count + 4), jnp.float32),
        ],
        compiler_params=pltpu.CompilerParams(vmem_limit_bytes=VMEM_BYTES),
        cost_estimate=pl.CostEstimate(
            flops=8 * strips.size, bytes_accessed=6 * strips.size, transcendentals=0
        ),
    )(failed, weights, strips, saved)


def spread_kernel(failed, rebuilt, short, back):
    lost_a = failed[0, lax.axis_index("row")]
    for c in range(back.shape[0]):
        back[c, 0:GROUP, :] = short[chip_slot(c // 2), 0:GROUP, :]
        back[c, GROUP:, :] = rebuilt[jnp.where(lost_a == c, 0, 1)]


def spread_whole(failed, rebuilt, short):
    chips, lines, half = short.shape
    return pl.pallas_call(
        spread_kernel,
        out_shape=jax.ShapeDtypeStruct((2 * chips, lines, half), jnp.float32),
        in_specs=[SMEM, VMEM, VMEM],
        out_specs=VMEM,
        compiler_params=pltpu.CompilerParams(vmem_limit_bytes=VMEM_BYTES),
    )(failed, rebuilt, short)


def beside(cells):
    half = cells.shape[0] // 2
    return jnp.concatenate([cells[:half], cells[half:]], axis=1)


def below(cells):
    half = cells.shape[1] // 2
    return jnp.concatenate([cells[:, :half], cells[:, half:]], axis=0)


def mix_pair(operator, flat):
    high = flat.astype(jnp.bfloat16)
    low = (flat - high.astype(jnp.float32)).astype(jnp.bfloat16)
    terms = jnp.concatenate([high, low, high], axis=0)
    return flat + jnp.tanh(jnp.dot(operator[...], terms, preferred_element_type=jnp.float32))


def mix_strip(operator, lost, sent, base, ocean, strip, store):
    fields, columns = ocean.shape[1:]
    wide = 2 * fields
    head = None
    for t in range(0, strip, 2):
        units = []
        for q in (t, t + 1):
            own = slice(GROUP + q * wide, GROUP + (q + 1) * wide)
            units.append(jnp.where(lost, beside(sent(own)), ocean[base + q]))
        done = mix_pair(operator, jnp.concatenate(units, axis=0)).reshape(2, fields, columns)
        store(t, done)
        if t == 0:
            head = done[0]
    return head


def my_place(failed):
    line = lax.axis_index("row")
    member = lax.axis_index(MEMBERS)
    lost = (failed[0, line] == member) | (failed[1, line] == member)
    return line, member, member % 2, lost


def double_operator(op):
    fields = op.shape[0]
    wide = 2 * fields
    tall = lax.broadcasted_iota(jnp.int32, (wide, fields), 0) % fields
    tall = (tall == lax.broadcasted_iota(jnp.int32, (wide, fields), 1)).astype(jnp.float32)
    flat = lax.broadcasted_iota(jnp.int32, (fields, wide), 1) % fields
    flat = (flat == lax.broadcasted_iota(jnp.int32, (fields, wide), 0)).astype(jnp.float32)
    exact = dict(preferred_element_type=jnp.float32, precision=lax.Precision.HIGHEST)
    tiled = jnp.dot(jnp.dot(tall, op[...], **exact), flat, **exact)
    down = lax.broadcasted_iota(jnp.int32, (wide, wide), 0) // fields
    across = lax.broadcasted_iota(jnp.int32, (wide, wide), 1) // fields
    both = jnp.where(down == across, tiled, 0.0)
    high = both.astype(jnp.bfloat16)
    low = (both - high.astype(jnp.float32)).astype(jnp.bfloat16)
    return jnp.concatenate([high, high, low], axis=1)


def strip_sides(operator, tiles, core, shape, strip):
    fields, half = shape
    lane = lax.broadcasted_iota(jnp.int32, shape, 1)
    narrow = lane[:GROUP]
    ends = []
    for g in range(fields // GROUP):
        part = jnp.zeros((GROUP, half), jnp.float32)
        for n, tile in enumerate(tiles):
            shift = (2 * strip * (n - 2 * g)) % half
            near = pltpu.roll(tile, shift, 1) if shift else tile
            shift = (2 * strip * (n - 2 * g - 1)) % half
            far = pltpu.roll(tile, shift, 1) if shift else tile
            part = jnp.where(narrow // (2 * strip) == n, jnp.where(core == 0, near, far), part)
        ends.append(part)
    ends = jnp.concatenate(ends, axis=0)
    ends = jnp.concatenate([ends, ends], axis=1)
    ends = mix_pair(operator, jnp.concatenate([ends, ends], axis=0))[:fields, :half]
    ends = jnp.where(lane % 2 == 0, pltpu.roll(ends, half - 1, 1), pltpu.roll(ends, 1, 1))
    return [pltpu.roll(ends, half - 2 * strip * n, 1) if n else ends for n in range(len(tiles))]


def diffuse_row(read, store, side, t, number):
    fields, half = number.shape
    lane = lax.broadcasted_iota(jnp.int32, (fields, half), 1)
    side = pltpu.roll(side, half - 2 * t - 1, 1)
    for part in range(2):
        own = slice(part * half, (part + 1) * half)
        here = read(0, own)
        across = read(0, slice((1 - part) * half, (2 - part) * half))
        if part == 0:
            west = jnp.where(lane == 0, side, pltpu.roll(here, 1, 1))
            east = pltpu.roll(jnp.where(lane == 0, across, here), half - 1, 1)
        else:
            west = pltpu.roll(jnp.where(lane == half - 1, across, here), 1, 1)
            east = jnp.where(lane == half - 1, side, pltpu.roll(here, half - 1, 1))
        around = read(1, own) + read(-1, own) + east + west
        store(own, here + number * (around - 4.0 * here))


def rows_kernel(whole, failed, ocean, *refs):
    *sent, row_top, row_bottom = refs
    rows, fields, columns = ocean.shape
    wide = 2 * fields
    last = sent[0].shape[0] - 1
    first = slice(GROUP, GROUP + wide)
    final = slice(sent[0].shape[1] - wide, sent[0].shape[1])
    _, _, core, lost = my_place(failed)
    if whole:
        top, bottom = sent[0][0, first, :], sent[0][last, final, :]
    else:
        mine, other = sent
        top = jnp.where(core == 0, mine[0, first, :], other[0, first, :])
        bottom = jnp.where(core == 0, other[last, final, :], mine[last, final, :])
    row_top[...] = jnp.where(lost, top, below(ocean[0]))
    row_bottom[...] = jnp.where(lost, bottom, below(ocean[rows - 1]))


def outer_lines(failed, ocean, sent):
    rows, fields, columns = ocean.shape
    line = jax.ShapeDtypeStruct((2 * fields, columns // 2), jnp.float32)
    return pl.pallas_call(
        functools.partial(rows_kernel, len(sent) == 1),
        out_shape=(line, line),
        in_specs=[SMEM] + [VMEM] * (1 + len(sent)),
        out_specs=(VMEM, VMEM),
        compiler_params=pltpu.CompilerParams(vmem_limit_bytes=VMEM_BYTES),
    )(failed, ocean, *sent)


def first_kernel(
    whole,
    failed,
    ocean,
    sent,
    op,
    diffusivity,
    fresh,
    strips,
    operator,
    number_of,
    inner,
    sides,
    parity,
    sem,
):
    leave = pltpu.make_async_copy(fresh, parity, sem)
    leave.start()
    rows, fields, columns = ocean.shape
    half = columns // 2
    count = 2 * strips.shape[0]
    strip = rows // count
    _, _, core, lost = my_place(failed)
    operator[...] = double_operator(op)
    field = lax.broadcasted_iota(jnp.int32, (fields, half), 0)
    number = jnp.zeros((fields, half), jnp.float32)
    for f in range(fields):
        number = jnp.where(field == f, diffusivity[f], number)
    number_of[...] = number

    def source(p):
        return 2 * p + core if whole else chip_slot(p)

    tiles = [sent[source(p), 0:GROUP, :] for p in range(count // 2)]
    for p, side in enumerate(strip_sides(operator, tiles, core, (fields, half), strip)):
        sides[p] = side

    def mix(p):
        def store(t, done):
            strips[p, pl.ds(t, 2)] = done

        base = pl.multiple_of((2 * p + core) * strip, strip)
        at = source(p)
        mix_strip(operator, lost, lambda own: sent[at, own, :], base, ocean, strip, store)

    mix(0)

    @pl.loop(0, count // 2, unroll=4)
    def _(p):
        for t in range(1, strip - 1):

            def store(own, cells):
                inner[p, t - 1, :, own] = cells

            diffuse_row(lambda d, own: strips[p, t + d, :, own], store, sides[p], t, number)
        mix(jnp.minimum(p + 1, count // 2 - 1))

    leave.wait()


def first_half(failed, ocean, sent, op, diffusivity, fresh, whole, count):
    rows, fields, columns = ocean.shape
    half = columns // 2
    wide = 2 * fields
    shapes = [jax.ShapeDtypeStruct((count // 2, rows // count, fields, columns), jnp.float32)]
    shapes.append(jax.ShapeDtypeStruct((wide, 3 * wide), jnp.bfloat16))
    shapes.append(jax.ShapeDtypeStruct((fields, half), jnp.float32))
    inner = (count // 2, rows // count - 2, fields, columns)
    shapes.append(jax.ShapeDtypeStruct(inner, jnp.float32))
    shapes.append(jax.ShapeDtypeStruct((count // 2, fields, half), jnp.float32))
    shapes.append(jax.ShapeDtypeStruct(fresh.shape, jnp.float32))
    return pl.pallas_call(
        functools.partial(first_kernel, whole),
        out_shape=tuple(shapes),
        in_specs=[SMEM, VMEM, VMEM, VMEM, SMEM, VMEM],
        out_specs=(VMEM,) * 5 + (pl.BlockSpec(memory_space=pl.ANY),),
        scratch_shapes=[pltpu.SemaphoreType.DMA],
        compiler_params=pltpu.CompilerParams(vmem_limit_bytes=VMEM_BYTES),
        cost_estimate=pl.CostEstimate(
            flops=75 * ocean.size, bytes_accessed=4 * ocean.size, transcendentals=ocean.size // 2
        ),
    )(failed, ocean, sent, op, diffusivity, fresh)


def step_kernel(whole, failed, ocean, *refs):
    if whole:
        sent, strips, operator, number_of, inner, near, above, under, *refs = refs
    else:
        mine, other, strips, operator, number_of, inner, near, *refs = refs
    out, mixed, sides = refs
    rows, fields, columns = ocean.shape
    half = columns // 2
    wide = 2 * fields
    pairs = strips.shape[0]
    count = 2 * pairs
    strip = rows // count
    _, _, core, lost = my_place(failed)
    number = number_of[...]

    def prepare(p):
        kept = pl.multiple_of((2 * p + core) * strip, strip)
        base = pl.multiple_of((2 * p + 1 - core) * strip, strip)
        at = 2 * p + 1 - core if whole else chip_slot(p)
        source = sent if whole else other
        for t in range(0, strip, 2):
            mixed[pl.ds(kept + t + 1, 2)] = strips[p, pl.ds(t, 2)]

        def store(t, done):
            mixed[pl.ds(base + t + 1, 2)] = done

        head = mix_strip(operator, lost, lambda own: source[at, own, :], base, ocean, strip, store)
        return jnp.where(core == 0, strips[p, 0], head)

    if whole:
        outer = jnp.concatenate([beside(above[...]), beside(under[...])], axis=0)
        outer = mix_pair(operator, outer)
        mixed[0] = outer[:fields]
        mixed[rows + 1] = outer[fields:]
    else:
        mixed[0] = jnp.zeros((fields, columns), jnp.float32)
        mixed[rows + 1] = jnp.zeros((fields, columns), jnp.float32)
    tiles = []
    for p in range(pairs):
        tiles.append(sent[2 * p + 1 - core, 0:GROUP, :] if whole else other[chip_slot(p), 0:GROUP, :])
    for p, side in enumerate(strip_sides(operator, tiles, core, (fields, half), strip)):
        sides[2 * p + 1 - core] = side
        sides[2 * p + core] = near[p]
    prepare(0)

    def diffuse(s, t, under_row=None):
        i = s * strip + t + 1

        def read(d, own):
            if d == 1 and under_row is not None:
                return under_row[:, own]
            return mixed[i + d, :, own]

        def store(own, cells):
            out[i - 1, :, own] = cells

        diffuse_row(read, store, sides[s], t, number)

    @pl.loop(0, pairs, unroll=2)
    def _(p):
        out[pl.ds((2 * p + core) * strip + 1, strip - 2)] = inner[p]
        diffuse(2 * p, 0)
        for t in range(1, strip - 1):
            diffuse(2 * p + 1 - core, t)
        diffuse(2 * p, strip - 1)
        diffuse(2 * p + 1, 0)
        head = prepare(jnp.minimum(p + 1, pairs - 1))
        head = jnp.where(p == pairs - 1, mixed[rows + 1], head)
        diffuse(2 * p + 1, strip - 1, head)


def step(failed, ocean, sent, strips, operator, number_of, inner, near, *outer):
    rows, fields, columns = ocean.shape
    whole = len(sent) == 1
    pairs = strips.shape[0]
    return pl.pallas_call(
        functools.partial(step_kernel, whole),
        out_shape=jax.ShapeDtypeStruct(ocean.shape, jnp.float32),
        in_specs=[SMEM] + [VMEM] * (6 + len(sent) + len(outer)),
        out_specs=VMEM,
        scratch_shapes=[
            pltpu.VMEM((rows + 2, fields, columns), jnp.float32),
            pltpu.VMEM((2 * pairs, fields, columns // 2), jnp.float32),
        ],
        compiler_params=pltpu.CompilerParams(vmem_limit_bytes=VMEM_BYTES),
        cost_estimate=pl.CostEstimate(
            flops=100 * ocean.size, bytes_accessed=12 * ocean.size, transcendentals=ocean.size // 2
        ),
    )(failed, ocean, *sent, strips, operator, number_of, inner, near, *outer)


def ends_kernel(stepped, above, under, operator, number_of, out, row, sem):
    rows, fields, columns = stepped.shape
    places = (0, rows - 1)
    reads = [
        pltpu.make_async_copy(out.at[at], row.at[n], sem.at[n]) for n, at in enumerate(places)
    ]
    for copy in reads:
        copy.start()
    both = jnp.concatenate([beside(above[...]), beside(under[...])], axis=0)
    both = mix_pair(operator, both)
    number = jnp.concatenate([number_of[...], number_of[...]], axis=1)
    writes = []
    for n, at in enumerate(places):
        reads[n].wait()
        row[n] = row[n] + number * both[n * fields : (n + 1) * fields]
        writes.append(pltpu.make_async_copy(row.at[n], out.at[at], sem.at[n]))
        writes[n].start()
    for copy in writes:
        copy.wait()


def add_ends(stepped, above, under, operator, number_of):
    rows, fields, columns = stepped.shape
    anywhere = pl.BlockSpec(memory_space=pl.ANY)
    return pl.pallas_call(
        ends_kernel,
        out_shape=jax.ShapeDtypeStruct(stepped.shape, jnp.float32),
        in_specs=[anywhere] + [VMEM] * 4,
        out_specs=anywhere,
        input_output_aliases={0: 0},
        scratch_shapes=[
            pltpu.VMEM((2, fields, columns), jnp.float32),
            pltpu.SemaphoreType.DMA((2,)),
        ],
        compiler_params=pltpu.CompilerParams(vmem_limit_bytes=VMEM_BYTES),
    )(stepped, above, under, operator, number_of)


def per_device(
    ocean_state, saved_checksums, checksum_weights, failed_devices, column_op, diffusivity
):
    lines = lax.axis_size("row")
    rows, fields, columns = ocean_state.shape
    count = checksum_weights.shape[1]
    half = columns // 2
    strip = rows // count

    strips = lax.all_to_all(ocean_state, MEMBERS, 0, 0, tiled=True)
    strips, ocean, saved, weights, failed, op, number = lax.optimization_barrier(
        (
            strips,
            ocean_state,
            saved_checksums,
            checksum_weights,
            failed_devices.T,
            column_op,
            diffusivity,
        )
    )
    strips = strips.reshape(count, strip, fields, columns)
    fresh, rebuilt, back, shared = rebuild(failed, weights, strips, saved)

    def exchange_rows(ocean, sent):
        top, bottom = outer_lines(failed, ocean, sent)
        above = lax.ppermute(bottom, "row", [(r, r + 1) for r in range(lines - 1)])
        under = lax.ppermute(top, "row", [(r + 1, r) for r in range(lines - 1)])
        return above, under

    def exchange_chips(rebuilt, back, ocean, fresh):
        mine = lax.all_to_all(back, CHIPS, 0, 0, tiled=True)
        mine, ocean = lax.optimization_barrier((mine, ocean))
        other = lax.ppermute(mine, "core", [(0, 1), (1, 0)])
        *kept, parity = first_half(failed, ocean, mine, op, number, fresh, False, count)
        other, kept = lax.optimization_barrier((other, kept))
        above, under = exchange_rows(ocean, (mine, other))
        stepped = step(failed, ocean, (mine, other), *kept)
        return add_ends(stepped, above, under, *kept[1:3]), parity

    def exchange_whole(rebuilt, back, ocean, fresh):
        back = spread_whole(failed, rebuilt, back)
        sent = lax.all_to_all(back, MEMBERS, 0, 0, tiled=True)
        sent, ocean = lax.optimization_barrier((sent, ocean))
        above, under = exchange_rows(ocean, (sent,))
        *kept, parity = first_half(failed, ocean, sent, op, number, fresh, True, count)
        return step(failed, ocean, (sent,), *kept, above, under), parity

    return lax.cond(
        shared[0] != 0, exchange_whole, exchange_chips, rebuilt, back, ocean, fresh
    )


def solution(mesh):
    row, col = mesh.axis_names
    shape = (mesh.shape[row], 2, 4, 2)
    chips = jax.sharding.Mesh(mesh.devices.reshape(shape), ("row", "y_hi", "x", "core"))
    col = MEMBERS
    return jax.shard_map(
        per_device,
        mesh=chips,
        in_specs=(P("row", None, col), P(("row", *col), None, None, None), P(), P(), P(), P()),
        out_specs=(P("row", None, col), P(("row", *col), None, None, None)),
        check_vma=False,
    )
```

```python
import functools

import jax
import jax.numpy as jnp
from jax import lax
from jax.experimental import pallas as pl
from jax.experimental.pallas import tpu as pltpu
from jax.sharding import PartitionSpec as P

VMEM_BYTES = 20 * 1024 * 1024
SMEM = pl.BlockSpec(memory_space=pltpu.SMEM)
VMEM = pl.BlockSpec(memory_space=pltpu.VMEM)

GROUP = 8
MEMBERS = ("y_hi", "x", "core")
CHIPS = ("x", "y_hi")


def chip_slot(chip):
    return (chip & 3) * 2 + (chip >> 2)


def column(weights, member):
    return [weights[k, member] for k in range(weights.shape[0])]


def dot(left, right):
    return sum(x * y for x, y in zip(left, right))


def rebuild_kernel(
    failed, weights, strips, saved, fresh, rebuilt, back, shared, edges, factors
):
    count, rows, fields, columns = strips.shape
    checks = saved.shape[1]
    half = columns // 2
    wide = 2 * fields
    lane = lax.broadcasted_iota(jnp.int32, (fields, half), 1)
    edges[...] = jnp.zeros_like(edges)
    line = lax.axis_index("row")
    lost = (failed[0, line], failed[1, line])

    any_shared = jnp.int32(0)
    for r in range(failed.shape[1]):
        any_shared |= ((failed[0, r] >> 1) == (failed[1, r] >> 1)).astype(jnp.int32)
    shared[0] = any_shared

    u, v = column(weights, lost[0]), column(weights, lost[1])
    gram_aa, gram_bb, gram_ab = dot(u, u) + 1, dot(v, v) + 1, dot(u, v)
    determinant = (gram_aa * gram_bb - gram_ab * gram_ab).astype(jnp.float32)
    scale = 1.0 / jnp.full((fields, columns), determinant, jnp.float32)
    for c in range(count):
        kept = ((lost[0] != c) & (lost[1] != c)).astype(jnp.int32)
        for k in range(checks):
            factors[k, c] = (kept * weights[k, c]).astype(jnp.float32)
    for k in range(checks):
        factors[k, count] = u[k].astype(jnp.float32)
        factors[k, count + 1] = v[k].astype(jnp.float32)
        factors[k, count + 2] = (gram_bb * u[k] - gram_ab * v[k]).astype(jnp.float32)
        factors[k, count + 3] = (gram_aa * v[k] - gram_ab * u[k]).astype(jnp.float32)

    def keep_edges(n, i, first, final):
        ends = pltpu.roll(jnp.where(lane == 0, first, final), 2 * i + 1, 1)
        edges[n] = jnp.where((lane == 2 * i) | (lane == 2 * i + 1), ends, edges[n])

    for i in range(rows):
        at = i * wide
        living = [None] * checks
        for c in range(count):
            block = strips[c, i]
            keep_edges(c, i, block[:, :half], block[:, half:])
            for k in range(checks):
                term = factors[k, c] * block
                living[k] = term if c == 0 else living[k] + term
        whole = [None, None]
        for k in range(checks):
            residue = saved[i, k] - living[k]
            for b in range(2):
                term = factors[k, count + 2 + b] * residue
                whole[b] = term if k == 0 else whole[b] + term
        whole = [x * scale for x in whole]
        for k in range(checks):
            fresh[i, k] = (
                living[k] + factors[k, count] * whole[0] + factors[k, count + 1] * whole[1]
            )
        for b in range(2):
            first, final = whole[b][:, :half], whole[b][:, half:]
            keep_edges(count + b, i, first, final)
            whole[b] = jnp.concatenate([first, final], axis=0)
            rebuilt[b, pl.ds(at, wide), :] = whole[b]
        for c in range(count // 2):
            chosen = jnp.where((lost[0] >> 1) == c, whole[0], whole[1])
            back[chip_slot(c), pl.ds(at + GROUP, wide), :] = chosen

    def recovered_edges(c):
        if c < 0 or c >= count:
            return jnp.zeros((fields, half), jnp.float32)
        raw = jnp.where(lost[1] == c, edges[count + 1], edges[c])
        return jnp.where(lost[0] == c, edges[count], raw)

    for c in range(0, count, 2):
        near = [recovered_edges(c + d) for d in (-1, 0, 1, 2)]
        both = jnp.where(lane % 2 == 0, near[0], near[2])
        both = both + pltpu.roll(jnp.where(lane % 2 == 0, near[1], near[3]), 2 * rows, 1)
        packed = both[:GROUP]
        for g in range(1, fields // GROUP):
            packed = packed + pltpu.roll(both[g * GROUP : (g + 1) * GROUP], 4 * rows * g, 1)
        back[chip_slot(c // 2), 0:GROUP, :] = packed


def rebuild(failed, weights, strips, saved):
    count, rows, fields, columns = strips.shape
    half = columns // 2
    whole = 2 * rows * fields
    checks = weights.shape[0]
    return pl.pallas_call(
        rebuild_kernel,
        out_shape=(
            jax.ShapeDtypeStruct(saved.shape, jnp.float32),
            jax.ShapeDtypeStruct((2, whole, half), jnp.float32),
            jax.ShapeDtypeStruct((count // 2, GROUP + whole, half), jnp.float32),
            jax.ShapeDtypeStruct((1,), jnp.int32),
        ),
        in_specs=[SMEM, SMEM, VMEM, VMEM],
        out_specs=(VMEM, VMEM, VMEM, SMEM),
        scratch_shapes=[
            pltpu.VMEM((count + 2, fields, half), jnp.float32),
            pltpu.SMEM((checks, count + 4), jnp.float32),
        ],
        compiler_params=pltpu.CompilerParams(vmem_limit_bytes=VMEM_BYTES),
        cost_estimate=pl.CostEstimate(
            flops=8 * strips.size, bytes_accessed=6 * strips.size, transcendentals=0
        ),
    )(failed, weights, strips, saved)


def spread_kernel(failed, rebuilt, short, back):
    lost_a = failed[0, lax.axis_index("row")]
    for c in range(back.shape[0]):
        back[c, 0:GROUP, :] = short[chip_slot(c // 2), 0:GROUP, :]
        back[c, GROUP:, :] = rebuilt[jnp.where(lost_a == c, 0, 1)]


def spread_whole(failed, rebuilt, short):
    chips, lines, half = short.shape
    return pl.pallas_call(
        spread_kernel,
        out_shape=jax.ShapeDtypeStruct((2 * chips, lines, half), jnp.float32),
        in_specs=[SMEM, VMEM, VMEM],
        out_specs=VMEM,
        compiler_params=pltpu.CompilerParams(vmem_limit_bytes=VMEM_BYTES),
    )(failed, rebuilt, short)


def beside(cells):
    half = cells.shape[0] // 2
    return jnp.concatenate([cells[:half], cells[half:]], axis=1)


def below(cells):
    half = cells.shape[1] // 2
    return jnp.concatenate([cells[:, :half], cells[:, half:]], axis=0)


def mix_pair(operator, flat):
    high = flat.astype(jnp.bfloat16)
    low = (flat - high.astype(jnp.float32)).astype(jnp.bfloat16)
    terms = jnp.concatenate([high, low, high], axis=0)
    return flat + jnp.tanh(jnp.dot(operator[...], terms, preferred_element_type=jnp.float32))


def mix_strip(operator, lost, sent, base, ocean, strip, store):
    fields, columns = ocean.shape[1:]
    wide = 2 * fields
    head = None
    for t in range(0, strip, 2):
        units = []
        for q in (t, t + 1):
            own = slice(GROUP + q * wide, GROUP + (q + 1) * wide)
            units.append(jnp.where(lost, beside(sent(own)), ocean[base + q]))
        done = mix_pair(operator, jnp.concatenate(units, axis=0)).reshape(2, fields, columns)
        store(t, done)
        if t == 0:
            head = done[0]
    return head


def my_place(failed):
    line = lax.axis_index("row")
    member = lax.axis_index(MEMBERS)
    lost = (failed[0, line] == member) | (failed[1, line] == member)
    return line, member, member % 2, lost


def double_operator(op):
    fields = op.shape[0]
    wide = 2 * fields
    tall = lax.broadcasted_iota(jnp.int32, (wide, fields), 0) % fields
    tall = (tall == lax.broadcasted_iota(jnp.int32, (wide, fields), 1)).astype(jnp.float32)
    flat = lax.broadcasted_iota(jnp.int32, (fields, wide), 1) % fields
    flat = (flat == lax.broadcasted_iota(jnp.int32, (fields, wide), 0)).astype(jnp.float32)
    exact = dict(preferred_element_type=jnp.float32, precision=lax.Precision.HIGHEST)
    tiled = jnp.dot(jnp.dot(tall, op[...], **exact), flat, **exact)
    down = lax.broadcasted_iota(jnp.int32, (wide, wide), 0) // fields
    across = lax.broadcasted_iota(jnp.int32, (wide, wide), 1) // fields
    both = jnp.where(down == across, tiled, 0.0)
    high = both.astype(jnp.bfloat16)
    low = (both - high.astype(jnp.float32)).astype(jnp.bfloat16)
    return jnp.concatenate([high, high, low], axis=1)


def strip_sides(operator, tiles, core, shape, strip):
    fields, half = shape
    lane = lax.broadcasted_iota(jnp.int32, shape, 1)
    narrow = lane[:GROUP]
    ends = []
    for g in range(fields // GROUP):
        part = jnp.zeros((GROUP, half), jnp.float32)
        for n, tile in enumerate(tiles):
            shift = (2 * strip * (n - 2 * g)) % half
            near = pltpu.roll(tile, shift, 1) if shift else tile
            shift = (2 * strip * (n - 2 * g - 1)) % half
            far = pltpu.roll(tile, shift, 1) if shift else tile
            part = jnp.where(narrow // (2 * strip) == n, jnp.where(core == 0, near, far), part)
        ends.append(part)
    ends = jnp.concatenate(ends, axis=0)
    ends = jnp.concatenate([ends, ends], axis=1)
    ends = mix_pair(operator, jnp.concatenate([ends, ends], axis=0))[:fields, :half]
    ends = jnp.where(lane % 2 == 0, pltpu.roll(ends, half - 1, 1), pltpu.roll(ends, 1, 1))
    return [pltpu.roll(ends, half - 2 * strip * n, 1) if n else ends for n in range(len(tiles))]


def diffuse_row(read, store, side, t, number):
    fields, half = number.shape
    lane = lax.broadcasted_iota(jnp.int32, (fields, half), 1)
    side = pltpu.roll(side, half - 2 * t - 1, 1)
    for part in range(2):
        own = slice(part * half, (part + 1) * half)
        here = read(0, own)
        across = read(0, slice((1 - part) * half, (2 - part) * half))
        if part == 0:
            west = jnp.where(lane == 0, side, pltpu.roll(here, 1, 1))
            east = pltpu.roll(jnp.where(lane == 0, across, here), half - 1, 1)
        else:
            west = pltpu.roll(jnp.where(lane == half - 1, across, here), 1, 1)
            east = jnp.where(lane == half - 1, side, pltpu.roll(here, half - 1, 1))
        around = read(1, own) + read(-1, own) + east + west
        store(own, here + number * (around - 4.0 * here))


def rows_kernel(whole, failed, ocean, *refs):
    *sent, row_top, row_bottom = refs
    rows, fields, columns = ocean.shape
    wide = 2 * fields
    last = sent[0].shape[0] - 1
    first = slice(GROUP, GROUP + wide)
    final = slice(sent[0].shape[1] - wide, sent[0].shape[1])
    _, _, core, lost = my_place(failed)
    if whole:
        top, bottom = sent[0][0, first, :], sent[0][last, final, :]
    else:
        mine, other = sent
        top = jnp.where(core == 0, mine[0, first, :], other[0, first, :])
        bottom = jnp.where(core == 0, other[last, final, :], mine[last, final, :])
    row_top[...] = jnp.where(lost, top, below(ocean[0]))
    row_bottom[...] = jnp.where(lost, bottom, below(ocean[rows - 1]))


def outer_lines(failed, ocean, sent):
    rows, fields, columns = ocean.shape
    line = jax.ShapeDtypeStruct((2 * fields, columns // 2), jnp.float32)
    return pl.pallas_call(
        functools.partial(rows_kernel, len(sent) == 1),
        out_shape=(line, line),
        in_specs=[SMEM] + [VMEM] * (1 + len(sent)),
        out_specs=(VMEM, VMEM),
        compiler_params=pltpu.CompilerParams(vmem_limit_bytes=VMEM_BYTES),
    )(failed, ocean, *sent)


def first_kernel(
    whole,
    failed,
    ocean,
    sent,
    op,
    diffusivity,
    fresh,
    strips,
    operator,
    number_of,
    inner,
    sides,
    parity,
    sem,
):
    leave = pltpu.make_async_copy(fresh, parity, sem)
    leave.start()
    rows, fields, columns = ocean.shape
    half = columns // 2
    count = 2 * strips.shape[0]
    strip = rows // count
    _, _, core, lost = my_place(failed)
    operator[...] = double_operator(op)
    field = lax.broadcasted_iota(jnp.int32, (fields, half), 0)
    number = jnp.zeros((fields, half), jnp.float32)
    for f in range(fields):
        number = jnp.where(field == f, diffusivity[f], number)
    number_of[...] = number

    def source(p):
        return 2 * p + core if whole else chip_slot(p)

    tiles = [sent[source(p), 0:GROUP, :] for p in range(count // 2)]
    for p, side in enumerate(strip_sides(operator, tiles, core, (fields, half), strip)):
        sides[p] = side

    def mix(p):
        def store(t, done):
            strips[p, pl.ds(t, 2)] = done

        base = pl.multiple_of((2 * p + core) * strip, strip)
        at = source(p)
        mix_strip(operator, lost, lambda own: sent[at, own, :], base, ocean, strip, store)

    mix(0)

    @pl.loop(0, count // 2, unroll=8)
    def _(p):
        for t in range(1, strip - 1):

            def store(own, cells):
                inner[p, t - 1, :, own] = cells

            diffuse_row(lambda d, own: strips[p, t + d, :, own], store, sides[p], t, number)
        mix(jnp.minimum(p + 1, count // 2 - 1))

    leave.wait()


def first_half(failed, ocean, sent, op, diffusivity, fresh, whole, count):
    rows, fields, columns = ocean.shape
    half = columns // 2
    wide = 2 * fields
    shapes = [jax.ShapeDtypeStruct((count // 2, rows // count, fields, columns), jnp.float32)]
    shapes.append(jax.ShapeDtypeStruct((wide, 3 * wide), jnp.bfloat16))
    shapes.append(jax.ShapeDtypeStruct((fields, half), jnp.float32))
    inner = (count // 2, rows // count - 2, fields, columns)
    shapes.append(jax.ShapeDtypeStruct(inner, jnp.float32))
    shapes.append(jax.ShapeDtypeStruct((count // 2, fields, half), jnp.float32))
    shapes.append(jax.ShapeDtypeStruct(fresh.shape, jnp.float32))
    return pl.pallas_call(
        functools.partial(first_kernel, whole),
        out_shape=tuple(shapes),
        in_specs=[SMEM, VMEM, VMEM, VMEM, SMEM, VMEM],
        out_specs=(VMEM,) * 5 + (pl.BlockSpec(memory_space=pl.ANY),),
        scratch_shapes=[pltpu.SemaphoreType.DMA],
        compiler_params=pltpu.CompilerParams(vmem_limit_bytes=VMEM_BYTES),
        cost_estimate=pl.CostEstimate(
            flops=75 * ocean.size, bytes_accessed=4 * ocean.size, transcendentals=ocean.size // 2
        ),
    )(failed, ocean, sent, op, diffusivity, fresh)


def step_kernel(whole, failed, ocean, *refs):
    if whole:
        sent, strips, operator, number_of, inner, near, above, under, *refs = refs
    else:
        mine, other, strips, operator, number_of, inner, near, *refs = refs
    out, mixed, sides = refs
    rows, fields, columns = ocean.shape
    half = columns // 2
    wide = 2 * fields
    pairs = strips.shape[0]
    count = 2 * pairs
    strip = rows // count
    _, _, core, lost = my_place(failed)
    number = number_of[...]

    def prepare(p):
        kept = pl.multiple_of((2 * p + core) * strip, strip)
        base = pl.multiple_of((2 * p + 1 - core) * strip, strip)
        at = 2 * p + 1 - core if whole else chip_slot(p)
        source = sent if whole else other
        for t in range(0, strip, 2):
            mixed[pl.ds(kept + t + 1, 2)] = strips[p, pl.ds(t, 2)]

        def store(t, done):
            mixed[pl.ds(base + t + 1, 2)] = done

        head = mix_strip(operator, lost, lambda own: source[at, own, :], base, ocean, strip, store)
        return jnp.where(core == 0, strips[p, 0], head)

    if whole:
        outer = jnp.concatenate([beside(above[...]), beside(under[...])], axis=0)
        outer = mix_pair(operator, outer)
        mixed[0] = outer[:fields]
        mixed[rows + 1] = outer[fields:]
    else:
        mixed[0] = jnp.zeros((fields, columns), jnp.float32)
        mixed[rows + 1] = jnp.zeros((fields, columns), jnp.float32)
    tiles = []
    for p in range(pairs):
        tiles.append(sent[2 * p + 1 - core, 0:GROUP, :] if whole else other[chip_slot(p), 0:GROUP, :])
    for p, side in enumerate(strip_sides(operator, tiles, core, (fields, half), strip)):
        sides[2 * p + 1 - core] = side
        sides[2 * p + core] = near[p]
    prepare(0)

    def diffuse(s, t, under_row=None):
        i = s * strip + t + 1

        def read(d, own):
            if d == 1 and under_row is not None:
                return under_row[:, own]
            return mixed[i + d, :, own]

        def store(own, cells):
            out[i - 1, :, own] = cells

        diffuse_row(read, store, sides[s], t, number)

    @pl.loop(0, pairs, unroll=2)
    def _(p):
        out[pl.ds((2 * p + core) * strip + 1, strip - 2)] = inner[p]
        diffuse(2 * p, 0)
        for t in range(1, strip - 1):
            diffuse(2 * p + 1 - core, t)
        diffuse(2 * p, strip - 1)
        diffuse(2 * p + 1, 0)
        head = prepare(jnp.minimum(p + 1, pairs - 1))
        head = jnp.where(p == pairs - 1, mixed[rows + 1], head)
        diffuse(2 * p + 1, strip - 1, head)


def step(failed, ocean, sent, strips, operator, number_of, inner, near, *outer):
    rows, fields, columns = ocean.shape
    whole = len(sent) == 1
    pairs = strips.shape[0]
    return pl.pallas_call(
        functools.partial(step_kernel, whole),
        out_shape=jax.ShapeDtypeStruct(ocean.shape, jnp.float32),
        in_specs=[SMEM] + [VMEM] * (6 + len(sent) + len(outer)),
        out_specs=VMEM,
        scratch_shapes=[
            pltpu.VMEM((rows + 2, fields, columns), jnp.float32),
            pltpu.VMEM((2 * pairs, fields, columns // 2), jnp.float32),
        ],
        compiler_params=pltpu.CompilerParams(vmem_limit_bytes=VMEM_BYTES),
        cost_estimate=pl.CostEstimate(
            flops=100 * ocean.size, bytes_accessed=12 * ocean.size, transcendentals=ocean.size // 2
        ),
    )(failed, ocean, *sent, strips, operator, number_of, inner, near, *outer)


def ends_kernel(stepped, above, under, operator, number_of, out, row, sem):
    rows, fields, columns = stepped.shape
    places = (0, rows - 1)
    reads = [
        pltpu.make_async_copy(out.at[at], row.at[n], sem.at[n]) for n, at in enumerate(places)
    ]
    for copy in reads:
        copy.start()
    both = jnp.concatenate([beside(above[...]), beside(under[...])], axis=0)
    both = mix_pair(operator, both)
    number = jnp.concatenate([number_of[...], number_of[...]], axis=1)
    writes = []
    for n, at in enumerate(places):
        reads[n].wait()
        row[n] = row[n] + number * both[n * fields : (n + 1) * fields]
        writes.append(pltpu.make_async_copy(row.at[n], out.at[at], sem.at[n]))
        writes[n].start()
    for copy in writes:
        copy.wait()


def add_ends(stepped, above, under, operator, number_of):
    rows, fields, columns = stepped.shape
    anywhere = pl.BlockSpec(memory_space=pl.ANY)
    return pl.pallas_call(
        ends_kernel,
        out_shape=jax.ShapeDtypeStruct(stepped.shape, jnp.float32),
        in_specs=[anywhere] + [VMEM] * 4,
        out_specs=anywhere,
        input_output_aliases={0: 0},
        scratch_shapes=[
            pltpu.VMEM((2, fields, columns), jnp.float32),
            pltpu.SemaphoreType.DMA((2,)),
        ],
        compiler_params=pltpu.CompilerParams(vmem_limit_bytes=VMEM_BYTES),
    )(stepped, above, under, operator, number_of)


def per_device(
    ocean_state, saved_checksums, checksum_weights, failed_devices, column_op, diffusivity
):
    lines = lax.axis_size("row")
    rows, fields, columns = ocean_state.shape
    count = checksum_weights.shape[1]
    half = columns // 2
    strip = rows // count

    strips = lax.all_to_all(ocean_state, MEMBERS, 0, 0, tiled=True)
    strips, ocean, saved, weights, failed, op, number = lax.optimization_barrier(
        (
            strips,
            ocean_state,
            saved_checksums,
            checksum_weights,
            failed_devices.T,
            column_op,
            diffusivity,
        )
    )
    strips = strips.reshape(count, strip, fields, columns)
    fresh, rebuilt, back, shared = rebuild(failed, weights, strips, saved)

    def exchange_rows(ocean, sent):
        top, bottom = outer_lines(failed, ocean, sent)
        above = lax.ppermute(bottom, "row", [(r, r + 1) for r in range(lines - 1)])
        under = lax.ppermute(top, "row", [(r + 1, r) for r in range(lines - 1)])
        return above, under

    def exchange_chips(rebuilt, back, ocean, fresh):
        mine = lax.all_to_all(back, CHIPS, 0, 0, tiled=True)
        mine, ocean = lax.optimization_barrier((mine, ocean))
        other = lax.ppermute(mine, "core", [(0, 1), (1, 0)])
        *kept, parity = first_half(failed, ocean, mine, op, number, fresh, False, count)
        other, kept = lax.optimization_barrier((other, kept))
        above, under = exchange_rows(ocean, (mine, other))
        stepped = step(failed, ocean, (mine, other), *kept)
        return add_ends(stepped, above, under, *kept[1:3]), parity

    def exchange_whole(rebuilt, back, ocean, fresh):
        back = spread_whole(failed, rebuilt, back)
        sent = lax.all_to_all(back, MEMBERS, 0, 0, tiled=True)
        sent, ocean = lax.optimization_barrier((sent, ocean))
        above, under = exchange_rows(ocean, (sent,))
        *kept, parity = first_half(failed, ocean, sent, op, number, fresh, True, count)
        return step(failed, ocean, (sent,), *kept, above, under), parity

    return lax.cond(
        shared[0] != 0, exchange_whole, exchange_chips, rebuilt, back, ocean, fresh
    )


def solution(mesh):
    row, col = mesh.axis_names
    shape = (mesh.shape[row], 2, 4, 2)
    chips = jax.sharding.Mesh(mesh.devices.reshape(shape), ("row", "y_hi", "x", "core"))
    col = MEMBERS
    return jax.shard_map(
        per_device,
        mesh=chips,
        in_specs=(P("row", None, col), P(("row", *col), None, None, None), P(), P(), P(), P()),
        out_specs=(P("row", None, col), P(("row", *col), None, None, None)),
        check_vma=False,
    )
```
